32 devices in a mesh: dp: 8 (over z, y), seq: 4 (over x, core).
Axes of the slice: x: 2, y: 2, z: 4, core: 2. Of those that a mesh axis runs over, the one named last changes fastest.
Arguments:
- tokens: bfloat16 [8192, 2048], P(('dp', 'seq')), may hold values from -6 to 6
- row_lengths: int32 [8, 4], P('dp'), may hold values from 1 to 1021, as said below
- branch_weight: bfloat16 [2048, 2560], P(('dp', 'seq')), may hold values from -0.125 to 0.125
- inner_weight: bfloat16 [2048, 2560], P(('dp', 'seq')), may hold values from -0.125 to 0.125
- output_weight: bfloat16 [2560, 2048], P(('dp', 'seq')), may hold values from -0.5 to 0.5
- rate_weight: bfloat16 [2560, 256], P(('dp', 'seq')), may hold values from -0.375 to 0.375
- entry_weight: bfloat16 [2560, 256], P(('dp', 'seq')), may hold values from -0.375 to 0.375
- rate_bias: bfloat16 [2560], P(('dp', 'seq')), may hold values from -3 to 3
- entry_bias: bfloat16 [2560], P(('dp', 'seq')), may hold values from -3 to 3
- conv_weight: bfloat16 [4, 2560], P(None, ('dp', 'seq')), may hold values from -3 to 3
- conv_bias: bfloat16 [2560], P(('dp', 'seq')), may hold values from -2 to 2
- recur_param: bfloat16 [2560], P(('dp', 'seq')), may hold values from 3.8 to 13
- norm_gain: bfloat16 [2048], P(('dp', 'seq')), may hold values from 0.5 to 1.5
- mlp_gain: bfloat16 [2048], P(('dp', 'seq')), may hold values from 0.5 to 1.5
- gate_weight: bfloat16 [2048, 6144], P(None, 'seq'), may hold values from -0.125 to 0.125
- up_weight: bfloat16 [2048, 6144], P(None, 'seq'), may hold values from -0.125 to 0.125
- down_weight: bfloat16 [6144, 2048], P('seq'), may hold values from -0.15625 to 0.15625
- cotangent: bfloat16 [8192, 2048], P(('dp', 'seq')), may hold values from -6 to 6
Outputs:
- result: bfloat16 [8192, 2048], P(('dp', 'seq'))
- grad_tokens: float32 [8192, 2048], P(('dp', 'seq'))
- grad_branch: float32 [2048, 2560], P(('dp', 'seq'))
- grad_inner: float32 [2048, 2560], P(('dp', 'seq'))
- grad_output: float32 [2560, 2048], P(('dp', 'seq'))
- grad_rate: float32 [2560, 256], P(('dp', 'seq'))
- grad_entry: float32 [2560, 256], P(('dp', 'seq'))
- grad_rate_bias: float32 [2560], P(('dp', 'seq'))
- grad_entry_bias: float32 [2560], P(('dp', 'seq'))
- grad_conv: float32 [4, 2560], P(None, ('dp', 'seq'))
- grad_conv_bias: float32 [2560], P(('dp', 'seq'))
- grad_recur: float32 [2560], P(('dp', 'seq'))
- grad_norm_gain: float32 [2048], P(('dp', 'seq'))
- grad_mlp_gain: float32 [2048], P(('dp', 'seq'))
- grad_gate: float32 [2048, 6144], P('dp', 'seq')
- grad_up: float32 [2048, 6144], P('dp', 'seq')
- grad_down: float32 [6144, 2048], P('seq', 'dp')
The draws below stay inside these ranges and needn't reach their ends.
Inputs may be any that keep to these rules, and one draw needn't show every extreme that they name: `row_lengths`: each group's 4 lengths sum to 1024. In each group one row, at a place drawn from the seed, starts within the first 256 tokens and ends within the last 256; every other row has fewer than 64 tokens.
All inputs are finite; a program needn't handle non-finite values.
Results may differ from the reference program's by a relative error of at most 0.014.
Values may be sent and summed in bfloat16 or wider, within the bound.
A program may use at most 256 MiB of HBM per device.

```python
import math
import jax
import jax.numpy as jnp
from jax import lax

D = 2048
R = 2560
BLOCK = 256
FF = 6144
WIDTH = 4
ROWS = 4
TOK_DEV = 256
HEADS = 10
GROUP_TOK = 1024
TOKENS = 8192
N_DP = 8


def draw_row_lengths(key, part):
    key = jax.random.fold_in(key, 11)
    short_key, long_key, group_key = jax.random.split(key, 3)
    shorts = jax.random.randint(short_key, (N_DP, ROWS), 1, TOK_DEV // ROWS)
    picked = jax.random.randint(group_key, (), 0, N_DP)
    group_index = jnp.arange(N_DP, dtype=jnp.int32)[:, None]
    shorts = jnp.where(group_index == picked, 1, shorts)
    chosen = jax.random.randint(long_key, (N_DP, 1), 0, ROWS)
    column = jnp.arange(ROWS, dtype=jnp.int32)[None, :]
    is_long = column == chosen
    others = jnp.sum(jnp.where(is_long, 0, shorts), axis=1, keepdims=True)
    return jnp.where(is_long, GROUP_TOK - others, shorts).astype(jnp.int32)


def draw_recur_param(key, part):
    key = jax.random.fold_in(key, 23)
    coin_key, slow_key, fast_key = jax.random.split(key, 3)
    share = 0.5
    slow = jnp.exp(jax.random.uniform(slow_key, (R,), jnp.float32, math.log(0.05 / GROUP_TOK), math.log(0.4 / GROUP_TOK)))
    fast = jnp.exp(jax.random.uniform(fast_key, (R,), jnp.float32, math.log(0.008), math.log(0.02)))
    speeds = jnp.where(jax.random.uniform(coin_key, (R,), jnp.float32) < share, slow, fast)
    return (-jnp.log(jnp.expm1(speeds))).astype(jnp.bfloat16)


def steps_of(rng, extent, cuts, smallest, top_value):
    def one(axis_at, shards_of):
        heights = jax.random.uniform(jax.random.fold_in(jax.random.fold_in(rng, 6), axis_at), (shards_of,), jnp.float32, smallest / len(cuts), top_value / len(cuts))
        return jnp.repeat(jnp.exp(heights), extent[axis_at] // shards_of).reshape((-1,) + (1,) * (len(extent) - axis_at - 1))

    level = one(*cuts[0])
    for cut in cuts[1:]:
        level = level * one(*cut)
    return level


def noise(key, dims, scale, bound, cuts=(), kind=jnp.bfloat16):
    gain = steps_of(key, dims, cuts, -0.22, 0.18) if cuts else 1.0
    entries = jax.random.normal(key, dims, jnp.float32) * scale * gain
    return jnp.minimum(jnp.maximum(entries, -bound), bound).astype(kind)


def setup_inputs(seed: int = 0) -> dict:
    splits = jax.random.split(jax.random.key(seed), 19)
    return {
        "tokens": noise(splits[0], (TOKENS, D), 1.0, 6.0, ((0, 32),)),
        "row_lengths": draw_row_lengths(jax.random.fold_in(splits[18], 71), 0),
        "branch_weight": noise(splits[2], (D, R), D ** -0.5, 0.125, ((0, 32),)),
        "inner_weight": noise(splits[3], (D, R), D ** -0.5, 0.125, ((0, 32),)),
        "output_weight": noise(splits[4], (R, D), (R // 16) ** -0.5, 0.5, ((0, 32),)),
        "rate_weight": noise(splits[5], (R, BLOCK), BLOCK ** -0.5, 0.375, ((0, 32),)),
        "entry_weight": noise(splits[6], (R, BLOCK), BLOCK ** -0.5, 0.375, ((0, 32),)),
        "rate_bias": noise(splits[7], (R,), 0.5, 3.0, ((0, 32),)),
        "entry_bias": noise(splits[8], (R,), 0.5, 3.0, ((0, 32),)),
        "conv_weight": noise(splits[9], (WIDTH, R), WIDTH ** -0.5, 3.0, ((1, 32),)),
        "conv_bias": noise(splits[10], (R,), 0.3, 2.0, ((0, 32),)),
        "recur_param": draw_recur_param(jax.random.fold_in(splits[18], 71), 0),
        "norm_gain": jnp.clip(1.0 + 0.1 * jax.random.normal(splits[12], (D,), jnp.float32), 0.5, 1.5).astype(jnp.bfloat16),
        "mlp_gain": jnp.clip(1.0 + 0.1 * jax.random.normal(splits[13], (D,), jnp.float32), 0.5, 1.5).astype(jnp.bfloat16),
        "gate_weight": noise(splits[14], (D, FF), D ** -0.5, 0.125, ((1, 4),)),
        "up_weight": noise(splits[15], (D, FF), D ** -0.5, 0.125, ((1, 4),)),
        "down_weight": noise(splits[16], (FF, D), (FF // 4) ** -0.5, 0.15625, ((0, 4),)),
        "cotangent": noise(splits[17], (TOKENS, D), 1.0, 6.0, ((0, 32),)),
    }


EPSILON = 1e-06
HIGHEST = lax.Precision.HIGHEST

@jax.custom_vjp
def low(v):
    return lax.optimization_barrier(v.astype(jnp.bfloat16)).astype(jnp.float32)

@jax.custom_vjp
def low_back(v):
    return v

def low_keep(v):
    return (low(v), None)

def low_pass(kept, grad):
    return (grad,)

def back_keep(v):
    return (v, None)

def back_low(kept, grad):
    return (low(grad),)
low.defvjp(low_keep, low_pass)
low_back.defvjp(back_keep, back_low)

def matmul(left_side, right_side):
    return jnp.dot(left_side, right_side, preferred_element_type=jnp.float32, precision=HIGHEST)

def rms_norm(values, gain_vector):
    inv_scale = lax.rsqrt(lax.optimization_barrier(jnp.mean(values * values, axis=-1, keepdims=True)) + EPSILON)
    return values * inv_scale * gain_vector

def combine(earlier, latter):
    return (earlier[0] * latter[0], latter[0] * earlier[1] + latter[1])

def row_offsets(lengths, places):
    row_ends = jnp.cumsum(lengths).astype(jnp.int32)
    starts = (row_ends - lengths).astype(jnp.int32)
    row_begin = lax.optimization_barrier(jnp.max(jnp.where(starts[None, :] <= places[:, None], starts[None, :], 0), axis=1))
    return (places - row_begin).astype(jnp.int32)

def lru_terms(keeping, pre_rate, pre_entry, conv_value, recur_value):
    rate_sig = jax.nn.sigmoid(pre_rate)
    entry_sig = jax.nn.sigmoid(pre_entry)
    decay_base = jnp.exp(-8.0 * rate_sig * jax.nn.softplus(-recur_value))
    sources = jnp.sqrt(1.0 - decay_base * decay_base) * entry_sig * conv_value
    return (decay_base * keeping, sources)

def block_product(values, weight):
    tok_count = values.shape[0]
    head_view = values.reshape(tok_count, HEADS, BLOCK)
    block_table = weight.reshape(HEADS, BLOCK, BLOCK)
    return jnp.einsum('thc,hcd->thd', head_view, block_table, precision=HIGHEST).reshape(tok_count, R)

def group_forward(values, lengths, params):
    branch_weight, inner_weight, output_weight, rate_weight, entry_weight, rate_bias, entry_bias, conv_weight, conv_bias, recur_param, norm_gain, mlp_gain, gate_weight, up_weight, down_weight = params
    tok_count = values.shape[0]
    offsets = row_offsets(lengths, jnp.arange(tok_count, dtype=jnp.int32))
    normed = low(rms_norm(values, norm_gain))
    branch = jax.nn.gelu(low_back(matmul(normed, branch_weight)))
    inner_low = low(low_back(matmul(normed, inner_weight)))
    padded = jnp.concatenate([jnp.zeros((WIDTH - 1, R), jnp.float32), inner_low], axis=0)
    conv_sum = jnp.zeros((tok_count, R), jnp.float32) + conv_bias
    for tap_index in range(WIDTH):
        usable = (offsets >= tap_index).astype(jnp.float32)[:, None]
        window = padded[WIDTH - 1 - tap_index:WIDTH - 1 - tap_index + tok_count]
        conv_sum = conv_sum + conv_weight[tap_index] * usable * window
    conv_value = low(conv_sum)
    pre_rate = low_back(block_product(conv_value, rate_weight)) + rate_bias
    pre_entry = low_back(block_product(conv_value, entry_weight)) + entry_bias
    keeping = (offsets > 0).astype(jnp.float32)[:, None]
    decays, sources = lru_terms(keeping, pre_rate, pre_entry, conv_value, recur_param)
    prefix, states = lax.associative_scan(combine, (decays, sources))
    mixed_low = low(branch * states)
    middle = values + low_back(matmul(mixed_low, output_weight))
    normed_mid = low(rms_norm(middle, mlp_gain))
    gate_pre = low_back(matmul(normed_mid, gate_weight))
    up_pre = low_back(matmul(normed_mid, up_weight))
    hidden = low(jax.nn.gelu(gate_pre) * up_pre)
    return middle + low_back(matmul(hidden, down_weight))

def reference(tokens, row_lengths, branch_weight, inner_weight, output_weight, rate_weight, entry_weight, rate_bias, entry_bias, conv_weight, conv_bias, recur_param, norm_gain, mlp_gain, gate_weight, up_weight, down_weight, cotangent):
    params = tuple((one_array.astype(jnp.float32) for one_array in (branch_weight, inner_weight, output_weight, rate_weight, entry_weight, rate_bias, entry_bias, conv_weight, conv_bias, recur_param, norm_gain, mlp_gain, gate_weight, up_weight, down_weight)))
    groups = tokens.astype(jnp.float32).reshape(N_DP, GROUP_TOK, D)
    checked = jax.checkpoint(group_forward)

    def forward(inputs, weights):
        return lax.map(lambda group_pair: checked(group_pair[0], group_pair[1], weights), (inputs, row_lengths))
    outputs, pullback = jax.vjp(forward, groups, params)
    grad_groups, gradients = pullback(cotangent.astype(jnp.float32).reshape(N_DP, GROUP_TOK, D))
    result = outputs.reshape(TOKENS, D).astype(jnp.bfloat16)
    return (result, grad_groups.reshape(TOKENS, D), gradients[0], gradients[1], gradients[2], gradients[3], gradients[4], gradients[5], gradients[6], gradients[7], gradients[8], gradients[9], gradients[10], gradients[11], gradients[12], gradients[13], gradients[14])
```

```python
from functools import partial

import jax
import jax.numpy as jnp
from jax import lax
from jax.experimental import pallas as pl
from jax.experimental.pallas import tpu as pltpu
from jax.sharding import PartitionSpec as P

BLOCK = 256
WIDTH = 4
EPSILON = 1e-06
LANES = 128
VMEM_BYTES = 56 * 1024 * 1024
ENTRY_TILE = 256
MLP_TILE = 256
GRAD_TILE = 512
EXIT_TILE = 256
BOTH = ("dp", "seq")
F32 = jnp.float32
BF16 = jnp.bfloat16


def dot(left, right):
    return jnp.dot(left, right, preferred_element_type=F32)


def contract_rows(left, right):
    return lax.dot_general(left, right, (((0,), (0,)), ((), ())), preferred_element_type=F32)


def contract_cols(left, right):
    return lax.dot_general(left, right, (((1,), (1,)), ((), ())), preferred_element_type=F32)


class Place:
    def __init__(self):
        self.n_dp = lax.axis_size("dp")
        self.n_seq = lax.axis_size("seq")
        self.n_q = self.n_dp // 2
        self.n_x = self.n_seq // 2
        self.dp = lax.axis_index("dp")
        self.seq = lax.axis_index("seq")
        self.p = self.dp % 2
        self.q = self.dp // 2
        self.c = self.seq % 2
        self.x = self.seq // 2

    def swap_core(self, a):
        return lax.ppermute(a, "seq", [(i, i ^ 1) for i in range(self.n_seq)])

    def swap_pair(self, a):
        return lax.ppermute(a, "dp", [(i, i ^ 1) for i in range(self.n_dp)])

    def step_x(self, a, places, way):
        return lax.ppermute(
            a, "seq", [(2 * i + c, 2 * (i + way) + c) for i in places for c in range(2)]
        )

    def step_q(self, a, places, way):
        return lax.ppermute(
            a, "dp", [(2 * i + p, 2 * (i + way) + p) for i in places for p in range(2)]
        )


def add_low(*terms):
    total = terms[0].astype(F32)
    for term in terms[1:]:
        total = total + term.astype(F32)
    return total


def line_sum(block_of, count, here, step):
    if count == 1:
        return block_of(here).astype(F32)
    if count == 2:
        got = step(block_of(1 - here), [0, 1], None)
        return add_low(block_of(here), got)
    up = down = None
    for k in range(1, count):
        send_up = block_of(jnp.minimum(count - k + here, count - 1))
        if up is not None:
            send_up = add_low(send_up, up).astype(BF16)
        up = step(send_up, range(0, min(k, count - 1)), 1)
        send_down = block_of(jnp.maximum(k + here - count, 0))
        if down is not None:
            send_down = add_low(send_down, down).astype(BF16)
        down = step(send_down, range(max(count - k, 1), count), -1)
    return add_low(block_of(here), up, down)


def line_gather(block, count, here, step):
    if count == 1:
        return block[None]
    if count == 2:
        got = step(block, [0, 1], None)
        return jnp.where(here == 0, jnp.stack([block, got]), jnp.stack([got, block]))
    rows = jnp.zeros((count,) + block.shape, block.dtype)
    rows = lax.dynamic_update_index_in_dim(rows, block, here, 0)
    up = down = block
    for k in range(1, count):
        up = step(up, range(k - 1, count - 1), 1)
        down = step(down, range(1, count - k + 1), -1)
        from_up = lax.dynamic_update_index_in_dim(rows, up, jnp.maximum(here - k, 0), 0)
        rows = jnp.where(here - k >= 0, from_up, rows)
        from_down = lax.dynamic_update_index_in_dim(rows, down, jnp.minimum(here + k, count - 1), 0)
        rows = jnp.where(here + k < count, from_down, rows)
    return rows


def x_step(place):
    def step(a, places, way):
        if way is None:
            return lax.ppermute(a, "seq", [(i, i ^ 2) for i in range(place.n_seq)])
        return place.step_x(a, places, way)

    return step


def q_step(place):
    def step(a, places, way):
        if way is None:
            return lax.ppermute(a, "dp", [(i, i ^ 2) for i in range(place.n_dp)])
        return place.step_q(a, places, way)

    return step


def gather_seq(place, block):
    rows = line_gather(block, place.n_x, place.x, x_step(place))
    other = place.swap_core(rows)
    first = jnp.where(place.c == 0, rows, other)
    second = jnp.where(place.c == 0, other, rows)
    return jnp.stack([first, second], axis=1).reshape((place.n_seq,) + block.shape)


def scatter_seq(place, whole):
    view = whole.reshape((place.n_x, 2) + whole.shape[1:])
    mine = lax.dynamic_index_in_dim(view, place.c, 1, False)
    theirs = lax.dynamic_index_in_dim(view, 1 - place.c, 1, False)
    chip = add_low(mine, place.swap_core(theirs)).astype(BF16)
    return line_sum(
        lambda i: lax.dynamic_index_in_dim(chip, i, 0, False), place.n_x, place.x, x_step(place)
    )


def gather_plane(place, block):
    if place.n_x != 2:
        both = jnp.where(
            place.p == 0,
            jnp.stack([block, place.swap_pair(block)]),
            jnp.stack([place.swap_pair(block), block]),
        )
        rows = gather_seq(place, both)
        return jnp.swapaxes(rows, 0, 1)
    half = block.shape[0] // 2
    step = x_step(place)
    by_x = step(block, [0, 1], None)
    by_y = place.swap_pair(block)
    corner_low = step(by_y[:half], [0, 1], None)
    corner_high = place.swap_pair(by_x[half:])
    corner = jnp.concatenate([corner_low, corner_high], axis=0)
    mine = jnp.where(place.x == 0, jnp.stack([block, by_x]), jnp.stack([by_x, block]))
    away = jnp.where(place.x == 0, jnp.stack([by_y, corner]), jnp.stack([corner, by_y]))
    rows = jnp.where(place.p == 0, jnp.stack([mine, away]), jnp.stack([away, mine]))
    other = place.swap_core(rows)
    first = jnp.where(place.c == 0, rows, other)
    second = jnp.where(place.c == 0, other, rows)
    return jnp.stack([first, second], axis=2).reshape((2, place.n_seq) + block.shape)


def scatter_plane(place, whole):
    view = whole.reshape((2, place.n_x, 2) + whole.shape[2:])
    mine = lax.dynamic_index_in_dim(view, place.c, 2, False)
    theirs = lax.dynamic_index_in_dim(view, 1 - place.c, 2, False)
    chip = add_low(mine, place.swap_core(theirs)).astype(BF16)
    if place.n_x != 2:
        near = lax.dynamic_index_in_dim(chip, place.p, 0, False)
        far = lax.dynamic_index_in_dim(chip, 1 - place.p, 0, False)
        pair = add_low(near, place.swap_pair(far)).astype(BF16)
        return line_sum(
            lambda i: lax.dynamic_index_in_dim(pair, i, 0, False), place.n_x, place.x, x_step(place)
        )
    half = whole.shape[2] // 2
    step = x_step(place)

    def part(p, x):
        return lax.dynamic_index_in_dim(lax.dynamic_index_in_dim(chip, p, 0, False), x, 0, False)

    corner = part(1 - place.p, 1 - place.x)
    low = step(corner[:half], [0, 1], None)
    high = place.swap_pair(corner[half:])
    to_y = part(1 - place.p, place.x)
    to_x = part(place.p, 1 - place.x)
    to_y = jnp.concatenate([add_low(to_y[:half], low).astype(BF16), to_y[half:]], axis=0)
    to_x = jnp.concatenate([to_x[:half], add_low(to_x[half:], high).astype(BF16)], axis=0)
    got_y = place.swap_pair(to_y)
    got_x = step(to_x, [0, 1], None)
    return add_low(part(place.p, place.x), got_x, got_y)


def sum_dp(place, whole):
    view = whole.reshape((place.n_q, 2) + whole.shape[1:])
    mine = lax.dynamic_index_in_dim(view, place.p, 1, False)
    theirs = lax.dynamic_index_in_dim(view, 1 - place.p, 1, False)
    pair = add_low(mine, place.swap_pair(theirs)).astype(BF16)
    return line_sum(
        lambda i: lax.dynamic_index_in_dim(pair, i, 0, False), place.n_q, place.q, q_step(place)
    )


def split_pair(place, total, axis):
    half = total.shape[axis] // 2
    mine = lax.dynamic_slice_in_dim(total, place.p * half, half, axis)
    theirs = lax.dynamic_slice_in_dim(total, (1 - place.p) * half, half, axis).astype(BF16)
    got = place.swap_pair(theirs).astype(F32)
    pair = [jnp.concatenate(two, axis=1 - axis) for two in ([mine, got], [got, mine])]
    return jnp.where(place.p == 0, *pair)


def turned(place, a, back):
    route = [(s * place.n_dp + j, j * place.n_seq + s) for s in range(place.n_seq) for j in range(place.n_dp)]
    if back:
        route = [(there, here) for here, there in route]
    return lax.ppermute(a, BOTH, route)


def window(place, a, axis, own, spread):
    start = own * place.seq % BLOCK
    if own % BLOCK == 0:
        return a
    if 2 * own % BLOCK == 0 and spread == own + BLOCK // 2:
        edge = BLOCK // 2
        last = lax.slice_in_dim(a, own - edge, own, axis=axis)
        first = lax.slice_in_dim(a, 0, edge, axis=axis)
        got = place.swap_core(jnp.where(place.c == 0, last, first))
        return jnp.where(
            place.c == 0,
            jnp.concatenate([a, got], axis=axis),
            jnp.concatenate([got, a], axis=axis),
        )
    whole = lax.all_gather(a, "seq", axis=axis, tiled=True)
    begin = jnp.minimum(own * place.seq - start, whole.shape[axis] - spread)
    return lax.dynamic_slice_in_dim(whole, begin, spread, axis=axis)


def row_offsets(lengths, places):
    row_ends = jnp.cumsum(lengths)
    starts = row_ends - lengths
    row_begin = jnp.max(jnp.where(starts[None, :] <= places[:, None], starts[None, :], 0), axis=1)
    return places - row_begin


def shift_rows(a, distance, fill):
    count = a.shape[0]
    if distance > 0:
        return jnp.concatenate([jnp.full((distance, a.shape[1]), fill, a.dtype), a[: count - distance]], 0)
    return jnp.concatenate([a[-distance:], jnp.full((-distance, a.shape[1]), fill, a.dtype)], 0)


def scan_rows(decay, source, way):
    distance = 1
    while distance < decay.shape[0]:
        source = source + decay * shift_rows(source, way * distance, 0.0)
        decay = decay * shift_rows(decay, way * distance, 1.0)
        distance *= 2
    return decay, source


def gelu_parts(v):
    root = 0.7978845608028654
    cubic = 0.044715
    inner = root * (v + cubic * v * v * v)
    tanh = jnp.tanh(inner)
    value = 0.5 * v * (1.0 + tanh)
    slope = 0.5 * (1.0 + tanh) + 0.5 * v * (1.0 - tanh * tanh) * root * (1.0 + 3.0 * cubic * v * v)
    return value, slope


def softplus_row(recur):
    return jnp.maximum(-recur, 0.0) + jnp.log1p(jnp.exp(-jnp.abs(recur)))


def lru_parts(pre_rate, pre_entry, soft):
    rate = jax.nn.sigmoid(pre_rate)
    entry = jax.nn.sigmoid(pre_entry)
    power = 8.0 * soft * rate
    decay = jnp.exp(-power)
    twice = 2.0 * power
    series = twice * (
        1.0 - twice * (0.5 - twice * (1.0 / 6.0 - twice * (1.0 / 24.0 - twice * (1.0 / 120.0))))
    )
    square = jnp.where(twice < 0.25, series, 1.0 - decay * decay)
    return rate, entry, decay, square


STEP_ROWS = 64
TILE = 8


def row_steps(count):
    return count // STEP_ROWS


def step_rows(i):
    return pl.ds(pl.multiple_of(i * STEP_ROWS, STEP_ROWS), STEP_ROWS)


def tile_before(i):
    return pl.ds(pl.multiple_of(jnp.maximum(i * STEP_ROWS - TILE, 0), TILE), TILE)


def tile_after(i, count):
    return pl.ds(pl.multiple_of(jnp.minimum((i + 1) * STEP_ROWS, count - TILE), TILE), TILE)


def tile_sum(a):
    return jnp.sum(a.reshape(-1, TILE, a.shape[1]), axis=0)


def conv_kernel(inner_ref, taps_ref, offset_ref, conv_ref):
    taps = taps_ref[...]

    def step(i, carry):
        r = step_rows(i)
        near = jnp.concatenate([inner_ref[tile_before(i), :], inner_ref[r, :]], axis=0).astype(F32)
        offset = offset_ref[r, :]
        total = taps[WIDTH : WIDTH + 1, :] + taps[0:1, :] * near[TILE:]
        for k in range(1, WIDTH):
            total = total + taps[k : k + 1, :] * jnp.where(offset >= k, near[TILE - k : TILE - k + STEP_ROWS], 0.0)
        conv_ref[r, :] = total.astype(BF16)
        return carry

    lax.fori_loop(0, row_steps(inner_ref.shape[0]), step, 0, unroll=4)


def forward_kernel(rate_ref, entry_ref, conv_ref, branch_ref, vec_ref, offset_ref, states_ref, mixed_ref):
    vec = vec_ref[...]
    soft = softplus_row(vec[2:3, :])

    def step(i, carry):
        r = step_rows(i)
        _, entry, decay, square = lru_parts(rate_ref[r, :] + vec[0:1, :], entry_ref[r, :] + vec[1:2, :], soft)
        source = jnp.sqrt(square) * entry * conv_ref[r, :].astype(F32)
        decay = jnp.where(offset_ref[r, :] > 0, decay, 0.0)
        product, local = scan_rows(decay, source, 1)
        states = local + product * carry
        states_ref[r, :] = states
        mixed_ref[r, :] = (gelu_parts(branch_ref[r, :])[0] * states).astype(BF16)
        return states[STEP_ROWS - 1 :, :]

    lax.fori_loop(0, row_steps(states_ref.shape[0]), step, jnp.zeros_like(soft), unroll=4)


def backward_kernel(
    rate_ref, entry_ref, conv_ref, branch_ref, vec_ref, offset_ref, states_ref, back_ref,
    back_branch_ref, back_gates_ref, direct_ref, sums_ref,
):
    vec = vec_ref[...]
    recur = vec[2:3, :]
    soft = softplus_row(recur)
    steps = row_steps(states_ref.shape[0])

    def step(n, carry):
        later, later_decay, rate_sum, entry_sum, recur_sum = carry
        i = steps - 1 - n
        r = step_rows(i)
        rate, entry, decay, square = lru_parts(rate_ref[r, :] + vec[0:1, :], entry_ref[r, :] + vec[1:2, :], soft)
        conv = conv_ref[r, :].astype(F32)
        states = states_ref[r, :]
        back_mixed = back_ref[r, :]
        value, slope = gelu_parts(branch_ref[r, :])
        back_branch_ref[r, :] = (back_mixed * states * slope).astype(BF16)
        keep = offset_ref[r, :] > 0
        kept_decay = jnp.where(keep, decay, 0.0)
        following = jnp.concatenate([kept_decay[1:], later_decay], axis=0)
        product, local = scan_rows(following, back_mixed * value, -1)
        adjoint = local + product * later
        inverse = lax.rsqrt(square)
        root = square * inverse
        pulled = adjoint * entry * conv
        previous = jnp.concatenate([states_ref[tile_before(i), :][TILE - 1 :], states[: STEP_ROWS - 1]], axis=0)
        back_decay = adjoint * jnp.where(keep, previous, 0.0) - pulled * decay * inverse
        back_power = back_decay * decay * rate
        back_rate = back_power * (-8.0 * soft) * (1.0 - rate)
        back_entry = pulled * root * (1.0 - entry)
        back_gates_ref[0, r, :] = back_rate.astype(BF16)
        back_gates_ref[1, r, :] = back_entry.astype(BF16)
        direct_ref[r, :] = adjoint * root * entry
        return (
            adjoint[:1], kept_decay[:1], rate_sum + tile_sum(back_rate), entry_sum + tile_sum(back_entry),
            recur_sum + tile_sum(back_power),
        )

    row, tile = jnp.zeros_like(recur), jnp.zeros((TILE, recur.shape[1]), F32)
    _, _, rate_sum, entry_sum, recur_sum = lax.fori_loop(0, steps, step, (row, row, tile, tile, tile), unroll=4)
    total = lambda a: jnp.sum(a, axis=0, keepdims=True)
    sums_ref[...] = jnp.concatenate(
        [
            total(rate_sum),
            total(entry_sum),
            total(recur_sum) * (8.0 * jax.nn.sigmoid(-recur)),
            jnp.zeros((TILE - 3,) + recur.shape[1:], F32),
        ],
        axis=0,
    )


def conv_back_kernel(direct_ref, gates_ref, inner_ref, taps_ref, offset_ref, back_ref, sums_ref):
    count = direct_ref.shape[0]
    taps = taps_ref[...]
    steps = row_steps(count)

    def step(i, sums):
        r, before, after = step_rows(i), tile_before(i), tile_after(i, count)
        last = jnp.where(i + 1 < steps, 1.0, 0.0)
        here = direct_ref[r, :] + gates_ref[r, :]
        wide = jnp.concatenate([here, (direct_ref[after, :] + gates_ref[after, :]) * last], axis=0)
        offset = jnp.concatenate([offset_ref[r, :], offset_ref[after, :]], axis=0)
        inner = jnp.concatenate([inner_ref[before, :], inner_ref[r, :]], axis=0).astype(F32)
        total = taps[0:1, :] * here
        new = [sums[0] + tile_sum(here * inner[TILE:])]
        for k in range(1, WIDTH):
            masked = jnp.where(offset >= k, wide, 0.0)
            total = total + taps[k : k + 1, :] * masked[k : k + STEP_ROWS]
            new.append(sums[k] + tile_sum(masked[:STEP_ROWS] * inner[TILE - k : TILE - k + STEP_ROWS]))
        new.append(sums[WIDTH] + tile_sum(here))
        back_ref[r, :] = total.astype(BF16)
        return tuple(new)

    tile = jnp.zeros((TILE, taps.shape[1]), F32)
    sums = lax.fori_loop(0, steps, step, (tile,) * (WIDTH + 1), unroll=4)
    rows = [jnp.sum(a, axis=0, keepdims=True) for a in sums]
    sums_ref[...] = jnp.concatenate(rows + [jnp.zeros((TILE - len(rows), taps.shape[1]), F32)], axis=0)


def forward_gates_kernel(
    first_ref, block_ref, w_rate_ref, w_entry_ref, conv_ref, branch_ref, vec_ref, offset_ref, states_ref, mixed_ref,
    rate_ref, entry_ref,
):
    rate_ref[...] = dot(block_ref[...], w_rate_ref[...])
    entry_ref[...] = dot(block_ref[...], w_entry_ref[...])
    forward_kernel(rate_ref, entry_ref, conv_ref, branch_ref, vec_ref, offset_ref, states_ref, mixed_ref)


def backward_gates_kernel(
    first_ref, block_ref, w_rate_ref, w_entry_ref, conv_ref, branch_ref, vec_ref, offset_ref, states_ref, back_ref,
    back_branch_ref, back_gates_ref, direct_ref, sums_ref, rate_ref, entry_ref,
):
    rate_ref[...] = dot(block_ref[...], w_rate_ref[...])
    entry_ref[...] = dot(block_ref[...], w_entry_ref[...])
    backward_kernel(
        rate_ref, entry_ref, conv_ref, branch_ref, vec_ref, offset_ref, states_ref, back_ref,
        back_branch_ref, back_gates_ref, direct_ref, sums_ref,
    )


def conv_wide_kernel(first_ref, inner_ref, taps_ref, offset_ref, conv_ref):
    conv_kernel(inner_ref, taps_ref, offset_ref, conv_ref)


def conv_back_gates_kernel(
    first_ref, gates_ref, w_rate_ref, w_entry_ref, direct_ref, inner_ref, taps_ref, offset_ref, back_ref, sums_ref,
    total_ref,
):
    total_ref[...] = contract_cols(gates_ref[0], w_rate_ref[...]) + contract_cols(gates_ref[1], w_entry_ref[...])
    conv_back_kernel(direct_ref, total_ref, inner_ref, taps_ref, offset_ref, back_ref, sums_ref)


def by_block(kernel, first, ins, outs, scratch, own):
    def spec(how, shape):
        rows = shape[-2]
        half = BLOCK // LANES
        return {
            "own": pl.BlockSpec((rows, LANES), lambda j, f: (0, j)),
            "wide": pl.BlockSpec((rows, LANES), lambda j, f: (0, f[0] + j)),
            "block": pl.BlockSpec((rows, BLOCK), lambda j, f: (0, (f[0] + j) // half)),
            "wide2": pl.BlockSpec((2, rows, LANES), lambda j, f: (0, 0, f[0] + j)),
            "block2": pl.BlockSpec((2, rows, BLOCK), lambda j, f: (0, 0, (f[0] + j) // half)),
            "columns": pl.BlockSpec((BLOCK, LANES), lambda j, f: ((f[0] + j) // half, (f[0] + j) % half)),
            "rows": pl.BlockSpec((LANES, BLOCK), lambda j, f: (f[0] + j, 0)),
            "one": pl.BlockSpec((rows, 1), lambda j, f: (0, 0)),
        }[how]

    count = ins[0][1].shape[-2]
    return pl.pallas_call(
        kernel,
        grid_spec=pltpu.PrefetchScalarGridSpec(
            num_scalar_prefetch=1,
            grid=(own // LANES,),
            in_specs=[spec(how, a.shape) for how, a in ins],
            out_specs=[spec(how, shape) for how, shape, _ in outs],
            scratch_shapes=[pltpu.VMEM((count, LANES), F32)] * scratch,
        ),
        out_shape=[jax.ShapeDtypeStruct(shape, kind) for _, shape, kind in outs],
        compiler_params=pltpu.CompilerParams(vmem_limit_bytes=VMEM_BYTES),
        cost_estimate=pl.CostEstimate(
            flops=60 * count * own,
            bytes_accessed=sum(a.size * a.dtype.itemsize for _, a in ins) * 2,
            transcendentals=4 * count * own,
        ),
    )(first, *(a for _, a in ins))


def fill_edge(place, wide, own):
    edge = wide.shape[-1] - own
    from_lane = jnp.where(place.c == 0, own - edge, edge)
    to_lane = jnp.where(place.c == 0, own, 0)
    got = place.swap_core(lax.dynamic_slice_in_dim(wide, from_lane, edge, axis=wide.ndim - 1))
    return lax.dynamic_update_slice_in_dim(wide, got, to_lane, axis=wide.ndim - 1)


def by_channel(kernel, ins, outs, width, cost=40):
    padded = -(-width // LANES) * LANES

    def widened(a):
        return a if a.shape[1] in (1, padded) else jnp.pad(a, ((0, 0), (0, padded - width)))

    ins = [widened(a) for a in ins]
    specs = [
        pl.BlockSpec((a.shape[0], 1), lambda i: (0, 0))
        if a.shape[1] == 1
        else pl.BlockSpec((a.shape[0], LANES), lambda i: (0, i))
        for a in ins
    ]
    results = pl.pallas_call(
        kernel,
        grid=(padded // LANES,),
        in_specs=specs,
        out_specs=[
            pl.BlockSpec(rows + (LANES,), lambda i, rows=rows: (0,) * len(rows) + (i,)) for rows, _ in outs
        ],
        out_shape=[jax.ShapeDtypeStruct(rows + (padded,), kind) for rows, kind in outs],
        compiler_params=pltpu.CompilerParams(vmem_limit_bytes=VMEM_BYTES),
        cost_estimate=pl.CostEstimate(
            flops=cost * outs[0][0][0] * padded,
            bytes_accessed=sum(a.size * a.dtype.itemsize for a in ins) * 2,
            transcendentals=4 * outs[0][0][0] * padded,
        ),
    )(*ins)
    return [a[..., :width] for a in results]


def rms_norm(values, gain):
    return values * lax.rsqrt(jnp.mean(values * values, axis=-1, keepdims=True) + EPSILON) * gain


def rms_back(values, gain, back):
    scale = lax.rsqrt(jnp.mean(values * values, axis=-1, keepdims=True) + EPSILON)
    unit = values * scale
    grad_gain = jnp.sum(back * unit, axis=0)
    lifted = back * gain
    return scale * (lifted - unit * jnp.mean(lifted * unit, axis=-1, keepdims=True)), grad_gain


class Near:
    def __init__(self):
        self.n_dp, self.n_seq = lax.axis_size("dp"), lax.axis_size("seq")
        self.n_q = self.n_dp // 2
        self.dp, self.seq = lax.axis_index("dp"), lax.axis_index("seq")
        self.p, self.q = self.dp % 2, self.dp // 2
        self.c, self.x = self.seq % 2, self.seq // 2
        self.core = {"dp": self.dp, "seq": self.seq + 1 - 2 * self.c}
        self.over_x = {"dp": self.dp, "seq": self.seq + 2 - 4 * self.x}
        self.over_y = {"dp": self.dp + 1 - 2 * self.p, "seq": self.seq}

    def z(self, way):
        return {"dp": self.dp + 2 * way, "seq": self.seq}


def signal(device):
    pl.semaphore_signal(
        pltpu.get_barrier_semaphore(), inc=1, device_id=device, device_id_type=pl.DeviceIdType.MESH
    )


def remote(source, target, sems, index, device):
    return pltpu.make_async_remote_copy(
        src_ref=source,
        dst_ref=target,
        send_sem=sems[0].at[index],
        recv_sem=sems[1].at[index],
        device_id=device,
        device_id_type=pl.DeviceIdType.MESH,
    )


def gather_kernel(in_pack, out_pack, tok, cot, in_all, out_all, group_x, cot_c, cot_o, send, recv, local):
    near = Near()
    n_q, n_seq, n_dp = near.n_q, near.n_seq, near.n_dp
    dp, seq, p, q = near.dp, near.seq, near.p, near.q
    sems = (send, recv)
    place = dp * n_seq + seq
    to_dp, to_seq = place % n_dp, place // n_dp
    origin = seq * n_dp + dp
    turned_to = {"dp": to_dp, "seq": to_seq}
    turned_from = {"dp": origin // n_seq, "seq": origin % n_seq}
    moves = jnp.logical_or(to_dp != dp, to_seq != seq)
    above, below = q + 1 < n_q, q >= 1

    A2A, TURN, TOK, COT, TOKC, COTC, YB, YIN = 0, 3, 4, 5, 6, 8, 10, 11
    YOUT = YIN + n_q
    ZIN, ZOUT, ZB = YOUT + n_q, YOUT + n_q + n_q, YOUT + 3 * n_q
    SEND_DOWN = ZB + 2 * n_q

    for d in range(1, n_seq):
        signal({"dp": dp, "seq": (seq + d) % n_seq})
    signal(near.over_y)
    pl.when(above)(lambda: signal(near.z(1)))
    pl.when(below)(lambda: signal(near.z(-1)))
    pl.when(moves)(lambda: signal(turned_from))
    pl.semaphore_wait(
        pltpu.get_barrier_semaphore(),
        n_seq + above.astype(jnp.int32) + below.astype(jnp.int32) + moves.astype(jnp.int32),
    )

    sent = []

    def go(copy):
        copy.start()
        sent.append(copy)
        return copy

    for d in range(1, n_seq):
        peer = (seq + d) % n_seq
        go(remote(in_pack.at[peer], in_all.at[dp, seq], sems, A2A + d - 1, {"dp": dp, "seq": peer}))
    turn = remote(out_pack, out_all.at[to_dp], sems, TURN, turned_to)
    keep = [
        pltpu.make_async_copy(in_pack.at[seq], in_all.at[dp, seq], local.at[0]),
        pltpu.make_async_copy(tok, group_x.at[seq], local.at[1]),
        pltpu.make_async_copy(cot, cot_c.at[0], local.at[2]),
    ]
    stay = pltpu.make_async_copy(out_pack, out_all.at[dp], local.at[3])
    pl.when(moves)(turn.start)
    pl.when(jnp.logical_not(moves))(stay.start)
    for copy in keep:
        copy.start()
    go(remote(tok, group_x.at[seq], sems, TOK, near.over_x))
    go(remote(cot, cot_c.at[1], sems, COT, near.over_x))
    go(remote(tok, group_x.at[seq], sems, TOKC, near.core))
    go(remote(cot, cot_o.at[0], sems, COTC, near.core))

    def lines(block):
        d = 2 * block + p
        return [(ZIN + block, in_all.at[d, pl.ds(0, n_seq - 1)]), (ZOUT + block, out_all.at[d])]

    def corners(block):
        return [(ZB + 2 * block + i, in_all.at[2 * block + i, n_seq - 1]) for i in range(2)]

    def z_copy(number, ref, way):
        index = number if way > 0 else number + (SEND_DOWN - ZIN)
        return pltpu.make_async_remote_copy(
            src_ref=ref, dst_ref=ref, send_sem=send.at[index], recv_sem=recv.at[number],
            device_id=near.z(way), device_id_type=pl.DeviceIdType.MESH,
        )

    def y_copies(block):
        d = 2 * block + p
        return [
            remote(in_all.at[d, pl.ds(0, n_seq - 1)], in_all.at[d, pl.ds(0, n_seq - 1)], sems, YIN + block, near.over_y),
            remote(out_all.at[d], out_all.at[d], sems, YOUT + block, near.over_y),
        ]

    def y_arrivals(block):
        d = 2 * block + 1 - p
        return [
            remote(in_all.at[d, pl.ds(0, n_seq - 1)], in_all.at[d, pl.ds(0, n_seq - 1)], sems, YIN + block, near.over_y),
            remote(out_all.at[d], out_all.at[d], sems, YOUT + block, near.over_y),
        ]

    for d in range(1, n_seq):
        source = (seq + n_seq - d) % n_seq
        remote(in_pack.at[0], in_all.at[dp, source], sems, A2A + d - 1, {"dp": dp, "seq": source}).wait_recv()
    keep[0].wait()
    y_first = remote(in_all.at[dp, n_seq - 1], in_all.at[dp, n_seq - 1], sems, YB, near.over_y)
    go(y_first)

    def both_ways(pairs):
        for number, ref in pairs:
            pl.when(above)(lambda number=number, ref=ref: z_copy(number, ref, 1).start())
            pl.when(below)(lambda number=number, ref=ref: z_copy(number, ref, -1).start())

    own, own_y = lines(q), y_copies(q)
    both_ways(own[:1])
    go(own_y[0])
    pl.when(moves)(lambda: remote(out_pack, out_all.at[dp], sems, TURN, turned_to).wait_recv())
    pl.when(jnp.logical_not(moves))(stay.wait)
    both_ways(own[1:])
    go(own_y[1])
    other = 2 * q + 1 - p
    remote(in_all.at[other, n_seq - 1], in_all.at[other, n_seq - 1], sems, YB, near.over_y).wait_recv()
    both_ways(corners(q))

    for k in range(1, n_q):
        for way in (1, -1):
            block = q - way * k
            there = block >= 0 if way > 0 else block < n_q
            on = above if way > 0 else below

            def arrived(block=block, way=way, on=on):
                for (number, ref), y_copy in zip(lines(block), y_copies(block)):
                    z_copy(number, ref, way).wait_recv()
                    pl.when(on)(lambda number=number, ref=ref: z_copy(number, ref, way).start())
                    y_copy.start()
                for number, ref in corners(block):
                    z_copy(number, ref, way).wait_recv()
                    pl.when(on)(lambda number=number, ref=ref: z_copy(number, ref, way).start())

            pl.when(there)(arrived)
        if k == 1:
            other_x = seq + 2 - 4 * near.x
            remote(tok, group_x.at[other_x], sems, TOK, near.over_x).wait_recv()
            go(remote(group_x.at[other_x], group_x.at[other_x], sems, TOKC + 1, near.core))
            remote(cot, cot_c.at[1], sems, COT, near.over_x).wait_recv()
            go(remote(cot_c.at[1], cot_o.at[1], sems, COTC + 1, near.core))

    for block in range(n_q):
        for copy in y_arrivals(block):
            copy.wait_recv()
    for number, place_at in ((0, seq + 1 - 2 * near.c), (1, seq + 1 - 2 * near.c + 2 - 4 * near.x)):
        remote(tok, group_x.at[place_at], sems, TOKC + number, near.core).wait_recv()
        remote(cot, cot_o.at[number], sems, COTC + number, near.core).wait_recv()

    for copy in sent:
        copy.wait_send()
    pl.when(moves)(turn.wait_send)
    keep[1].wait()
    keep[2].wait()
    for k in range(n_q):
        for way in (1, -1):
            block = q - way * k
            there = block >= 0 if way > 0 else block < n_q
            on = above if way > 0 else below

            def gone(block=block, way=way, on=on, k=k):
                for number, ref in lines(block) + corners(block):
                    pl.when(on)(lambda number=number, ref=ref: z_copy(number, ref, way).wait_send())
                if k > 0:
                    for copy in y_copies(block):
                        copy.wait_send()

            pl.when(there)(gone)


def gather_all(place, in_pack, out_pack, tok, cot):
    n_dp, n_seq, n_q = place.n_dp, place.n_seq, place.n_q
    kept = [pl.BlockSpec(memory_space=pl.ANY)] * 5
    total = 11 + 6 * n_q + 4 * n_q
    return pl.pallas_call(
        gather_kernel,
        in_specs=[pl.BlockSpec(memory_space=pltpu.VMEM)] * 4,
        out_specs=kept,
        out_shape=[
            jax.ShapeDtypeStruct((n_dp,) + in_pack.shape, BF16),
            jax.ShapeDtypeStruct((n_dp,) + out_pack.shape, BF16),
            jax.ShapeDtypeStruct((n_seq,) + tok.shape, BF16),
            jax.ShapeDtypeStruct((2,) + cot.shape, BF16),
            jax.ShapeDtypeStruct((2,) + cot.shape, BF16),
        ],
        scratch_shapes=[
            pltpu.SemaphoreType.DMA((total,)),
            pltpu.SemaphoreType.DMA((total,)),
            pltpu.SemaphoreType.DMA((4,)),
        ],
        compiler_params=pltpu.CompilerParams(
            collective_id=0, has_side_effects=True, vmem_limit_bytes=VMEM_BYTES
        ),
        name="gather_all",
    )(in_pack, out_pack, tok, cot)


CHUNKS = 4


class Chunks:
    def __init__(self, sems, rows):
        self.sems, self.size, self.sent = sems, rows // CHUNKS, []

    def rows(self, i):
        return pl.ds(i * self.size, self.size)

    def copy(self, group, i, source, target, device):
        return remote(source, target, self.sems, CHUNKS * group + i, device)

    def go(self, group, i, source, target, device):
        copy = self.copy(group, i, source, target, device)
        copy.start()
        self.sent.append(copy)

    def arrived(self, group, i, target, device):
        self.copy(group, i, target, target, device).wait_recv()

    def finish(self):
        for copy in self.sent:
            copy.wait_send()


def greet(devices):
    for device in devices:
        signal(device)
    pl.semaphore_wait(pltpu.get_barrier_semaphore(), len(devices))


def middle_kernel(
    mixed, w_out, tok, gain, cot_c, cot_o, away, middle, rows, pair_cot,
    part, from_core, to_x, from_x, normed, send, recv, local,
    cots_here, cot_send, cot_recv, cot_local,
):
    near = Near()
    x, c, seq = near.x, near.c, near.seq
    ch = Chunks((send, recv), tok.shape[0])
    all_chunks = range(CHUNKS)
    seq_x, seq_c = seq + 2 - 4 * x, seq + 1 - 2 * c
    seq_cx = seq_c + 2 - 4 * x
    loads = [
        pltpu.make_async_copy(source, cots_here.at[n], cot_local.at[n]) for n, source in enumerate((cot_c, cot_o, away))
    ]
    for load in loads:
        load.start()
    greet([near.core, near.over_x, near.over_y])
    far_cot = remote(cots_here.at[2], pair_cot.at[1, 1], (cot_send, cot_recv), 0, near.core)
    cots = [
        pltpu.make_async_copy(cots_here.at[n], pair_cot.at[i], cot_local.at[n])
        for n, i in enumerate(((0, 0), (0, 1), (1, 0)))
    ]
    CORE_FAR, CORE_NEAR, SUM_X, OWN_X, OWN_Y, OWN_C, FWD_X, FWD_Y, FWD_C = 0, 1, 2, 3, 4, 5, 6, 7, 8
    FWD_C2, FWD_C3 = 9, 10

    for group, slot, at in ((CORE_FAR, 0, seq_cx), (CORE_NEAR, 1, seq_c)):
        part[at, :, :] = dot(mixed[at], w_out[...]).astype(BF16)
        for i in all_chunks:
            r = ch.rows(i)
            ch.go(group, i, part.at[at, r], from_core.at[slot, r], near.core)
        own = seq_x if slot == 0 else seq
        part[own, :, :] = dot(mixed[own], w_out[...]).astype(BF16)
    for i in all_chunks:
        r = ch.rows(i)
        ch.arrived(CORE_FAR, i, from_core.at[0, r], near.core)
        to_x[r, :] = (part[seq_x, r, :].astype(F32) + from_core[0, r, :].astype(F32)).astype(BF16)
        ch.go(SUM_X, i, to_x.at[r], from_x.at[r], near.over_x)
    for load in loads:
        load.wait()
    far_cot.start()
    for copy in cots:
        copy.start()
    kept = []
    for i in all_chunks:
        r = ch.rows(i)
        ch.arrived(CORE_NEAR, i, from_core.at[1, r], near.core)
        ch.arrived(SUM_X, i, from_x.at[r], near.over_x)
        total = tok[r, :].astype(F32) + (
            part[seq, r, :].astype(F32) + from_core[1, r, :].astype(F32) + from_x[r, :].astype(F32)
        )
        middle[r, :] = total
        scale = lax.rsqrt(jnp.mean(total * total, axis=-1, keepdims=True) + EPSILON)
        normed[r, :] = (total * scale * gain[...]).astype(BF16)
        ch.go(OWN_X, i, normed.at[r], rows.at[0, 0, 1, r], near.over_x)
        ch.go(OWN_Y, i, normed.at[r], rows.at[1, 0, 0, r], near.over_y)
        ch.go(OWN_C, i, normed.at[r], rows.at[0, 1, 0, r], near.core)
        keep = pltpu.make_async_copy(normed.at[r], rows.at[0, 0, 0, r], local.at[i])
        keep.start()
        kept.append(keep)
    for i in all_chunks:
        r = ch.rows(i)
        here = rows.at[0, 0, 1, r]
        ch.arrived(OWN_X, i, here, near.over_x)
        if i >= CHUNKS // 2:
            ch.go(FWD_Y, i, here, rows.at[1, 0, 1, r], near.over_y)
        ch.go(FWD_C, i, here, rows.at[0, 1, 1, r], near.core)
        here = rows.at[1, 0, 0, r]
        ch.arrived(OWN_Y, i, here, near.over_y)
        if i < CHUNKS // 2:
            ch.go(FWD_X, i, here, rows.at[1, 0, 1, r], near.over_x)
        ch.go(FWD_C2, i, here, rows.at[1, 1, 0, r], near.core)
    for i in all_chunks:
        r = ch.rows(i)
        here = rows.at[1, 0, 1, r]
        if i < CHUNKS // 2:
            ch.arrived(FWD_X, i, here, near.over_x)
        else:
            ch.arrived(FWD_Y, i, here, near.over_y)
        ch.go(FWD_C3, i, here, rows.at[1, 1, 1, r], near.core)
    for group, at in ((OWN_C, (0, 0)), (FWD_C, (0, 1)), (FWD_C2, (1, 0)), (FWD_C3, (1, 1))):
        for i in all_chunks:
            ch.arrived(group, i, rows.at[at[0], 1, at[1], ch.rows(i)], near.core)
    for keep in kept + cots:
        keep.wait()
    far_cot.wait()
    ch.finish()


def sum_middle(place, mixed, w_out, tok, gain, cot_c, cot_o, away):
    count, width = tok.shape
    vmem, kept = pl.BlockSpec(memory_space=pltpu.VMEM), pl.BlockSpec(memory_space=pl.ANY)
    return pl.pallas_call(
        middle_kernel,
        in_specs=[vmem, vmem, vmem, vmem, kept, kept, kept],
        out_specs=[vmem, kept, kept],
        out_shape=[
            jax.ShapeDtypeStruct((count, width), F32),
            jax.ShapeDtypeStruct((2, 2, 2, count, width), BF16),
            jax.ShapeDtypeStruct((2, 2, 2, count, width), BF16),
        ],
        scratch_shapes=[
            pltpu.VMEM((place.n_seq, count, width), BF16),
            pltpu.VMEM((2, count, width), BF16),
            pltpu.VMEM((count, width), BF16),
            pltpu.VMEM((count, width), BF16),
            pltpu.VMEM((count, width), BF16),
            pltpu.SemaphoreType.DMA((11 * CHUNKS,)),
            pltpu.SemaphoreType.DMA((11 * CHUNKS,)),
            pltpu.SemaphoreType.DMA((CHUNKS,)),
            pltpu.VMEM((3,) + cot_c.shape, BF16),
            pltpu.SemaphoreType.DMA((1,)),
            pltpu.SemaphoreType.DMA((1,)),
            pltpu.SemaphoreType.DMA((3,)),
        ],
        compiler_params=pltpu.CompilerParams(
            collective_id=1, has_side_effects=True, vmem_limit_bytes=VMEM_BYTES
        ),
        name="sum_middle",
    )(mixed.reshape(place.n_seq, count, -1), w_out, tok, gain, cot_c, cot_o, away)


class Piece:
    def __init__(self, kind, refs, start, rows):
        self.kind = kind
        self.part, self.total, self.up, self.down, self.low = refs[:5]
        self.over, self.pair = refs[5:] if len(refs) > 5 else (None, self.part)
        self.start, self.count = start, rows
        self.rows = pl.ds(start, rows)
        self.width = self.low.shape[1]

    def at(self, ref, block):
        return ref.at[block, self.rows]

    def read(self, ref, block):
        return ref[block, self.rows, :].astype(F32)

    def columns(self, block, width):
        return pl.ds(block * width if isinstance(block, int) else pl.multiple_of(block * width, width), width)

    def pair_at(self, block):
        if self.kind == "columns":
            return self.pair.at[self.rows, self.columns(block, self.width)]
        return self.pair.at[block, self.rows]

    def pair_value(self, block):
        if self.kind == "columns":
            return self.pair[self.rows, self.columns(block, self.width)]
        return self.pair[block, self.rows, :]

    def side(self, way):
        return self.up if way > 0 else self.down


class LineSums:
    def __init__(self, near, pieces, sems, local):
        self.near, self.pieces, self.sems, self.local = near, pieces, sems, local
        n_q, n_seq, n_dp = near.n_q, near.n_seq, near.n_dp
        self.ends = n_q + 2 * (n_q - 1)
        self.per = self.ends + n_seq
        owner = near.seq * n_dp + near.dp
        self.to_dp, self.to_seq = owner // n_seq, owner % n_seq
        self.moves = jnp.logical_or(self.to_dp != near.dp, self.to_seq != near.seq)
        self.above, self.below = near.q + 1 < n_q, near.q >= 1

    def y_copy(self, n, block):
        piece, near = self.pieces[n], self.near
        source = piece.at(piece.part, 2 * block + 1 - near.p)
        return remote(source, piece.at(piece.over, block), self.sems, n * self.per + block, near.over_y)

    def z_copy(self, n, k, way, arrival=False):
        piece, n_q = self.pieces[n], self.near.n_q
        side = piece.side(way)
        target = piece.at(side, k - 1)
        if arrival:
            source = target
        elif k == 1:
            source = piece.pair_at(n_q - 1 if way > 0 else 0)
        else:
            source = piece.at(side, k - 2)
        number = n * self.per + n_q + (k - 1) * 2 + (way < 0)
        return remote(source, target, self.sems, number, self.near.z(way))

    def sends(self, k, way):
        q, n_q = self.near.q, self.near.n_q
        if way > 0:
            return jnp.logical_and(q <= k - 1, self.above)
        return jnp.logical_and(q >= n_q - k, self.below)

    def gets(self, k, way):
        q, n_q = self.near.q, self.near.n_q
        if way > 0:
            return jnp.logical_and(q <= k, self.below)
        return jnp.logical_and(q + 1 >= n_q - k, self.above)

    def y_start(self, *numbers):
        for n in numbers:
            for block in range(self.near.n_q):
                self.y_copy(n, block).start()

    def pair_up(self, n):
        piece = self.pieces[n]
        for block in range(self.near.n_q):
            self.y_copy(n, block).wait_recv()
            total = piece.read(piece.part, 2 * block + self.near.p) + piece.read(piece.over, block)
            piece.pair[block, piece.rows, :] = total.astype(BF16)

    def z_step(self, n, k):
        piece, q, n_q = self.pieces[n], self.near.q, self.near.n_q
        for way in (1, -1):

            def stage(way=way):
                side = piece.side(way)
                if k > 1:
                    block = n_q - k + q if way > 0 else k + q - n_q
                    came = self.gets(k - 1, way)

                    def add():
                        self.z_copy(n, k - 1, way, True).wait_recv()
                        total = piece.read(side, k - 2) + piece.pair_value(block).astype(F32)
                        side[k - 2, piece.rows, :] = total.astype(BF16)

                    def begin():
                        side[k - 2, piece.rows, :] = piece.pair_value(block)

                    pl.when(came)(add)
                    pl.when(jnp.logical_not(came))(begin)
                self.z_copy(n, k, way).start()

            pl.when(self.sends(k, way))(stage)

    def owners(self, n):
        piece, near = self.pieces[n], self.near
        if piece.kind == "turn":
            return [(None, self.moves)]
        if piece.kind == "rows":
            other = piece.start // (piece.low.shape[0] // 2)
            return [(other, near.p != other)]
        if piece.kind == "columns":
            return [(near.p, None), (1 - near.p, True)]
        each = piece.low.shape[0] // near.n_seq
        first = piece.start // each
        return [(j, near.seq != j) for j in range(first, first + piece.count // each)]

    def end_refs(self, n, j, source=None):
        piece, near = self.pieces[n], self.near
        if piece.kind == "turn":
            return piece.low.at[piece.rows], piece.total.at[piece.rows]
        if piece.kind == "rows":
            to = pl.ds(piece.start % (piece.low.shape[0] // 2), piece.count)
            p = near.p if source is None else source
            return piece.low.at[piece.rows], piece.total.at[to, piece.columns(p, piece.width)]
        if piece.kind == "columns":
            p = near.p if source is None else source
            return piece.low.at[piece.rows, piece.columns(j, piece.width // 2)], piece.total.at[p, piece.rows]
        each = piece.low.shape[0] // near.n_seq
        seq = near.seq if source is None else source
        return piece.low.at[pl.ds(j * each, each)], piece.total.at[:, piece.columns(seq, piece.width)]

    def end_copy(self, n, j, source=None):
        piece, near = self.pieces[n], self.near
        here, target = self.end_refs(n, j, source)
        first = n * self.per + self.ends
        if piece.kind == "turn":
            return remote(here, target, self.sems, first, {"dp": self.to_dp, "seq": self.to_seq})
        if piece.kind in ("rows", "columns"):
            return remote(target if source is not None else here, target, self.sems, first, near.over_y)
        if source is not None:
            return remote(target, target, self.sems, first + source, {"dp": near.dp, "seq": j})
        return pltpu.make_async_remote_copy(
            src_ref=here, dst_ref=target, send_sem=self.sems[0].at[first + j],
            recv_sem=self.sems[1].at[first + near.seq],
            device_id={"dp": near.dp, "seq": j}, device_id_type=pl.DeviceIdType.MESH,
        )

    def stay_copy(self, n, j):
        here, target = self.end_refs(n, j)
        return pltpu.make_async_copy(here, target, self.local.at[n])

    def finish(self, n):
        piece, k = self.pieces[n], self.near.n_q - 1
        piece.low[piece.rows, :] = piece.pair_value(self.near.q)

        def add(way):
            self.z_copy(n, k, way, True).wait_recv()
            total = piece.low[piece.rows, :].astype(F32) + piece.read(piece.side(way), k - 1)
            piece.low[piece.rows, :] = total.astype(BF16)

        pl.when(self.below)(lambda: add(1))
        pl.when(self.above)(lambda: add(-1))
        for j, away in self.owners(n):
            if piece.kind == "columns":
                (self.end_copy if away else self.stay_copy)(n, j).start()
                continue
            pl.when(away)(lambda j=j: self.end_copy(n, j).start())
            pl.when(jnp.logical_not(away))(lambda j=j: self.stay_copy(n, j).start())

    def z_steps(self, numbers, k):
        for n in numbers:
            self.z_step(n, k)

    def finish_all(self, numbers):
        for n in numbers:
            self.finish(n)

    def arrive(self, n, j):
        piece, near = self.pieces[n], self.near
        self.stay_copy(n, j).wait()
        if piece.kind in ("rows", "columns"):
            self.end_copy(n, j, 1 - near.p).wait_recv()
            return
        for source in range(near.n_seq):
            if source != j:
                self.end_copy(n, j, source).wait_recv()

    def close(self):
        for n, piece in enumerate(self.pieces):
            for j, away in self.owners(n):
                if piece.kind == "turn":
                    pl.when(away)(lambda n=n, j=j: self.end_copy(n, j).wait())
                    pl.when(jnp.logical_not(away))(lambda n=n, j=j: self.stay_copy(n, j).wait())
                elif piece.kind == "columns":
                    self.end_copy(n, j).wait_send() if away else self.arrive(n, j)
                else:
                    pl.when(away)(lambda n=n, j=j: self.end_copy(n, j).wait_send())
                    pl.when(jnp.logical_not(away))(lambda n=n, j=j: self.arrive(n, j))
            if piece.over is not None:
                for block in range(self.near.n_q):
                    self.y_copy(n, block).wait_send()
            for k in range(1, self.near.n_q):
                for way in (1, -1):
                    pl.when(self.sends(k, way))(lambda n=n, k=k, way=way: self.z_copy(n, k, way).wait_send())


def line_scratch(place, parts, cuts):
    n_q, n_seq = place.n_q, place.n_seq
    outs, scratch, pieces = [], [], 0
    for part, (kind, cut) in zip(parts, cuts):
        rows, cols = part.shape[-2:]
        if kind == "columns":
            cols = cols // n_q
        shape = {
            "seq": (rows // n_seq, n_seq * cols),
            "turn": (rows, cols),
            "rows": (rows // 2, 2 * cols),
            "columns": (2, rows, cols // 2),
        }[kind]
        outs.append(jax.ShapeDtypeStruct(shape, BF16))
        sizes = [(n_q - 1, rows, cols)] * 2 + [(rows, cols)]
        if kind in ("seq", "turn"):
            sizes += [(n_q, rows, cols)] * 2
        scratch += [pltpu.VMEM(size, BF16) for size in sizes]
        pieces += cut
    total = pieces * (n_q + 2 * (n_q - 1) + n_seq)
    sems = [
        pltpu.SemaphoreType.DMA((total,)),
        pltpu.SemaphoreType.DMA((total,)),
        pltpu.SemaphoreType.DMA((pieces,)),
    ]
    return outs, scratch + sems


def line_pieces(cuts, parts, totals, scratch):
    pieces, scratch = [], list(scratch)
    for (kind, cut), part, total in zip(cuts, parts, totals):
        take = 5 if kind in ("seq", "turn") else 3
        refs = [part, total] + scratch[:take]
        scratch = scratch[take:]
        rows = part.shape[-2] // cut
        pieces += [Piece(kind, refs, i * rows, rows) for i in range(cut)]
    return pieces


def greet_lines(near, others=()):
    above, below = near.q + 1 < near.n_q, near.q >= 1
    for device in others:
        signal(device)
    pl.when(above)(lambda: signal(near.z(1)))
    pl.when(below)(lambda: signal(near.z(-1)))
    return len(others) + above.astype(jnp.int32) + below.astype(jnp.int32)


def weight_sums_kernel(cuts, *refs):
    count = len(cuts)
    near = Near()
    x, c, seq, p, q, n_q = near.x, near.c, near.seq, near.p, near.q, near.n_q
    part, tok, back, gain, mid_grad = refs[:5]
    parts = refs[5 : 5 + count]
    grad_tok, gains = refs[5 + count : 7 + count]
    totals = refs[7 + count : 7 + 2 * count]
    own, from_core, from_x, gain_near, gain_line, send, recv, local, load, gain_send, gain_recv = refs[
        7 + 2 * count : 18 + 2 * count
    ]
    line_refs = refs[18 + 2 * count :]
    lines = LineSums(near, line_pieces(cuts, parts, totals, line_refs[:-3]), line_refs[-3:-1], line_refs[-1])
    ch = Chunks((send, recv), tok.shape[0])
    seq_x, seq_c = seq + 2 - 4 * x, seq + 1 - 2 * c
    seq_cx = seq_c + 2 - 4 * x
    loads = [
        pltpu.make_async_copy(part.at[at], own.at[i], load.at[i]) for i, at in enumerate((seq_x, seq))
    ]
    for copy in loads:
        copy.start()
    origin = near.dp * near.n_seq + seq
    others = [{"dp": near.dp, "seq": (seq + d) % near.n_seq} for d in range(1, near.n_seq)]
    others += [near.over_y]
    along = [{"dp": 2 * ((q + d) % n_q) + p, "seq": seq} for d in range(1, n_q)]
    for device in others + along:
        signal(device)
    pl.when(lines.moves)(lambda: signal({"dp": origin % near.n_dp, "seq": origin // near.n_dp}))
    pl.semaphore_wait(
        pltpu.get_barrier_semaphore(), len(others + along) + lines.moves.astype(jnp.int32)
    )
    CORE_FAR, CORE_NEAR, SUM_X = range(3)
    for group, at, slot in ((CORE_FAR, seq_cx, 0), (CORE_NEAR, seq_c, 1)):
        for i in range(CHUNKS):
            r = ch.rows(i)
            ch.go(group, i, part.at[at, r], from_core.at[slot, r], near.core)
    ready = [n for n, piece in enumerate(lines.pieces) if piece.over is None]
    waiting = [n for n, piece in enumerate(lines.pieces) if piece.over is not None]
    ahead = 2
    lines.y_start(*waiting[:ahead])
    lines.z_steps(ready, 1)
    for copy in loads:
        copy.wait()
    for i in range(CHUNKS):
        r = ch.rows(i)
        ch.arrived(CORE_FAR, i, from_core.at[0, r], near.core)
        from_core[0, r, :] = (own[0, r, :].astype(F32) + from_core[0, r, :].astype(F32)).astype(BF16)
        ch.go(SUM_X, i, from_core.at[0, r], from_x.at[r], near.over_x)
    lines.z_steps(ready, 2)
    gain_sum = jnp.zeros_like(gain)
    for i in range(CHUNKS):
        r = ch.rows(i)
        ch.arrived(CORE_NEAR, i, from_core.at[1, r], near.core)
        ch.arrived(SUM_X, i, from_x.at[r], near.over_x)
        total = own[1, r, :].astype(F32) + from_core[1, r, :].astype(F32) + from_x[r, :].astype(F32)
        value = tok[r, :].astype(F32)
        scale = lax.rsqrt(jnp.mean(value * value, axis=-1, keepdims=True) + EPSILON)
        unit = value * scale
        gain_sum = gain_sum + jnp.sum(total * unit, axis=0, keepdims=True)
        lifted = total * gain[...]
        grad_tok[r, :] = back[r, :] + scale * (
            lifted - unit * jnp.mean(lifted * unit, axis=-1, keepdims=True)
        )

    gain_near[0, :, :] = jnp.concatenate(
        [gain_sum, mid_grad[...], jnp.zeros((TILE - 2, gain.shape[1]), F32)], axis=0
    )
    pairs = [
        remote(gain_near.at[2 * i], gain_near.at[2 * i + 1], (gain_send, gain_recv), i, device)
        for i, device in enumerate((near.core, near.over_x, near.over_y))
    ]
    copies = [
        remote(gain_near.at[6], gain_line.at[i], (gain_send, gain_recv), 3 + i, device) for i, device in enumerate(along)
    ]

    def gain_step(i):
        if 0 < i <= 3:
            pairs[i - 1].wait()
            gain_near[2 * i, :, :] = gain_near[2 * i - 2, :, :] + gain_near[2 * i - 1, :, :]
        for copy in pairs[i : i + 1] if i < 3 else copies if i == 3 else []:
            copy.start()

    gain_step(0)
    for k in range(3, n_q):
        lines.z_steps(ready, k)
    gain_step(1)
    for t in range(len(waiting) + n_q):
        if t < len(waiting):
            lines.pair_up(waiting[t])
            lines.y_start(*waiting[t + ahead : t + ahead + 1])
        for k in range(1, n_q):
            if 0 <= t - (k - 1) < len(waiting):
                lines.z_step(waiting[t - (k - 1)], k)
        if 0 <= t - (n_q - 1) < len(waiting):
            lines.finish(waiting[t - (n_q - 1)])
        if t == 0:
            gain_step(2)
            lines.finish_all(ready)
        if t == 2:
            gain_step(3)
    total = gain_near[6, :, :]
    for i, copy in enumerate(copies):
        copy.wait()
        total = total + gain_line[i, :, :]
    gains[...] = total
    ch.finish()
    lines.close()


def weight_sums(place, part, tok, back, gain, mid_grad, parts, cuts):
    rows, width = tok.shape
    vmem, kept = pl.BlockSpec(memory_space=pltpu.VMEM), pl.BlockSpec(memory_space=pl.ANY)
    outs, scratch = line_scratch(place, parts, cuts)
    n_q = place.n_q
    return pl.pallas_call(
        partial(weight_sums_kernel, cuts),
        in_specs=[kept] + [vmem] * (4 + len(parts)),
        out_specs=[vmem, vmem] + [kept] * len(parts),
        out_shape=[jax.ShapeDtypeStruct((rows, width), F32), jax.ShapeDtypeStruct((TILE, width), F32)] + outs,
        scratch_shapes=[
            pltpu.VMEM((2, rows, width), BF16),
            pltpu.VMEM((2, rows, width), BF16),
            pltpu.VMEM((rows, width), BF16),
            pltpu.VMEM((7, TILE, width), F32),
            pltpu.VMEM((n_q - 1, TILE, width), F32),
            pltpu.SemaphoreType.DMA((3 * CHUNKS,)),
            pltpu.SemaphoreType.DMA((3 * CHUNKS,)),
            pltpu.SemaphoreType.DMA((1,)),
            pltpu.SemaphoreType.DMA((2,)),
            pltpu.SemaphoreType.DMA((2 + n_q,)),
            pltpu.SemaphoreType.DMA((2 + n_q,)),
        ]
        + scratch,
        compiler_params=pltpu.CompilerParams(
            collective_id=3, has_side_effects=True, vmem_limit_bytes=VMEM_BYTES
        ),
        name="weight_sums",
    )(part, tok, back, gain, mid_grad, *parts)


class PlaneSum:
    FAR, TO_X, TO_Y, NEAR = range(4)
    AT = {0: (1, 1), 1: (0, 1), 2: (1, 0), 3: (0, 0)}

    def __init__(self, near, ch, groups, part, local, own, from_core, corner_x, corner_y, got_x, got_y):
        self.near, self.ch, self.part, self.own, self.from_core = near, ch, part, own, from_core
        self.corner_x, self.corner_y, self.got_x, self.got_y = corner_x, corner_y, got_x, got_y
        self.core_group = groups
        self.cx, self.cy, self.gx, self.gy = range(groups + 4, groups + 8)
        half = CHUNKS // 2
        self.half, self.first, self.last = half, range(half), range(half, CHUNKS)
        self.loads = [pltpu.make_async_copy(part.at[i, 0], own.at[i], local.at[i]) for i in range(2)]
        for load in self.loads:
            load.start()

    def to_core(self, group, chunks):
        other_p, other_x = self.AT[group]
        for i in chunks:
            r = self.ch.rows(i)
            self.ch.go(
                self.core_group + group, i, self.part.at[other_p, 1, other_x, r], self.from_core.at[group, r], self.near.core
            )

    def on_chip(self, group, i):
        r = self.ch.rows(i)
        other_p, other_x = self.AT[group]
        self.ch.arrived(self.core_group + group, i, self.from_core.at[group, r], self.near.core)
        return self.own[other_p, other_x, r, :].astype(F32) + self.from_core[group, r, :].astype(F32)

    def start(self):
        for load in self.loads:
            load.wait()
        self.to_core(self.FAR, (0, self.half, 1, self.half + 1))
        self.to_core(self.TO_X, self.first)
        self.to_core(self.TO_Y, self.last)
        self.to_core(self.TO_X, self.last)
        self.to_core(self.TO_Y, self.first)
        self.to_core(self.NEAR, range(CHUNKS))

    def corners(self):
        near, ch = self.near, self.ch
        for i in (0, self.half, 1, self.half + 1):
            r = ch.rows(i)
            self.from_core[self.FAR, r, :] = self.on_chip(self.FAR, i).astype(BF16)
            if i < self.half:
                ch.go(self.cx, i, self.from_core.at[self.FAR, r], self.corner_x.at[r], near.over_x)
            else:
                b = ch.rows(i - self.half)
                ch.go(self.cy, i - self.half, self.from_core.at[self.FAR, r], self.corner_y.at[b], near.over_y)

    def straight(self):
        for i, j in zip(self.first, self.last):
            self.along(self.TO_X, i, self.on_chip(self.TO_X, i))
            self.along(self.TO_Y, j, self.on_chip(self.TO_Y, j))

    def along(self, group, i, total):
        r = self.ch.rows(i)
        self.from_core[group, r, :] = total.astype(BF16)
        if group == self.TO_X:
            self.ch.go(self.gx, i, self.from_core.at[group, r], self.got_x.at[r], self.near.over_x)
        else:
            self.ch.go(self.gy, i, self.from_core.at[group, r], self.got_y.at[r], self.near.over_y)

    def turned(self):
        ch = self.ch
        for i, j in zip(self.first, self.last):
            b = ch.rows(j - self.half)
            ch.arrived(self.cy, j - self.half, self.corner_y.at[b], self.near.over_y)
            self.along(self.TO_X, j, self.on_chip(self.TO_X, j) + self.corner_y[b, :].astype(F32))
            r = ch.rows(i)
            ch.arrived(self.cx, i, self.corner_x.at[r], self.near.over_x)
            self.along(self.TO_Y, i, self.on_chip(self.TO_Y, i) + self.corner_x[r, :].astype(F32))

    def total(self, i):
        r = self.ch.rows(i)
        total = self.on_chip(self.NEAR, i)
        self.ch.arrived(self.gx, i, self.got_x.at[r], self.near.over_x)
        self.ch.arrived(self.gy, i, self.got_y.at[r], self.near.over_y)
        return total + self.got_x[r, :].astype(F32) + self.got_y[r, :].astype(F32)

    @staticmethod
    def scratch(count, width):
        block = pltpu.VMEM((count, width), BF16)
        half = pltpu.VMEM((count // 2, width), BF16)
        return [
            pltpu.VMEM((2, 2, count, width), BF16), pltpu.VMEM((4, count, width), BF16), half, half, block, block
        ]


def back_middle_kernel(cuts, *refs):
    count = len(cuts)
    part, down_part, middle, cot, gain = refs[:5]
    grads = refs[5 : 5 + count]
    back, rows, gain_grad, result = refs[5 + count : 9 + count]
    totals = refs[9 + count : 9 + 2 * count]
    rest = refs[9 + 2 * count :]
    plane_a, plane_b, low = rest[:6], rest[6:12], rest[12]
    send, recv, local, loads_a, loads_b = rest[13:18]
    line_refs = rest[18:]
    near = Near()
    x, c, seq = near.x, near.c, near.seq
    ch = Chunks((send, recv), cot.shape[0])
    seq_x, seq_c = seq + 2 - 4 * x, seq + 1 - 2 * c
    seq_cx = seq_c + 2 - 4 * x
    lines = LineSums(near, line_pieces(cuts, grads, totals, line_refs[:-3]), line_refs[-3:-1], line_refs[-1])
    main = PlaneSum(near, ch, 0, part, loads_a, *plane_a)
    side = PlaneSum(near, ch, 8, down_part, loads_b, *plane_b)
    expected = greet_lines(near, [near.core, near.over_x, near.over_y])
    pl.semaphore_wait(pltpu.get_barrier_semaphore(), expected)
    OWN_X, OWN_C, FWD_C = 16, 17, 18
    half = len(lines.pieces) // 2
    early, late = range(half), range(half, 2 * half)
    steps = range(1, near.n_q)
    schedule = [partial(lines.z_steps, group, k) for k in steps for group in (early, late)]
    schedule += [partial(lines.finish_all, early), partial(lines.finish_all, late)]
    schedule = iter(schedule)

    def along_z():
        work = next(schedule, None)
        if work is not None:
            work()

    main.start()
    along_z()
    along_z()
    main.corners()
    along_z()
    main.straight()
    main.turned()
    side.start()
    along_z()
    gain_sum = jnp.zeros_like(gain)
    kept = []
    for i in range(CHUNKS):
        r = ch.rows(i)
        total = main.total(i)
        value = middle[r, :]
        scale = lax.rsqrt(jnp.mean(value * value, axis=-1, keepdims=True) + EPSILON)
        unit = value * scale
        gain_sum = gain_sum + jnp.sum(total * unit, axis=0, keepdims=True)
        lifted = total * gain[...]
        whole = cot[r, :].astype(F32) + scale * (lifted - unit * jnp.mean(lifted * unit, axis=-1, keepdims=True))
        back[r, :] = whole
        low[r, :] = whole.astype(BF16)
        ch.go(OWN_X, i, low.at[r], rows.at[seq, r], near.over_x)
        ch.go(OWN_C, i, low.at[r], rows.at[seq, r], near.core)
        keep = pltpu.make_async_copy(low.at[r], rows.at[seq, r], local.at[i])
        keep.start()
        kept.append(keep)
    gain_grad[...] = gain_sum
    side.corners()
    along_z()
    side.straight()
    along_z()
    for i in range(CHUNKS):
        here = rows.at[seq_x, ch.rows(i)]
        ch.arrived(OWN_X, i, here, near.over_x)
        ch.go(FWD_C, i, here, here, near.core)
    side.turned()
    along_z()
    for i in range(CHUNKS):
        r = ch.rows(i)
        result[r, :] = (middle[r, :] + side.total(i)).astype(BF16)
    for _ in range(2 * near.n_q):
        along_z()
    for i in range(CHUNKS):
        ch.arrived(OWN_C, i, rows.at[seq_c, ch.rows(i)], near.core)
        ch.arrived(FWD_C, i, rows.at[seq_cx, ch.rows(i)], near.core)
    for keep in kept:
        keep.wait()
    ch.finish()
    lines.close()


def sum_back_middle(place, part, down_part, middle, cot, gain, grads):
    count, width = cot.shape
    cuts = (("columns", 4), ("rows", 4))
    vmem, kept = pl.BlockSpec(memory_space=pltpu.VMEM), pl.BlockSpec(memory_space=pl.ANY)
    outs, scratch = line_scratch(place, grads, cuts)
    return pl.pallas_call(
        partial(back_middle_kernel, cuts),
        in_specs=[kept, kept] + [vmem] * (3 + len(grads)),
        out_specs=[vmem, kept, vmem, vmem] + [kept] * len(grads),
        out_shape=[
            jax.ShapeDtypeStruct((count, width), F32),
            jax.ShapeDtypeStruct((place.n_seq, count, width), BF16),
            jax.ShapeDtypeStruct((1, width), F32),
            jax.ShapeDtypeStruct((count, width), BF16),
        ]
        + outs,
        scratch_shapes=PlaneSum.scratch(count, width)
        + PlaneSum.scratch(count, width)
        + [
            pltpu.VMEM((count, width), BF16),
            pltpu.SemaphoreType.DMA((19 * CHUNKS,)),
            pltpu.SemaphoreType.DMA((19 * CHUNKS,)),
            pltpu.SemaphoreType.DMA((CHUNKS,)),
            pltpu.SemaphoreType.DMA((2,)),
            pltpu.SemaphoreType.DMA((2,)),
        ]
        + scratch,
        compiler_params=pltpu.CompilerParams(
            collective_id=2, has_side_effects=True, vmem_limit_bytes=VMEM_BYTES
        ),
        name="sum_back_middle",
    )(part, down_part, middle, cot, gain, *grads)


def entry_kernel(x_ref, w_ref, normed_ref, branch_ref, inner_ref, gains_ref):
    own = branch_ref.shape[1]

    @pl.when(pl.program_id(0) == 0)
    def _():
        gains_ref[...] = w_ref[:, 2 * own :].astype(F32).T[:TILE, :]

    value = x_ref[...].astype(F32)
    scale = lax.rsqrt(jnp.mean(value * value, axis=-1, keepdims=True) + EPSILON)
    normed = (value * scale * gains_ref[0:1, :]).astype(BF16)
    normed_ref[...] = normed
    inner_ref[...] = dot(normed, w_ref[:, own : 2 * own]).astype(BF16)
    branch_ref[...] = dot(normed, w_ref[:, :own])


def entry_products(x, weights, own, tile):
    rows, width = x.shape
    whole = lambda shape: pl.BlockSpec(shape, lambda i: (0, 0), pipeline_mode=pl.Buffered(1))
    by_tile = lambda cols: pl.BlockSpec((tile, cols), lambda i: (i, 0))
    return pl.pallas_call(
        entry_kernel,
        grid=(rows // tile,),
        in_specs=[by_tile(width), whole(weights.shape)],
        out_specs=[by_tile(width), by_tile(own), by_tile(own), pl.BlockSpec((TILE, width), lambda i: (0, 0))],
        out_shape=[
            jax.ShapeDtypeStruct((rows, width), BF16),
            jax.ShapeDtypeStruct((rows, own), F32),
            jax.ShapeDtypeStruct((rows, own), BF16),
            jax.ShapeDtypeStruct((TILE, width), F32),
        ],
        compiler_params=pltpu.CompilerParams(vmem_limit_bytes=VMEM_BYTES),
        cost_estimate=pl.CostEstimate(
            flops=4 * rows * width * own, bytes_accessed=weights.size * 2 + rows * (width * 4 + own * 6), transcendentals=rows
        ),
        name="entry_products",
    )(x, weights)


def mlp_kernel(
    p_ref, x_ref, cot_ref, gate_ref, up_ref, down_ref, hidden_ref, back_gate_ref, back_up_ref, down_part_ref, back_ref
):
    x = x_ref[...]
    gate_pre = dot(x, gate_ref[...])
    up_pre = dot(x, up_ref[...])
    back_hidden = contract_cols(cot_ref[...], down_ref[...])
    value, slope = gelu_parts(gate_pre)
    hidden = (value * up_pre).astype(BF16)
    back_gate = (back_hidden * up_pre * slope).astype(BF16)
    back_up = (back_hidden * value).astype(BF16)
    hidden_ref[...] = hidden
    back_gate_ref[...] = back_gate
    back_up_ref[...] = back_up
    down_part_ref[...] = dot(hidden, down_ref[...]).astype(BF16)
    back_ref[...] = (contract_cols(back_gate, gate_ref[...]) + contract_cols(back_up, up_ref[...])).astype(BF16)


def mlp_products(p, x, cot, gate_weight, up_weight, down_weight, tile):
    rows, width = x.shape
    units = gate_weight.shape[1] // 2
    by_tile = lambda cols: pl.BlockSpec((tile, cols), lambda i, p: (i, 0))
    half = lambda shape, at: pl.BlockSpec(shape, at, pipeline_mode=pl.Buffered(1))
    columns = half((width, units), lambda i, p: (0, p[0]))
    return pl.pallas_call(
        mlp_kernel,
        grid_spec=pltpu.PrefetchScalarGridSpec(
            num_scalar_prefetch=1,
            grid=(rows // tile,),
            in_specs=[
                by_tile(width), by_tile(width), columns, columns, half((units, width), lambda i, p: (p[0], 0))
            ],
            out_specs=[by_tile(units)] * 3 + [by_tile(width)] * 2,
        ),
        out_shape=[jax.ShapeDtypeStruct((rows, units), BF16)] * 3 + [jax.ShapeDtypeStruct((rows, width), BF16)] * 2,
        compiler_params=pltpu.CompilerParams(vmem_limit_bytes=VMEM_BYTES),
        cost_estimate=pl.CostEstimate(
            flops=12 * rows * width * units, bytes_accessed=rows * width * 8 + units * width * 6, transcendentals=rows * units
        ),
        name="mlp_products",
    )(p, x, cot, gate_weight, up_weight, down_weight)


def mlp_grads_kernel(x_ref, cot_ref, hidden_ref, back_gate_ref, back_up_ref, down_ref, gate_ref, up_ref):
    x = x_ref[...]
    down_ref[...] = contract_rows(hidden_ref[...], cot_ref[...]).astype(BF16)
    gate_ref[...] = contract_rows(x, back_gate_ref[...]).astype(BF16)
    up_ref[...] = contract_rows(x, back_up_ref[...]).astype(BF16)


def mlp_grads(x, cot, hidden, back_gate, back_up, tile):
    rows, width = x.shape
    units = hidden.shape[1]
    columns = pl.BlockSpec((rows, tile), lambda i: (0, i))
    whole = pl.BlockSpec((rows, units), lambda i: (0, 0), pipeline_mode=pl.Buffered(1))
    by_tile = pl.BlockSpec((tile, units), lambda i: (i, 0))
    return pl.pallas_call(
        mlp_grads_kernel,
        grid=(width // tile,),
        in_specs=[columns, columns, whole, whole, whole],
        out_specs=[pl.BlockSpec((units, tile), lambda i: (0, i)), by_tile, by_tile],
        out_shape=[jax.ShapeDtypeStruct((units, width), BF16)] + [jax.ShapeDtypeStruct((width, units), BF16)] * 2,
        compiler_params=pltpu.CompilerParams(vmem_limit_bytes=VMEM_BYTES),
        cost_estimate=pl.CostEstimate(
            flops=6 * rows * width * units, bytes_accessed=rows * width * 4 + units * (rows + width) * 6, transcendentals=0
        ),
        name="mlp_grads",
    )(x, cot, hidden, back_gate, back_up)


def exit_kernel(
    normed_ref, back_out_ref, w_ref, branch_ref, inner_ref, mixed_ref,
    grad_branch_ref, grad_inner_ref, grad_output_ref, part_ref,
):
    own = branch_ref.shape[1]
    normed = normed_ref[...]
    grad_branch_ref[...] = contract_rows(normed, branch_ref[...]).astype(BF16)
    grad_inner_ref[...] = contract_rows(normed, inner_ref[...]).astype(BF16)
    grad_output_ref[...] = contract_rows(mixed_ref[...], back_out_ref[...]).astype(BF16)
    part_ref[...] = (
        contract_cols(branch_ref[...], w_ref[:, :own]) + contract_cols(inner_ref[...], w_ref[:, own : 2 * own])
    ).astype(BF16)


def exit_products(normed, back_out, weights, back_branch, back_inner, mixed, tile):
    rows, width = normed.shape
    own = mixed.shape[1]
    columns = pl.BlockSpec((rows, tile), lambda i: (0, i))
    whole = pl.BlockSpec((rows, own), lambda i: (0, 0), pipeline_mode=pl.Buffered(1))
    by_tile = lambda cols: pl.BlockSpec((tile, cols), lambda i: (i, 0))
    return pl.pallas_call(
        exit_kernel,
        grid=(width // tile,),
        in_specs=[columns, columns, by_tile(weights.shape[1]), whole, whole, whole],
        out_specs=[by_tile(own), by_tile(own), pl.BlockSpec((own, tile), lambda i: (0, i)), columns],
        out_shape=[
            jax.ShapeDtypeStruct((width, own), BF16),
            jax.ShapeDtypeStruct((width, own), BF16),
            jax.ShapeDtypeStruct((own, width), BF16),
            jax.ShapeDtypeStruct((rows, width), BF16),
        ],
        compiler_params=pltpu.CompilerParams(vmem_limit_bytes=VMEM_BYTES),
        cost_estimate=pl.CostEstimate(
            flops=10 * rows * width * own, bytes_accessed=rows * width * 6 + own * (rows + width) * 10, transcendentals=0
        ),
        name="exit_products",
    )(normed, back_out, weights, back_branch, back_inner, mixed)


def shards(
    tokens, row_lengths, branch_weight, inner_weight, output_weight, rate_weight, entry_weight,
    rate_bias, entry_bias, conv_weight, conv_bias, recur_param, norm_gain, mlp_gain,
    gate_weight, up_weight, down_weight, cotangent,
):
    place = Place()
    n_dp, n_seq = place.n_dp, place.n_seq
    tok, width = tokens.shape
    count = tok * n_seq
    rec = branch_weight.shape[1]
    own = rec // n_seq
    blocks = max(-(-(own * (s + 1)) // BLOCK) - own * s // BLOCK for s in range(n_seq))
    spread = blocks * BLOCK
    d_rows = branch_weight.shape[0]
    r_rows = output_weight.shape[0]

    gains = jnp.stack([norm_gain, mlp_gain], axis=1)
    gains = jnp.pad(gains, ((0, 0), (0, LANES - 2)))
    cut = lambda w: w.reshape(d_rows, n_seq, own).swapaxes(0, 1)
    in_pack = jnp.concatenate(
        [cut(branch_weight), cut(inner_weight), jnp.broadcast_to(gains[None], (n_seq,) + gains.shape)], axis=2
    )
    vectors = jnp.concatenate(
        [conv_weight, jnp.stack([conv_bias, rate_bias, entry_bias, recur_param])], axis=0
    )
    vectors = jnp.pad(vectors.T, ((0, 0), (0, LANES - 2 * WIDTH)))
    out_pack = jnp.concatenate([output_weight, rate_weight, entry_weight, vectors], axis=1)
    fast = place.n_x == 2
    if fast:
        in_all, out_all, group_x, cot_c, cot_o = gather_all(place, in_pack, out_pack, tokens, cotangent)
        in_all = in_all.reshape(n_dp * n_seq * d_rows, -1)
        out_all = out_all.reshape(n_dp * r_rows, -1)
    else:
        in_pack = lax.all_to_all(in_pack, "seq", 0, 0, tiled=True).reshape(n_seq * d_rows, -1)
        out_pack = turned(place, out_pack, False)
        in_all = lax.all_gather(in_pack, "dp", axis=0, tiled=True)
        out_all = lax.all_gather(out_pack, "dp", axis=0, tiled=True)
        group_x = gather_seq(place, tokens)
        group_c = gather_seq(place, cotangent)
    w_out = out_all[:, :width]
    gate_rows = window(place, out_all[:, width : width + 2 * BLOCK], 0, own, spread)
    w_rate, w_entry = gate_rows[:, :BLOCK], gate_rows[:, BLOCK:]
    vec = out_all[:, width + 2 * BLOCK : width + 2 * BLOCK + 2 * WIDTH].astype(F32).T
    taps = jnp.pad(vec[: WIDTH + 1], ((0, 7 - WIDTH), (0, 0)))
    gate_vec = jnp.pad(vec[WIDTH + 1 :], ((0, 9 - 2 * WIDTH + WIDTH), (0, 0)))
    first = own * place.seq - jnp.minimum(own * place.seq // BLOCK * BLOCK, rec - spread)
    owned = lambda a, axis: lax.dynamic_slice_in_dim(a, first, own, axis=axis) if spread != own else a

    group_x = group_x.reshape(count, width)
    away = place.swap_pair(cot_c if fast else group_c)
    offsets = row_offsets(row_lengths[0], jnp.arange(count, dtype=jnp.int32))[:, None]

    normed, branch_pre, inner, gain_rows = entry_products(group_x, in_all, own, ENTRY_TILE)
    gain_in, gain_mid = gain_rows[0:1], gain_rows[1:2]
    heads = partial(jnp.einsum, preferred_element_type=F32)
    if fast:
        gate_first = (own * place.seq % BLOCK // LANES).astype(jnp.int32)[None]
        (conv_wide,) = by_block(
            conv_wide_kernel, gate_first, [("own", inner), ("own", taps), ("one", offsets)],
            [("wide", (count, spread), BF16)], 0, own,
        )
        conv_wide = fill_edge(place, conv_wide, own)
        gate_ins = [("block", conv_wide), ("columns", w_rate), ("columns", w_entry), ("wide", conv_wide)]
        gate_ins += [("own", branch_pre), ("own", gate_vec), ("one", offsets)]
        states, mixed = by_block(
            forward_gates_kernel, gate_first, gate_ins,
            [("own", (count, own), F32), ("own", (count, own), BF16)], 2, own,
        )
    else:
        (conv,) = by_channel(conv_kernel, [inner, taps, offsets], [((count,), BF16)], own)
        conv_wide = window(place, conv, 1, own, spread)
        conv_heads = conv_wide.reshape(count, blocks, BLOCK)
        pre_rate, pre_entry = (
            owned(heads("tbc,bcd->tbd", conv_heads, w.reshape(blocks, BLOCK, BLOCK)).reshape(count, spread), 1)
            for w in (w_rate, w_entry)
        )
        states, mixed = by_channel(
            forward_kernel,
            [pre_rate, pre_entry, conv, branch_pre, gate_vec, offsets],
            [((count,), F32), ((count,), BF16)],
            own,
        )
    mixed, away = lax.optimization_barrier((mixed, away))
    whole_x = tokens.astype(F32)
    if fast:
        middle, rows, pair_cot = sum_middle(place, mixed, w_out, tokens, gain_mid, cot_c, cot_o, away)
    else:
        out_part = dot(mixed, w_out).astype(BF16).reshape(n_seq, tok, width)
        middle = whole_x + scatter_seq(place, out_part)
        rows = gather_plane(place, rms_norm(middle, gain_mid).astype(BF16))
        pair_cot = jnp.stack([jnp.where(place.p == 0, group_c, away), jnp.where(place.p == 0, away, group_c)])
    rows, pair_cot = rows.reshape(2 * count, width), pair_cot.reshape(2 * count, width)

    units = gate_weight.shape[1] // 2
    hidden, back_gate, back_up, down_part, back_part = mlp_products(
        place.p.astype(jnp.int32)[None], rows, pair_cot, gate_weight, up_weight, down_weight, MLP_TILE
    )

    n_q = place.n_q
    grad_down_part, grad_gate_part, grad_up_part = mlp_grads(rows, pair_cot, hidden, back_gate, back_up, GRAD_TILE)
    grad_gate_part, grad_up_part = (a.reshape(n_q, -1, units) for a in (grad_gate_part, grad_up_part))
    if fast:
        plane = (2, 2, 2, tok, width)
        back_middle, back_out, grad_mlp_gain, result, down_sum, gate_sum = sum_back_middle(
            place, back_part.reshape(plane), down_part.reshape(plane), middle, cotangent, gain_mid,
            [grad_down_part, grad_gate_part],
        )
        grad_mlp_gain = grad_mlp_gain[0]
    else:
        plane = (2, n_seq, tok, width)
        result = (middle + scatter_plane(place, down_part.reshape(plane))).astype(BF16)
        back_norm, grad_mlp_gain = rms_back(middle, gain_mid, scatter_plane(place, back_part.reshape(plane)))
        back_middle = cotangent.astype(F32) + back_norm
        back_out = gather_seq(place, back_middle.astype(BF16))
        step = q_step(place)
        strip = width // n_q
        down_sum = line_sum(
            lambda i: lax.dynamic_slice_in_dim(grad_down_part, i * strip, strip, 1), n_q, place.q, step
        )
        gate_sum, up_sum = (
            line_sum(partial(lax.dynamic_index_in_dim, a, axis=0, keepdims=False), n_q, place.q, step)
            for a in (grad_gate_part, grad_up_part)
        )
        down_sum, gate_sum, up_sum = (
            split_pair(place, a, axis) for a, axis in ((down_sum, 1), (gate_sum, 0), (up_sum, 0))
        )
    back_out = back_out.reshape(count, width)

    back_mixed = contract_cols(back_out, w_out)
    if fast:
        back_branch, back_gates, direct, gate_sums = by_block(
            backward_gates_kernel, gate_first, gate_ins + [("own", states), ("own", back_mixed)],
            [("own", (count, own), BF16), ("wide2", (2, count, spread), BF16), ("own", (count, own), F32),
             ("own", (TILE, own), F32)], 2, own,
        )
        back_gates = fill_edge(place, back_gates, own)
        back_inner, conv_sums = by_block(
            conv_back_gates_kernel, gate_first,
            [("block2", back_gates), ("rows", w_rate), ("rows", w_entry), ("own", direct), ("own", inner),
             ("own", taps), ("one", offsets)],
            [("own", (count, own), BF16), ("own", (TILE, own), F32)], 1, own,
        )
    else:
        back_branch, back_gates, direct, gate_sums = by_channel(
            backward_kernel,
            [pre_rate, pre_entry, conv, branch_pre, gate_vec, offsets, states, back_mixed],
            [((count,), BF16), ((2, count), BF16), ((count,), F32), ((TILE,), F32)],
            own,
        )
        back_gates = jnp.stack([window(place, a, 1, own, spread) for a in (back_gates[0], back_gates[1])])
        gates_back = sum(
            heads("tbd,bcd->tbc", a.reshape(count, blocks, BLOCK), w.reshape(blocks, BLOCK, BLOCK)).reshape(count, spread)
            for a, w in ((back_gates[0], w_rate), (back_gates[1], w_entry))
        )
        back_inner, conv_sums = by_channel(
            conv_back_kernel,
            [direct, owned(gates_back, 1), inner, taps, offsets],
            [((count,), BF16), ((TILE,), F32)],
            own,
        )
    grad_rate_part, grad_entry_part = (
        owned(
            jnp.concatenate(
                [contract_rows(conv_wide[:, b : b + BLOCK], a[:, b : b + BLOCK]) for b in range(0, spread, BLOCK)], axis=0
            ),
            0,
        )
        for a in (back_gates[0], back_gates[1])
    )
    grad_branch_part, grad_inner_part, grad_output_part, normed_part = exit_products(
        normed, back_out, in_all, back_branch, back_inner, mixed, EXIT_TILE
    )
    normed_part = normed_part.reshape(n_seq, tok, width)

    sums = jnp.concatenate([conv_sums[: WIDTH + 1], gate_sums[:3]], axis=0).T
    sums = jnp.pad(sums, ((0, 0), (0, LANES - 2 * WIDTH))).astype(BF16)
    gate_grads = jnp.concatenate([grad_rate_part.astype(BF16), grad_entry_part.astype(BF16), sums], axis=1)
    parts = [
        a.reshape(n_dp, -1, a.shape[1]) for a in (grad_output_part, grad_branch_part, gate_grads, grad_inner_part)
    ]
    if fast:
        grad_tokens, gains, up_sum, output_sum, branch_sum, gates_sum, inner_sum = weight_sums(
            place, normed_part, tokens, back_middle, gain_in, grad_mlp_gain[None], [grad_up_part] + parts,
            (("rows", 4), ("turn", 1), ("seq", 2), ("turn", 1), ("seq", 2)),
        )
        gains = lax.dynamic_slice_in_dim(gains[:2], (place.dp * n_seq + place.seq) * d_rows, d_rows, axis=1)
    else:
        back_x, grad_norm_gain = rms_back(whole_x, gain_in, scatter_seq(place, normed_part))
        grad_tokens = back_middle + back_x
        gains = lax.psum_scatter(
            jnp.stack([grad_norm_gain, grad_mlp_gain]), BOTH, scatter_dimension=1, tiled=True
        )
        totals = [sum_dp(place, a) for a in parts]
        output_sum, gates_sum = (turned(place, totals[i], True) for i in (0, 2))
        branch_sum, inner_sum = (
            jnp.swapaxes(
                lax.all_to_all(totals[i].reshape(n_seq, d_rows, -1), "seq", 0, 0, tiled=True), 0, 1
            ).reshape(d_rows, rec)
            for i in (1, 3)
        )
    down_sum = down_sum.reshape(-1, width // n_dp)
    grad_output, grad_branch, gates_sum, grad_inner, grad_down, grad_gate, grad_up = (
        a.astype(F32) for a in (output_sum, branch_sum, gates_sum, inner_sum, down_sum, gate_sum, up_sum)
    )
    grad_rate = gates_sum[:, :BLOCK]
    grad_entry = gates_sum[:, BLOCK : 2 * BLOCK]
    vec_sum = gates_sum[:, 2 * BLOCK :]

    return (
        result,
        grad_tokens,
        grad_branch,
        grad_inner,
        grad_output,
        grad_rate,
        grad_entry,
        vec_sum[:, WIDTH + 1],
        vec_sum[:, WIDTH + 2],
        vec_sum[:, :WIDTH].T,
        vec_sum[:, WIDTH],
        vec_sum[:, WIDTH + 3],
        gains[0],
        gains[1],
        grad_gate,
        grad_up,
        grad_down,
    )


def solution(mesh):
    rows, flat = P(BOTH, None), P(BOTH)
    in_specs = (
        rows, P("dp", None), rows, rows, rows, rows, rows, flat, flat, P(None, BOTH), flat, flat, flat, flat,
        P(None, "seq"), P(None, "seq"), P("seq", None), rows,
    )
    out_specs = (
        rows, rows, rows, rows, rows, rows, rows, flat, flat, P(None, BOTH), flat, flat, flat, flat,
        P("dp", "seq"), P("dp", "seq"), P("seq", "dp"),
    )
    return jax.shard_map(shards, mesh=mesh, in_specs=in_specs, out_specs=out_specs, check_vma=False)
```

```python
from functools import partial

import jax
import jax.numpy as jnp
from jax import lax
from jax.experimental import pallas as pl
from jax.experimental.pallas import tpu as pltpu
from jax.sharding import PartitionSpec as P

BLOCK = 256
WIDTH = 4
EPSILON = 1e-06
LANES = 128
VMEM_BYTES = 56 * 1024 * 1024
ENTRY_TILE = 256
MLP_TILE = 256
GRAD_TILE = 512
EXIT_TILE = 256
BOTH = ("dp", "seq")
F32 = jnp.float32
BF16 = jnp.bfloat16


def dot(left, right):
    return jnp.dot(left, right, preferred_element_type=F32)


def contract_rows(left, right):
    return lax.dot_general(left, right, (((0,), (0,)), ((), ())), preferred_element_type=F32)


def contract_cols(left, right):
    return lax.dot_general(left, right, (((1,), (1,)), ((), ())), preferred_element_type=F32)


class Place:
    def __init__(self):
        self.n_dp = lax.axis_size("dp")
        self.n_seq = lax.axis_size("seq")
        self.n_q = self.n_dp // 2
        self.n_x = self.n_seq // 2
        self.dp = lax.axis_index("dp")
        self.seq = lax.axis_index("seq")
        self.p = self.dp % 2
        self.q = self.dp // 2
        self.c = self.seq % 2
        self.x = self.seq // 2

    def swap_core(self, a):
        return lax.ppermute(a, "seq", [(i, i ^ 1) for i in range(self.n_seq)])

    def swap_pair(self, a):
        return lax.ppermute(a, "dp", [(i, i ^ 1) for i in range(self.n_dp)])

    def step_x(self, a, places, way):
        return lax.ppermute(
            a, "seq", [(2 * i + c, 2 * (i + way) + c) for i in places for c in range(2)]
        )

    def step_q(self, a, places, way):
        return lax.ppermute(
            a, "dp", [(2 * i + p, 2 * (i + way) + p) for i in places for p in range(2)]
        )


def add_low(*terms):
    total = terms[0].astype(F32)
    for term in terms[1:]:
        total = total + term.astype(F32)
    return total


def line_sum(block_of, count, here, step):
    if count == 1:
        return block_of(here).astype(F32)
    if count == 2:
        got = step(block_of(1 - here), [0, 1], None)
        return add_low(block_of(here), got)
    up = down = None
    for k in range(1, count):
        send_up = block_of(jnp.minimum(count - k + here, count - 1))
        if up is not None:
            send_up = add_low(send_up, up).astype(BF16)
        up = step(send_up, range(0, min(k, count - 1)), 1)
        send_down = block_of(jnp.maximum(k + here - count, 0))
        if down is not None:
            send_down = add_low(send_down, down).astype(BF16)
        down = step(send_down, range(max(count - k, 1), count), -1)
    return add_low(block_of(here), up, down)


def line_gather(block, count, here, step):
    if count == 1:
        return block[None]
    if count == 2:
        got = step(block, [0, 1], None)
        return jnp.where(here == 0, jnp.stack([block, got]), jnp.stack([got, block]))
    rows = jnp.zeros((count,) + block.shape, block.dtype)
    rows = lax.dynamic_update_index_in_dim(rows, block, here, 0)
    up = down = block
    for k in range(1, count):
        up = step(up, range(k - 1, count - 1), 1)
        down = step(down, range(1, count - k + 1), -1)
        from_up = lax.dynamic_update_index_in_dim(rows, up, jnp.maximum(here - k, 0), 0)
        rows = jnp.where(here - k >= 0, from_up, rows)
        from_down = lax.dynamic_update_index_in_dim(rows, down, jnp.minimum(here + k, count - 1), 0)
        rows = jnp.where(here + k < count, from_down, rows)
    return rows


def x_step(place):
    def step(a, places, way):
        if way is None:
            return lax.ppermute(a, "seq", [(i, i ^ 2) for i in range(place.n_seq)])
        return place.step_x(a, places, way)

    return step


def q_step(place):
    def step(a, places, way):
        if way is None:
            return lax.ppermute(a, "dp", [(i, i ^ 2) for i in range(place.n_dp)])
        return place.step_q(a, places, way)

    return step


def gather_seq(place, block):
    rows = line_gather(block, place.n_x, place.x, x_step(place))
    other = place.swap_core(rows)
    first = jnp.where(place.c == 0, rows, other)
    second = jnp.where(place.c == 0, other, rows)
    return jnp.stack([first, second], axis=1).reshape((place.n_seq,) + block.shape)


def scatter_seq(place, whole):
    view = whole.reshape((place.n_x, 2) + whole.shape[1:])
    mine = lax.dynamic_index_in_dim(view, place.c, 1, False)
    theirs = lax.dynamic_index_in_dim(view, 1 - place.c, 1, False)
    chip = add_low(mine, place.swap_core(theirs)).astype(BF16)
    return line_sum(
        lambda i: lax.dynamic_index_in_dim(chip, i, 0, False), place.n_x, place.x, x_step(place)
    )


def gather_plane(place, block):
    if place.n_x != 2:
        both = jnp.where(
            place.p == 0,
            jnp.stack([block, place.swap_pair(block)]),
            jnp.stack([place.swap_pair(block), block]),
        )
        rows = gather_seq(place, both)
        return jnp.swapaxes(rows, 0, 1)
    half = block.shape[0] // 2
    step = x_step(place)
    by_x = step(block, [0, 1], None)
    by_y = place.swap_pair(block)
    corner_low = step(by_y[:half], [0, 1], None)
    corner_high = place.swap_pair(by_x[half:])
    corner = jnp.concatenate([corner_low, corner_high], axis=0)
    mine = jnp.where(place.x == 0, jnp.stack([block, by_x]), jnp.stack([by_x, block]))
    away = jnp.where(place.x == 0, jnp.stack([by_y, corner]), jnp.stack([corner, by_y]))
    rows = jnp.where(place.p == 0, jnp.stack([mine, away]), jnp.stack([away, mine]))
    other = place.swap_core(rows)
    first = jnp.where(place.c == 0, rows, other)
    second = jnp.where(place.c == 0, other, rows)
    return jnp.stack([first, second], axis=2).reshape((2, place.n_seq) + block.shape)


def scatter_plane(place, whole):
    view = whole.reshape((2, place.n_x, 2) + whole.shape[2:])
    mine = lax.dynamic_index_in_dim(view, place.c, 2, False)
    theirs = lax.dynamic_index_in_dim(view, 1 - place.c, 2, False)
    chip = add_low(mine, place.swap_core(theirs)).astype(BF16)
    if place.n_x != 2:
        near = lax.dynamic_index_in_dim(chip, place.p, 0, False)
        far = lax.dynamic_index_in_dim(chip, 1 - place.p, 0, False)
        pair = add_low(near, place.swap_pair(far)).astype(BF16)
        return line_sum(
            lambda i: lax.dynamic_index_in_dim(pair, i, 0, False), place.n_x, place.x, x_step(place)
        )
    half = whole.shape[2] // 2
    step = x_step(place)

    def part(p, x):
        return lax.dynamic_index_in_dim(lax.dynamic_index_in_dim(chip, p, 0, False), x, 0, False)

    corner = part(1 - place.p, 1 - place.x)
    low = step(corner[:half], [0, 1], None)
    high = place.swap_pair(corner[half:])
    to_y = part(1 - place.p, place.x)
    to_x = part(place.p, 1 - place.x)
    to_y = jnp.concatenate([add_low(to_y[:half], low).astype(BF16), to_y[half:]], axis=0)
    to_x = jnp.concatenate([to_x[:half], add_low(to_x[half:], high).astype(BF16)], axis=0)
    got_y = place.swap_pair(to_y)
    got_x = step(to_x, [0, 1], None)
    return add_low(part(place.p, place.x), got_x, got_y)


def sum_dp(place, whole):
    view = whole.reshape((place.n_q, 2) + whole.shape[1:])
    mine = lax.dynamic_index_in_dim(view, place.p, 1, False)
    theirs = lax.dynamic_index_in_dim(view, 1 - place.p, 1, False)
    pair = add_low(mine, place.swap_pair(theirs)).astype(BF16)
    return line_sum(
        lambda i: lax.dynamic_index_in_dim(pair, i, 0, False), place.n_q, place.q, q_step(place)
    )


def split_pair(place, total, axis):
    half = total.shape[axis] // 2
    mine = lax.dynamic_slice_in_dim(total, place.p * half, half, axis)
    theirs = lax.dynamic_slice_in_dim(total, (1 - place.p) * half, half, axis).astype(BF16)
    got = place.swap_pair(theirs).astype(F32)
    pair = [jnp.concatenate(two, axis=1 - axis) for two in ([mine, got], [got, mine])]
    return jnp.where(place.p == 0, *pair)


def turned(place, a, back):
    route = [(s * place.n_dp + j, j * place.n_seq + s) for s in range(place.n_seq) for j in range(place.n_dp)]
    if back:
        route = [(there, here) for here, there in route]
    return lax.ppermute(a, BOTH, route)


def window(place, a, axis, own, spread):
    start = own * place.seq % BLOCK
    if own % BLOCK == 0:
        return a
    if 2 * own % BLOCK == 0 and spread == own + BLOCK // 2:
        edge = BLOCK // 2
        last = lax.slice_in_dim(a, own - edge, own, axis=axis)
        first = lax.slice_in_dim(a, 0, edge, axis=axis)
        got = place.swap_core(jnp.where(place.c == 0, last, first))
        return jnp.where(
            place.c == 0,
            jnp.concatenate([a, got], axis=axis),
            jnp.concatenate([got, a], axis=axis),
        )
    whole = lax.all_gather(a, "seq", axis=axis, tiled=True)
    begin = jnp.minimum(own * place.seq - start, whole.shape[axis] - spread)
    return lax.dynamic_slice_in_dim(whole, begin, spread, axis=axis)


def row_offsets(lengths, places):
    row_ends = jnp.cumsum(lengths)
    starts = row_ends - lengths
    row_begin = jnp.max(jnp.where(starts[None, :] <= places[:, None], starts[None, :], 0), axis=1)
    return places - row_begin


def shift_rows(a, distance, fill):
    count = a.shape[0]
    if distance > 0:
        return jnp.concatenate([jnp.full((distance, a.shape[1]), fill, a.dtype), a[: count - distance]], 0)
    return jnp.concatenate([a[-distance:], jnp.full((-distance, a.shape[1]), fill, a.dtype)], 0)


def scan_rows(decay, source, way):
    distance = 1
    while distance < decay.shape[0]:
        source = source + decay * shift_rows(source, way * distance, 0.0)
        decay = decay * shift_rows(decay, way * distance, 1.0)
        distance *= 2
    return decay, source


def gelu_parts(v):
    root = 0.7978845608028654
    cubic = 0.044715
    inner = root * (v + cubic * v * v * v)
    tanh = jnp.tanh(inner)
    value = 0.5 * v * (1.0 + tanh)
    slope = 0.5 * (1.0 + tanh) + 0.5 * v * (1.0 - tanh * tanh) * root * (1.0 + 3.0 * cubic * v * v)
    return value, slope


def softplus_row(recur):
    return jnp.maximum(-recur, 0.0) + jnp.log1p(jnp.exp(-jnp.abs(recur)))


def lru_parts(pre_rate, pre_entry, soft):
    rate = jax.nn.sigmoid(pre_rate)
    entry = jax.nn.sigmoid(pre_entry)
    power = 8.0 * soft * rate
    decay = jnp.exp(-power)
    twice = 2.0 * power
    series = twice * (
        1.0 - twice * (0.5 - twice * (1.0 / 6.0 - twice * (1.0 / 24.0 - twice * (1.0 / 120.0))))
    )
    square = jnp.where(twice < 0.25, series, 1.0 - decay * decay)
    return rate, entry, decay, square


STEP_ROWS = 64
TILE = 8


def row_steps(count):
    return count // STEP_ROWS


def step_rows(i):
    return pl.ds(pl.multiple_of(i * STEP_ROWS, STEP_ROWS), STEP_ROWS)


def tile_before(i):
    return pl.ds(pl.multiple_of(jnp.maximum(i * STEP_ROWS - TILE, 0), TILE), TILE)


def tile_after(i, count):
    return pl.ds(pl.multiple_of(jnp.minimum((i + 1) * STEP_ROWS, count - TILE), TILE), TILE)


def tile_sum(a):
    return jnp.sum(a.reshape(-1, TILE, a.shape[1]), axis=0)


def mlp_tile(x, cot, gate_weight, up_weight, down_weight):
    gate_pre = dot(x, gate_weight)
    up_pre = dot(x, up_weight)
    back_hidden = contract_cols(cot, down_weight)
    value, slope = gelu_parts(gate_pre)
    hidden = (value * up_pre).astype(BF16)
    back_gate = (back_hidden * up_pre * slope).astype(BF16)
    back_up = (back_hidden * value).astype(BF16)
    down = dot(hidden, down_weight).astype(BF16)
    back = (contract_cols(back_gate, gate_weight) + contract_cols(back_up, up_weight)).astype(BF16)
    return hidden, back_gate, back_up, down, back


def conv_kernel(inner_ref, taps_ref, offset_ref, conv_ref):
    taps = taps_ref[...]

    def step(i, carry):
        r = step_rows(i)
        near = jnp.concatenate([inner_ref[tile_before(i), :], inner_ref[r, :]], axis=0).astype(F32)
        offset = offset_ref[r, :]
        total = taps[WIDTH : WIDTH + 1, :] + taps[0:1, :] * near[TILE:]
        for k in range(1, WIDTH):
            total = total + taps[k : k + 1, :] * jnp.where(offset >= k, near[TILE - k : TILE - k + STEP_ROWS], 0.0)
        conv_ref[r, :] = total.astype(BF16)
        return carry

    lax.fori_loop(0, row_steps(inner_ref.shape[0]), step, 0, unroll=4)


def forward_kernel(rate_ref, entry_ref, conv_ref, branch_ref, vec_ref, offset_ref, states_ref, mixed_ref):
    vec = vec_ref[...]
    soft = softplus_row(vec[2:3, :])

    def step(i, carry):
        r = step_rows(i)
        _, entry, decay, square = lru_parts(rate_ref[r, :] + vec[0:1, :], entry_ref[r, :] + vec[1:2, :], soft)
        source = jnp.sqrt(square) * entry * conv_ref[r, :].astype(F32)
        decay = jnp.where(offset_ref[r, :] > 0, decay, 0.0)
        product, local = scan_rows(decay, source, 1)
        states = local + product * carry
        states_ref[r, :] = states
        mixed_ref[r, :] = (gelu_parts(branch_ref[r, :])[0] * states).astype(BF16)
        return states[STEP_ROWS - 1 :, :]

    lax.fori_loop(0, row_steps(states_ref.shape[0]), step, jnp.zeros_like(soft), unroll=4)


def backward_kernel(
    rate_ref, entry_ref, conv_ref, branch_ref, vec_ref, offset_ref, states_ref, back_ref,
    back_branch_ref, back_gates_ref, direct_ref, sums_ref,
):
    vec = vec_ref[...]
    recur = vec[2:3, :]
    soft = softplus_row(recur)
    steps = row_steps(states_ref.shape[0])

    def step(n, carry):
        later, later_decay, rate_sum, entry_sum, recur_sum = carry
        i = steps - 1 - n
        r = step_rows(i)
        rate, entry, decay, square = lru_parts(rate_ref[r, :] + vec[0:1, :], entry_ref[r, :] + vec[1:2, :], soft)
        conv = conv_ref[r, :].astype(F32)
        states = states_ref[r, :]
        back_mixed = back_ref[r, :]
        value, slope = gelu_parts(branch_ref[r, :])
        back_branch_ref[r, :] = (back_mixed * states * slope).astype(BF16)
        keep = offset_ref[r, :] > 0
        kept_decay = jnp.where(keep, decay, 0.0)
        following = jnp.concatenate([kept_decay[1:], later_decay], axis=0)
        product, local = scan_rows(following, back_mixed * value, -1)
        adjoint = local + product * later
        inverse = lax.rsqrt(square)
        root = square * inverse
        pulled = adjoint * entry * conv
        previous = jnp.concatenate([states_ref[tile_before(i), :][TILE - 1 :], states[: STEP_ROWS - 1]], axis=0)
        back_decay = adjoint * jnp.where(keep, previous, 0.0) - pulled * decay * inverse
        back_power = back_decay * decay * rate
        back_rate = back_power * (-8.0 * soft) * (1.0 - rate)
        back_entry = pulled * root * (1.0 - entry)
        back_gates_ref[0, r, :] = back_rate.astype(BF16)
        back_gates_ref[1, r, :] = back_entry.astype(BF16)
        direct_ref[r, :] = adjoint * root * entry
        return (
            adjoint[:1], kept_decay[:1], rate_sum + tile_sum(back_rate), entry_sum + tile_sum(back_entry),
            recur_sum + tile_sum(back_power),
        )

    row, tile = jnp.zeros_like(recur), jnp.zeros((TILE, recur.shape[1]), F32)
    _, _, rate_sum, entry_sum, recur_sum = lax.fori_loop(0, steps, step, (row, row, tile, tile, tile), unroll=4)
    total = lambda a: jnp.sum(a, axis=0, keepdims=True)
    sums_ref[...] = jnp.concatenate(
        [
            total(rate_sum),
            total(entry_sum),
            total(recur_sum) * (8.0 * jax.nn.sigmoid(-recur)),
            jnp.zeros((TILE - 3,) + recur.shape[1:], F32),
        ],
        axis=0,
    )


def conv_back_kernel(direct_ref, gates_ref, inner_ref, taps_ref, offset_ref, back_ref, sums_ref):
    count = direct_ref.shape[0]
    taps = taps_ref[...]
    steps = row_steps(count)

    def step(i, sums):
        r, before, after = step_rows(i), tile_before(i), tile_after(i, count)
        last = jnp.where(i + 1 < steps, 1.0, 0.0)
        here = direct_ref[r, :] + gates_ref[r, :]
        wide = jnp.concatenate([here, (direct_ref[after, :] + gates_ref[after, :]) * last], axis=0)
        offset = jnp.concatenate([offset_ref[r, :], offset_ref[after, :]], axis=0)
        inner = jnp.concatenate([inner_ref[before, :], inner_ref[r, :]], axis=0).astype(F32)
        total = taps[0:1, :] * here
        new = [sums[0] + tile_sum(here * inner[TILE:])]
        for k in range(1, WIDTH):
            masked = jnp.where(offset >= k, wide, 0.0)
            total = total + taps[k : k + 1, :] * masked[k : k + STEP_ROWS]
            new.append(sums[k] + tile_sum(masked[:STEP_ROWS] * inner[TILE - k : TILE - k + STEP_ROWS]))
        new.append(sums[WIDTH] + tile_sum(here))
        back_ref[r, :] = total.astype(BF16)
        return tuple(new)

    tile = jnp.zeros((TILE, taps.shape[1]), F32)
    sums = lax.fori_loop(0, steps, step, (tile,) * (WIDTH + 1), unroll=4)
    rows = [jnp.sum(a, axis=0, keepdims=True) for a in sums]
    sums_ref[...] = jnp.concatenate(rows + [jnp.zeros((TILE - len(rows), taps.shape[1]), F32)], axis=0)


def forward_gates_kernel(
    first_ref, block_ref, w_rate_ref, w_entry_ref, conv_ref, branch_ref, vec_ref, offset_ref, states_ref, mixed_ref,
    rate_ref, entry_ref,
):
    rate_ref[...] = dot(block_ref[...], w_rate_ref[...])
    entry_ref[...] = dot(block_ref[...], w_entry_ref[...])
    forward_kernel(rate_ref, entry_ref, conv_ref, branch_ref, vec_ref, offset_ref, states_ref, mixed_ref)


def backward_gates_kernel(
    first_ref, block_ref, w_rate_ref, w_entry_ref, conv_ref, branch_ref, vec_ref, offset_ref, states_ref, back_ref,
    back_branch_ref, back_gates_ref, direct_ref, sums_ref, rate_ref, entry_ref,
):
    rate_ref[...] = dot(block_ref[...], w_rate_ref[...])
    entry_ref[...] = dot(block_ref[...], w_entry_ref[...])
    backward_kernel(
        rate_ref, entry_ref, conv_ref, branch_ref, vec_ref, offset_ref, states_ref, back_ref,
        back_branch_ref, back_gates_ref, direct_ref, sums_ref,
    )


def conv_wide_kernel(first_ref, inner_ref, taps_ref, offset_ref, conv_ref):
    conv_kernel(inner_ref, taps_ref, offset_ref, conv_ref)


def conv_back_gates_kernel(
    first_ref, gates_ref, w_rate_ref, w_entry_ref, direct_ref, inner_ref, taps_ref, offset_ref, back_ref, sums_ref,
    total_ref,
):
    total_ref[...] = contract_cols(gates_ref[0], w_rate_ref[...]) + contract_cols(gates_ref[1], w_entry_ref[...])
    conv_back_kernel(direct_ref, total_ref, inner_ref, taps_ref, offset_ref, back_ref, sums_ref)


def by_block(kernel, first, ins, outs, scratch, own):
    def spec(how, shape):
        rows = shape[-2]
        half = BLOCK // LANES
        return {
            "own": pl.BlockSpec((rows, LANES), lambda j, f: (0, j)),
            "wide": pl.BlockSpec((rows, LANES), lambda j, f: (0, f[0] + j)),
            "block": pl.BlockSpec((rows, BLOCK), lambda j, f: (0, (f[0] + j) // half)),
            "wide2": pl.BlockSpec((2, rows, LANES), lambda j, f: (0, 0, f[0] + j)),
            "block2": pl.BlockSpec((2, rows, BLOCK), lambda j, f: (0, 0, (f[0] + j) // half)),
            "columns": pl.BlockSpec((BLOCK, LANES), lambda j, f: ((f[0] + j) // half, (f[0] + j) % half)),
            "rows": pl.BlockSpec((LANES, BLOCK), lambda j, f: (f[0] + j, 0)),
            "one": pl.BlockSpec((rows, 1), lambda j, f: (0, 0)),
        }[how]

    count = ins[0][1].shape[-2]
    return pl.pallas_call(
        kernel,
        grid_spec=pltpu.PrefetchScalarGridSpec(
            num_scalar_prefetch=1,
            grid=(own // LANES,),
            in_specs=[spec(how, a.shape) for how, a in ins],
            out_specs=[spec(how, shape) for how, shape, _ in outs],
            scratch_shapes=[pltpu.VMEM((count, LANES), F32)] * scratch,
        ),
        out_shape=[jax.ShapeDtypeStruct(shape, kind) for _, shape, kind in outs],
        compiler_params=pltpu.CompilerParams(vmem_limit_bytes=VMEM_BYTES),
        cost_estimate=pl.CostEstimate(
            flops=60 * count * own,
            bytes_accessed=sum(a.size * a.dtype.itemsize for _, a in ins) * 2,
            transcendentals=4 * count * own,
        ),
    )(first, *(a for _, a in ins))


def fill_edge(place, wide, own):
    edge = wide.shape[-1] - own
    from_lane = jnp.where(place.c == 0, own - edge, edge)
    to_lane = jnp.where(place.c == 0, own, 0)
    got = place.swap_core(lax.dynamic_slice_in_dim(wide, from_lane, edge, axis=wide.ndim - 1))
    return lax.dynamic_update_slice_in_dim(wide, got, to_lane, axis=wide.ndim - 1)


def by_channel(kernel, ins, outs, width, cost=40):
    padded = -(-width // LANES) * LANES

    def widened(a):
        return a if a.shape[1] in (1, padded) else jnp.pad(a, ((0, 0), (0, padded - width)))

    ins = [widened(a) for a in ins]
    specs = [
        pl.BlockSpec((a.shape[0], 1), lambda i: (0, 0))
        if a.shape[1] == 1
        else pl.BlockSpec((a.shape[0], LANES), lambda i: (0, i))
        for a in ins
    ]
    results = pl.pallas_call(
        kernel,
        grid=(padded // LANES,),
        in_specs=specs,
        out_specs=[
            pl.BlockSpec(rows + (LANES,), lambda i, rows=rows: (0,) * len(rows) + (i,)) for rows, _ in outs
        ],
        out_shape=[jax.ShapeDtypeStruct(rows + (padded,), kind) for rows, kind in outs],
        compiler_params=pltpu.CompilerParams(vmem_limit_bytes=VMEM_BYTES),
        cost_estimate=pl.CostEstimate(
            flops=cost * outs[0][0][0] * padded,
            bytes_accessed=sum(a.size * a.dtype.itemsize for a in ins) * 2,
            transcendentals=4 * outs[0][0][0] * padded,
        ),
    )(*ins)
    return [a[..., :width] for a in results]


def rms_norm(values, gain):
    return values * lax.rsqrt(jnp.mean(values * values, axis=-1, keepdims=True) + EPSILON) * gain


def rms_back(values, gain, back):
    scale = lax.rsqrt(jnp.mean(values * values, axis=-1, keepdims=True) + EPSILON)
    unit = values * scale
    grad_gain = jnp.sum(back * unit, axis=0)
    lifted = back * gain
    return scale * (lifted - unit * jnp.mean(lifted * unit, axis=-1, keepdims=True)), grad_gain


class Near:
    def __init__(self):
        self.n_dp, self.n_seq = lax.axis_size("dp"), lax.axis_size("seq")
        self.n_q = self.n_dp // 2
        self.dp, self.seq = lax.axis_index("dp"), lax.axis_index("seq")
        self.p, self.q = self.dp % 2, self.dp // 2
        self.c, self.x = self.seq % 2, self.seq // 2
        self.core = {"dp": self.dp, "seq": self.seq + 1 - 2 * self.c}
        self.over_x = {"dp": self.dp, "seq": self.seq + 2 - 4 * self.x}
        self.over_y = {"dp": self.dp + 1 - 2 * self.p, "seq": self.seq}

    def z(self, way):
        return {"dp": self.dp + 2 * way, "seq": self.seq}


def signal(device):
    pl.semaphore_signal(
        pltpu.get_barrier_semaphore(), inc=1, device_id=device, device_id_type=pl.DeviceIdType.MESH
    )


def remote(source, target, sems, index, device):
    return pltpu.make_async_remote_copy(
        src_ref=source,
        dst_ref=target,
        send_sem=sems[0].at[index],
        recv_sem=sems[1].at[index],
        device_id=device,
        device_id_type=pl.DeviceIdType.MESH,
    )


def gather_kernel(in_pack, out_pack, tok, cot, in_all, out_all, group_x, cot_c, cot_o, send, recv, local):
    near = Near()
    n_q, n_seq, n_dp = near.n_q, near.n_seq, near.n_dp
    dp, seq, p, q = near.dp, near.seq, near.p, near.q
    sems = (send, recv)
    place = dp * n_seq + seq
    to_dp, to_seq = place % n_dp, place // n_dp
    origin = seq * n_dp + dp
    turned_to = {"dp": to_dp, "seq": to_seq}
    turned_from = {"dp": origin // n_seq, "seq": origin % n_seq}
    moves = jnp.logical_or(to_dp != dp, to_seq != seq)
    above, below = q + 1 < n_q, q >= 1

    A2A, TURN, TOK, COT, TOKC, COTC, YB, YIN = 0, 3, 4, 5, 6, 8, 10, 11
    YOUT = YIN + n_q
    ZIN, ZOUT, ZB = YOUT + n_q, YOUT + n_q + n_q, YOUT + 3 * n_q
    SEND_DOWN = ZB + 2 * n_q

    for d in range(1, n_seq):
        signal({"dp": dp, "seq": (seq + d) % n_seq})
    signal(near.over_y)
    pl.when(above)(lambda: signal(near.z(1)))
    pl.when(below)(lambda: signal(near.z(-1)))
    pl.when(moves)(lambda: signal(turned_from))
    pl.semaphore_wait(
        pltpu.get_barrier_semaphore(),
        n_seq + above.astype(jnp.int32) + below.astype(jnp.int32) + moves.astype(jnp.int32),
    )

    sent = []

    def go(copy):
        copy.start()
        sent.append(copy)
        return copy

    for d in range(1, n_seq):
        peer = (seq + d) % n_seq
        go(remote(in_pack.at[peer], in_all.at[dp, seq], sems, A2A + d - 1, {"dp": dp, "seq": peer}))
    turn = remote(out_pack, out_all.at[to_dp], sems, TURN, turned_to)
    keep = [
        pltpu.make_async_copy(in_pack.at[seq], in_all.at[dp, seq], local.at[0]),
        pltpu.make_async_copy(tok, group_x.at[seq], local.at[1]),
        pltpu.make_async_copy(cot, cot_c.at[0], local.at[2]),
    ]
    stay = pltpu.make_async_copy(out_pack, out_all.at[dp], local.at[3])
    pl.when(moves)(turn.start)
    pl.when(jnp.logical_not(moves))(stay.start)
    for copy in keep:
        copy.start()
    go(remote(tok, group_x.at[seq], sems, TOK, near.over_x))
    go(remote(cot, cot_c.at[1], sems, COT, near.over_x))
    go(remote(tok, group_x.at[seq], sems, TOKC, near.core))
    go(remote(cot, cot_o.at[0], sems, COTC, near.core))

    def lines(block):
        d = 2 * block + p
        return [(ZIN + block, in_all.at[d, pl.ds(0, n_seq - 1)]), (ZOUT + block, out_all.at[d])]

    def corners(block):
        return [(ZB + 2 * block + i, in_all.at[2 * block + i, n_seq - 1]) for i in range(2)]

    def z_copy(number, ref, way):
        index = number if way > 0 else number + (SEND_DOWN - ZIN)
        return pltpu.make_async_remote_copy(
            src_ref=ref, dst_ref=ref, send_sem=send.at[index], recv_sem=recv.at[number],
            device_id=near.z(way), device_id_type=pl.DeviceIdType.MESH,
        )

    def y_copies(block):
        d = 2 * block + p
        return [
            remote(in_all.at[d, pl.ds(0, n_seq - 1)], in_all.at[d, pl.ds(0, n_seq - 1)], sems, YIN + block, near.over_y),
            remote(out_all.at[d], out_all.at[d], sems, YOUT + block, near.over_y),
        ]

    def y_arrivals(block):
        d = 2 * block + 1 - p
        return [
            remote(in_all.at[d, pl.ds(0, n_seq - 1)], in_all.at[d, pl.ds(0, n_seq - 1)], sems, YIN + block, near.over_y),
            remote(out_all.at[d], out_all.at[d], sems, YOUT + block, near.over_y),
        ]

    for d in range(1, n_seq):
        source = (seq + n_seq - d) % n_seq
        remote(in_pack.at[0], in_all.at[dp, source], sems, A2A + d - 1, {"dp": dp, "seq": source}).wait_recv()
    keep[0].wait()
    y_first = remote(in_all.at[dp, n_seq - 1], in_all.at[dp, n_seq - 1], sems, YB, near.over_y)
    go(y_first)

    def both_ways(pairs):
        for number, ref in pairs:
            pl.when(above)(lambda number=number, ref=ref: z_copy(number, ref, 1).start())
            pl.when(below)(lambda number=number, ref=ref: z_copy(number, ref, -1).start())

    own, own_y = lines(q), y_copies(q)
    both_ways(own[:1])
    go(own_y[0])
    pl.when(moves)(lambda: remote(out_pack, out_all.at[dp], sems, TURN, turned_to).wait_recv())
    pl.when(jnp.logical_not(moves))(stay.wait)
    both_ways(own[1:])
    go(own_y[1])
    other = 2 * q + 1 - p
    remote(in_all.at[other, n_seq - 1], in_all.at[other, n_seq - 1], sems, YB, near.over_y).wait_recv()
    both_ways(corners(q))

    for k in range(1, n_q):
        for way in (1, -1):
            block = q - way * k
            there = block >= 0 if way > 0 else block < n_q
            on = above if way > 0 else below

            def arrived(block=block, way=way, on=on):
                for (number, ref), y_copy in zip(lines(block), y_copies(block)):
                    z_copy(number, ref, way).wait_recv()
                    pl.when(on)(lambda number=number, ref=ref: z_copy(number, ref, way).start())
                    y_copy.start()
                for number, ref in corners(block):
                    z_copy(number, ref, way).wait_recv()
                    pl.when(on)(lambda number=number, ref=ref: z_copy(number, ref, way).start())

            pl.when(there)(arrived)
        if k == 1:
            other_x = seq + 2 - 4 * near.x
            remote(tok, group_x.at[other_x], sems, TOK, near.over_x).wait_recv()
            go(remote(group_x.at[other_x], group_x.at[other_x], sems, TOKC + 1, near.core))
            remote(cot, cot_c.at[1], sems, COT, near.over_x).wait_recv()
            go(remote(cot_c.at[1], cot_o.at[1], sems, COTC + 1, near.core))

    for block in range(n_q):
        for copy in y_arrivals(block):
            copy.wait_recv()
    for number, place_at in ((0, seq + 1 - 2 * near.c), (1, seq + 1 - 2 * near.c + 2 - 4 * near.x)):
        remote(tok, group_x.at[place_at], sems, TOKC + number, near.core).wait_recv()
        remote(cot, cot_o.at[number], sems, COTC + number, near.core).wait_recv()

    for copy in sent:
        copy.wait_send()
    pl.when(moves)(turn.wait_send)
    keep[1].wait()
    keep[2].wait()
    for k in range(n_q):
        for way in (1, -1):
            block = q - way * k
            there = block >= 0 if way > 0 else block < n_q
            on = above if way > 0 else below

            def gone(block=block, way=way, on=on, k=k):
                for number, ref in lines(block) + corners(block):
                    pl.when(on)(lambda number=number, ref=ref: z_copy(number, ref, way).wait_send())
                if k > 0:
                    for copy in y_copies(block):
                        copy.wait_send()

            pl.when(there)(gone)


def gather_all(place, in_pack, out_pack, tok, cot):
    n_dp, n_seq, n_q = place.n_dp, place.n_seq, place.n_q
    kept = [pl.BlockSpec(memory_space=pl.ANY)] * 5
    total = 11 + 6 * n_q + 4 * n_q
    return pl.pallas_call(
        gather_kernel,
        in_specs=[pl.BlockSpec(memory_space=pltpu.VMEM)] * 4,
        out_specs=kept,
        out_shape=[
            jax.ShapeDtypeStruct((n_dp,) + in_pack.shape, BF16),
            jax.ShapeDtypeStruct((n_dp,) + out_pack.shape, BF16),
            jax.ShapeDtypeStruct((n_seq,) + tok.shape, BF16),
            jax.ShapeDtypeStruct((2,) + cot.shape, BF16),
            jax.ShapeDtypeStruct((2,) + cot.shape, BF16),
        ],
        scratch_shapes=[
            pltpu.SemaphoreType.DMA((total,)),
            pltpu.SemaphoreType.DMA((total,)),
            pltpu.SemaphoreType.DMA((4,)),
        ],
        compiler_params=pltpu.CompilerParams(
            collective_id=0, has_side_effects=True, vmem_limit_bytes=VMEM_BYTES
        ),
        name="gather_all",
    )(in_pack, out_pack, tok, cot)


CHUNKS = 4


class Chunks:
    def __init__(self, sems, rows):
        self.sems, self.size, self.sent = sems, rows // CHUNKS, []

    def rows(self, i):
        return pl.ds(i * self.size, self.size)

    def copy(self, group, i, source, target, device):
        return remote(source, target, self.sems, CHUNKS * group + i, device)

    def go(self, group, i, source, target, device):
        copy = self.copy(group, i, source, target, device)
        copy.start()
        self.sent.append(copy)

    def arrived(self, group, i, target, device):
        self.copy(group, i, target, target, device).wait_recv()

    def finish(self):
        for copy in self.sent:
            copy.wait_send()


def greet(devices):
    for device in devices:
        signal(device)
    pl.semaphore_wait(pltpu.get_barrier_semaphore(), len(devices))


def middle_kernel(
    mixed, w_out, tok, gain, cot_c, cot_o, away, gate_weight, up_weight, down_weight,
    middle, rows, pair_cot, hidden, back_gate, back_up, down_part, back_part,
    part, from_core, to_x, from_x, rows_here, cots_here, w_gate, w_up, w_down, units, wides,
    send, recv, cot_send, cot_recv, load_sem, keep_sem, out_sem,
):
    near = Near()
    p, x, c, seq = near.p, near.x, near.c, near.seq
    ch = Chunks((send, recv), tok.shape[0])
    all_chunks = range(CHUNKS)
    seq_x, seq_c = seq + 2 - 4 * x, seq + 1 - 2 * c
    seq_cx = seq_c + 2 - 4 * x
    count = units.shape[-1]
    half = pl.ds(pl.multiple_of(p * count, count), count)
    loads = [
        pltpu.make_async_copy(source, target, load_sem.at[n])
        for n, (source, target) in enumerate(
            (
                (cot_c, cots_here.at[pl.ds(0, 2)]),
                (cot_o, cots_here.at[pl.ds(2, 2)]),
                (away, cots_here.at[pl.ds(4, 2)]),
                (gate_weight.at[:, half], w_gate),
                (up_weight.at[:, half], w_up),
                (down_weight.at[half], w_down),
            )
        )
    ]
    for load in loads:
        load.start()
    greet([near.core, near.over_x, near.over_y])
    CORE_FAR, CORE_NEAR, SUM_X, OWN_X, OWN_Y, OWN_C, FWD_X, FWD_Y, FWD_C = 0, 1, 2, 3, 4, 5, 6, 7, 8
    FWD_C2, FWD_C3 = 9, 10
    OWN, X, C, CX, Y, XY, CY, CXY = range(8)

    for group, slot, at in ((CORE_FAR, 0, seq_cx), (CORE_NEAR, 1, seq_c)):
        part[at, :, :] = dot(mixed[at], w_out[...]).astype(BF16)
        for i in all_chunks:
            r = ch.rows(i)
            ch.go(group, i, part.at[at, r], from_core.at[slot, r], near.core)
        own = seq_x if slot == 0 else seq
        part[own, :, :] = dot(mixed[own], w_out[...]).astype(BF16)
    for i in all_chunks:
        r = ch.rows(i)
        ch.arrived(CORE_FAR, i, from_core.at[0, r], near.core)
        to_x[r, :] = (part[seq_x, r, :].astype(F32) + from_core[0, r, :].astype(F32)).astype(BF16)
        ch.go(SUM_X, i, to_x.at[r], from_x.at[r], near.over_x)
    for load in loads:
        load.wait()
    far_cot = remote(cots_here.at[pl.ds(Y, 2)], cots_here.at[pl.ds(CY, 2)], (cot_send, cot_recv), 0, near.core)
    far_cot.start()
    for i in all_chunks:
        r = ch.rows(i)
        ch.arrived(CORE_NEAR, i, from_core.at[1, r], near.core)
        ch.arrived(SUM_X, i, from_x.at[r], near.over_x)
        total = tok[r, :].astype(F32) + (
            part[seq, r, :].astype(F32) + from_core[1, r, :].astype(F32) + from_x[r, :].astype(F32)
        )
        middle[r, :] = total
        scale = lax.rsqrt(jnp.mean(total * total, axis=-1, keepdims=True) + EPSILON)
        rows_here[OWN, r, :] = (total * scale * gain[...]).astype(BF16)
        own = rows_here.at[OWN, r]
        ch.go(OWN_X, i, own, rows_here.at[X, r], near.over_x)
        ch.go(OWN_Y, i, own, rows_here.at[Y, r], near.over_y)
        ch.go(OWN_C, i, own, rows_here.at[C, r], near.core)
    keeps = []

    def keep(*slots):
        for slot in slots:
            copy = pltpu.make_async_copy(rows_here.at[slot], rows.at[slot], keep_sem.at[slot])
            copy.start()
            keeps.append(copy)

    def stored(n, slot):
        whole = [(units.at[n, i], ref.at[slot]) for i, ref in enumerate((hidden, back_gate, back_up))]
        whole += [(wides.at[n, i], ref.at[slot]) for i, ref in enumerate((down_part, back_part))]
        return [pltpu.make_async_copy(here, there, out_sem.at[n, i]) for i, (here, there) in enumerate(whole)]

    def products(first, second, before):
        def one(n, carry):
            slot = first + (second - first) * n
            if before is not None:
                for copy in stored(n, before[0] + (before[1] - before[0]) * n):
                    copy.wait()
            results = mlp_tile(rows_here[slot], cots_here[slot], w_gate[...], w_up[...], w_down[...])
            for i in range(3):
                units[n, i, :, :] = results[i]
            for i in range(2):
                wides[n, i, :, :] = results[3 + i]
            for copy in stored(n, slot):
                copy.start()
            return carry

        lax.fori_loop(0, 2, one, 0)

    def core_arrived(group, slot):
        for i in all_chunks:
            ch.arrived(group, i, rows_here.at[slot, ch.rows(i)], near.core)

    core_arrived(OWN_C, C)
    keep(OWN, C)
    products(OWN, C, None)
    for i in all_chunks:
        r = ch.rows(i)
        here = rows_here.at[X, r]
        ch.arrived(OWN_X, i, here, near.over_x)
        if i >= CHUNKS // 2:
            ch.go(FWD_Y, i, here, rows_here.at[XY, r], near.over_y)
        ch.go(FWD_C, i, here, rows_here.at[CX, r], near.core)
        here = rows_here.at[Y, r]
        ch.arrived(OWN_Y, i, here, near.over_y)
        if i < CHUNKS // 2:
            ch.go(FWD_X, i, here, rows_here.at[XY, r], near.over_x)
        ch.go(FWD_C2, i, here, rows_here.at[CY, r], near.core)
    keep(X, Y)
    products(X, Y, (OWN, C))
    for i in all_chunks:
        r = ch.rows(i)
        here = rows_here.at[XY, r]
        if i < CHUNKS // 2:
            ch.arrived(FWD_X, i, here, near.over_x)
        else:
            ch.arrived(FWD_Y, i, here, near.over_y)
        ch.go(FWD_C3, i, here, rows_here.at[CXY, r], near.core)
    core_arrived(FWD_C, CX)
    core_arrived(FWD_C2, CY)
    far_cot.wait()
    cots = pltpu.make_async_copy(cots_here, pair_cot, load_sem.at[0])
    cots.start()
    keep(CX, CY, XY)
    products(CX, CY, (X, Y))
    core_arrived(FWD_C3, CXY)
    keep(CXY)
    products(XY, CXY, (CX, CY))
    for n, slot in enumerate((XY, CXY)):
        for copy in stored(n, slot):
            copy.wait()
    for copy in keeps + [cots]:
        copy.wait()
    ch.finish()


def sum_middle(place, mixed, w_out, tok, gain, cot_c, cot_o, away, gate_weight, up_weight, down_weight):
    count, width = tok.shape
    units = gate_weight.shape[1] // 2
    vmem, kept = pl.BlockSpec(memory_space=pltpu.VMEM), pl.BlockSpec(memory_space=pl.ANY)
    wide, narrow = (jax.ShapeDtypeStruct((8, count, cols), BF16) for cols in (width, units))
    return pl.pallas_call(
        middle_kernel,
        in_specs=[vmem] * 4 + [kept] * 6,
        out_specs=[vmem] + [kept] * 7,
        out_shape=[jax.ShapeDtypeStruct((count, width), F32), wide, wide, narrow, narrow, narrow, wide, wide],
        scratch_shapes=[
            pltpu.VMEM((place.n_seq, count, width), BF16),
            pltpu.VMEM((2, count, width), BF16),
            pltpu.VMEM((count, width), BF16),
            pltpu.VMEM((count, width), BF16),
            pltpu.VMEM((8, count, width), BF16),
            pltpu.VMEM((8, count, width), BF16),
            pltpu.VMEM((width, units), BF16),
            pltpu.VMEM((width, units), BF16),
            pltpu.VMEM((units, width), BF16),
            pltpu.VMEM((2, 3, count, units), BF16),
            pltpu.VMEM((2, 2, count, width), BF16),
            pltpu.SemaphoreType.DMA((11 * CHUNKS,)),
            pltpu.SemaphoreType.DMA((11 * CHUNKS,)),
            pltpu.SemaphoreType.DMA((1,)),
            pltpu.SemaphoreType.DMA((1,)),
            pltpu.SemaphoreType.DMA((6,)),
            pltpu.SemaphoreType.DMA((8,)),
            pltpu.SemaphoreType.DMA((2, 5)),
        ],
        compiler_params=pltpu.CompilerParams(
            collective_id=1, has_side_effects=True, vmem_limit_bytes=VMEM_BYTES
        ),
        name="sum_middle",
    )(mixed.reshape(place.n_seq, count, -1), w_out, tok, gain, cot_c, cot_o, away, gate_weight, up_weight, down_weight)


class Piece:
    def __init__(self, kind, refs, start, rows):
        self.kind = kind
        self.part, self.total, self.up, self.down, self.low = refs[:5]
        self.over, self.pair = refs[5:] if len(refs) > 5 else (None, self.part)
        self.start, self.count = start, rows
        self.rows = pl.ds(start, rows)
        self.width = self.low.shape[1]

    def at(self, ref, block):
        return ref.at[block, self.rows]

    def read(self, ref, block):
        return ref[block, self.rows, :]

    def columns(self, block, width):
        return pl.ds(block * width if isinstance(block, int) else pl.multiple_of(block * width, width), width)

    def pair_at(self, block):
        if self.kind == "columns":
            return self.pair.at[self.rows, self.columns(block, self.width)]
        return self.pair.at[block, self.rows]

    def pair_value(self, block):
        if self.kind == "columns":
            return self.pair[self.rows, self.columns(block, self.width)]
        return self.pair[block, self.rows, :]

    def side(self, way):
        return self.up if way > 0 else self.down


class LineSums:
    def __init__(self, near, pieces, sems, local):
        self.near, self.pieces, self.sems, self.local = near, pieces, sems, local
        n_q, n_seq, n_dp = near.n_q, near.n_seq, near.n_dp
        self.ends = n_q + 2 * (n_q - 1)
        self.per = self.ends + n_seq
        owner = near.seq * n_dp + near.dp
        self.to_dp, self.to_seq = owner // n_seq, owner % n_seq
        self.moves = jnp.logical_or(self.to_dp != near.dp, self.to_seq != near.seq)
        self.above, self.below = near.q + 1 < n_q, near.q >= 1

    def y_copy(self, n, block):
        piece, near = self.pieces[n], self.near
        source = piece.at(piece.part, 2 * block + 1 - near.p)
        return remote(source, piece.at(piece.over, block), self.sems, n * self.per + block, near.over_y)

    def z_copy(self, n, k, way, arrival=False):
        piece, n_q = self.pieces[n], self.near.n_q
        side = piece.side(way)
        target = piece.at(side, k - 1)
        if arrival:
            source = target
        elif k == 1:
            source = piece.pair_at(n_q - 1 if way > 0 else 0)
        else:
            source = piece.at(side, k - 2)
        number = n * self.per + n_q + (k - 1) * 2 + (way < 0)
        return remote(source, target, self.sems, number, self.near.z(way))

    def sends(self, k, way):
        q, n_q = self.near.q, self.near.n_q
        if way > 0:
            return jnp.logical_and(q <= k - 1, self.above)
        return jnp.logical_and(q >= n_q - k, self.below)

    def gets(self, k, way):
        q, n_q = self.near.q, self.near.n_q
        if way > 0:
            return jnp.logical_and(q <= k, self.below)
        return jnp.logical_and(q + 1 >= n_q - k, self.above)

    def y_start(self, *numbers):
        for n in numbers:
            for block in range(self.near.n_q):
                self.y_copy(n, block).start()

    def pair_up(self, n):
        piece = self.pieces[n]
        for block in range(self.near.n_q):
            self.y_copy(n, block).wait_recv()
            total = piece.read(piece.part, 2 * block + self.near.p) + piece.read(piece.over, block)
            piece.pair[block, piece.rows, :] = total

    def z_step(self, n, k):
        piece, q, n_q = self.pieces[n], self.near.q, self.near.n_q
        for way in (1, -1):

            def stage(way=way):
                side = piece.side(way)
                if k > 1:
                    block = n_q - k + q if way > 0 else k + q - n_q
                    came = self.gets(k - 1, way)

                    def add():
                        self.z_copy(n, k - 1, way, True).wait_recv()
                        total = piece.read(side, k - 2) + piece.pair_value(block)
                        side[k - 2, piece.rows, :] = total

                    def begin():
                        side[k - 2, piece.rows, :] = piece.pair_value(block)

                    pl.when(came)(add)
                    pl.when(jnp.logical_not(came))(begin)
                self.z_copy(n, k, way).start()

            pl.when(self.sends(k, way))(stage)

    def owners(self, n):
        piece, near = self.pieces[n], self.near
        if piece.kind == "turn":
            return [(None, self.moves)]
        if piece.kind == "rows":
            other = piece.start // (piece.low.shape[0] // 2)
            return [(other, near.p != other)]
        if piece.kind == "columns":
            return [(near.p, None), (1 - near.p, True)]
        each = piece.low.shape[0] // near.n_seq
        first = piece.start // each
        return [(j, near.seq != j) for j in range(first, first + piece.count // each)]

    def end_refs(self, n, j, source=None):
        piece, near = self.pieces[n], self.near
        if piece.kind == "turn":
            return piece.low.at[piece.rows], piece.total.at[piece.rows]
        if piece.kind == "rows":
            to = pl.ds(piece.start % (piece.low.shape[0] // 2), piece.count)
            p = near.p if source is None else source
            return piece.low.at[piece.rows], piece.total.at[to, piece.columns(p, piece.width)]
        if piece.kind == "columns":
            p = near.p if source is None else source
            return piece.low.at[piece.rows, piece.columns(j, piece.width // 2)], piece.total.at[p, piece.rows]
        each = piece.low.shape[0] // near.n_seq
        seq = near.seq if source is None else source
        return piece.low.at[pl.ds(j * each, each)], piece.total.at[:, piece.columns(seq, piece.width)]

    def end_copy(self, n, j, source=None):
        piece, near = self.pieces[n], self.near
        here, target = self.end_refs(n, j, source)
        first = n * self.per + self.ends
        if piece.kind == "turn":
            return remote(here, target, self.sems, first, {"dp": self.to_dp, "seq": self.to_seq})
        if piece.kind in ("rows", "columns"):
            return remote(target if source is not None else here, target, self.sems, first, near.over_y)
        if source is not None:
            return remote(target, target, self.sems, first + source, {"dp": near.dp, "seq": j})
        return pltpu.make_async_remote_copy(
            src_ref=here, dst_ref=target, send_sem=self.sems[0].at[first + j],
            recv_sem=self.sems[1].at[first + near.seq],
            device_id={"dp": near.dp, "seq": j}, device_id_type=pl.DeviceIdType.MESH,
        )

    def stay_copy(self, n, j):
        here, target = self.end_refs(n, j)
        return pltpu.make_async_copy(here, target, self.local.at[n])

    def finish(self, n):
        piece, k = self.pieces[n], self.near.n_q - 1
        piece.low[piece.rows, :] = piece.pair_value(self.near.q)

        def add(way):
            self.z_copy(n, k, way, True).wait_recv()
            piece.low[piece.rows, :] = piece.low[piece.rows, :] + piece.read(piece.side(way), k - 1)

        pl.when(self.below)(lambda: add(1))
        pl.when(self.above)(lambda: add(-1))
        for j, away in self.owners(n):
            if piece.kind == "columns":
                (self.end_copy if away else self.stay_copy)(n, j).start()
                continue
            pl.when(away)(lambda j=j: self.end_copy(n, j).start())
            pl.when(jnp.logical_not(away))(lambda j=j: self.stay_copy(n, j).start())

    def z_steps(self, numbers, k):
        for n in numbers:
            self.z_step(n, k)

    def finish_all(self, numbers):
        for n in numbers:
            self.finish(n)

    def arrive(self, n, j):
        piece, near = self.pieces[n], self.near
        self.stay_copy(n, j).wait()
        if piece.kind in ("rows", "columns"):
            self.end_copy(n, j, 1 - near.p).wait_recv()
            return
        for source in range(near.n_seq):
            if source != j:
                self.end_copy(n, j, source).wait_recv()

    def close(self):
        for n, piece in enumerate(self.pieces):
            for j, away in self.owners(n):
                if piece.kind == "turn":
                    pl.when(away)(lambda n=n, j=j: self.end_copy(n, j).wait())
                    pl.when(jnp.logical_not(away))(lambda n=n, j=j: self.stay_copy(n, j).wait())
                elif piece.kind == "columns":
                    self.end_copy(n, j).wait_send() if away else self.arrive(n, j)
                else:
                    pl.when(away)(lambda n=n, j=j: self.end_copy(n, j).wait_send())
                    pl.when(jnp.logical_not(away))(lambda n=n, j=j: self.arrive(n, j))
            if piece.over is not None:
                for block in range(self.near.n_q):
                    self.y_copy(n, block).wait_send()
            for k in range(1, self.near.n_q):
                for way in (1, -1):
                    pl.when(self.sends(k, way))(lambda n=n, k=k, way=way: self.z_copy(n, k, way).wait_send())


def line_scratch(place, parts, cuts):
    n_q, n_seq = place.n_q, place.n_seq
    outs, scratch, pieces = [], [], 0
    for part, (kind, cut) in zip(parts, cuts):
        rows, cols = part.shape[-2:]
        if kind == "columns":
            cols = cols // n_q
        shape = {
            "seq": (rows // n_seq, n_seq * cols),
            "turn": (rows, cols),
            "rows": (rows // 2, 2 * cols),
            "columns": (2, rows, cols // 2),
        }[kind]
        outs.append(jax.ShapeDtypeStruct(shape, BF16))
        sizes = [(n_q - 1, rows, cols)] * 2 + [(rows, cols)]
        if kind in ("seq", "turn"):
            sizes += [(n_q, rows, cols)] * 2
        scratch += [pltpu.VMEM(size, BF16) for size in sizes]
        pieces += cut
    total = pieces * (n_q + 2 * (n_q - 1) + n_seq)
    sems = [
        pltpu.SemaphoreType.DMA((total,)),
        pltpu.SemaphoreType.DMA((total,)),
        pltpu.SemaphoreType.DMA((pieces,)),
    ]
    return outs, scratch + sems


def line_pieces(cuts, parts, totals, scratch):
    pieces, scratch = [], list(scratch)
    for (kind, cut), part, total in zip(cuts, parts, totals):
        take = 5 if kind in ("seq", "turn") else 3
        refs = [part, total] + scratch[:take]
        scratch = scratch[take:]
        rows = part.shape[-2] // cut
        pieces += [Piece(kind, refs, i * rows, rows) for i in range(cut)]
    return pieces


def greet_lines(near, others=()):
    above, below = near.q + 1 < near.n_q, near.q >= 1
    for device in others:
        signal(device)
    pl.when(above)(lambda: signal(near.z(1)))
    pl.when(below)(lambda: signal(near.z(-1)))
    return len(others) + above.astype(jnp.int32) + below.astype(jnp.int32)


def weight_sums_kernel(cuts, *refs):
    count = len(cuts)
    near = Near()
    x, c, seq, p, q, n_q = near.x, near.c, near.seq, near.p, near.q, near.n_q
    part, tok, back, gain, mid_grad = refs[:5]
    parts = refs[5 : 5 + count]
    grad_tok, gains = refs[5 + count : 7 + count]
    totals = refs[7 + count : 7 + 2 * count]
    own, from_core, from_x, gain_near, gain_line, send, recv, local, load, gain_send, gain_recv = refs[
        7 + 2 * count : 18 + 2 * count
    ]
    line_refs = refs[18 + 2 * count :]
    lines = LineSums(near, line_pieces(cuts, parts, totals, line_refs[:-3]), line_refs[-3:-1], line_refs[-1])
    ch = Chunks((send, recv), tok.shape[0])
    seq_x, seq_c = seq + 2 - 4 * x, seq + 1 - 2 * c
    seq_cx = seq_c + 2 - 4 * x
    loads = [
        pltpu.make_async_copy(part.at[at], own.at[i], load.at[i]) for i, at in enumerate((seq_x, seq))
    ]
    for copy in loads:
        copy.start()
    origin = near.dp * near.n_seq + seq
    others = [{"dp": near.dp, "seq": (seq + d) % near.n_seq} for d in range(1, near.n_seq)]
    others += [near.over_y]
    along = [{"dp": 2 * ((q + d) % n_q) + p, "seq": seq} for d in range(1, n_q)]
    for device in others + along:
        signal(device)
    pl.when(lines.moves)(lambda: signal({"dp": origin % near.n_dp, "seq": origin // near.n_dp}))
    pl.semaphore_wait(
        pltpu.get_barrier_semaphore(), len(others + along) + lines.moves.astype(jnp.int32)
    )
    CORE_FAR, CORE_NEAR, SUM_X = range(3)
    for group, at, slot in ((CORE_FAR, seq_cx, 0), (CORE_NEAR, seq_c, 1)):
        for i in range(CHUNKS):
            r = ch.rows(i)
            ch.go(group, i, part.at[at, r], from_core.at[slot, r], near.core)
    ready = [n for n, piece in enumerate(lines.pieces) if piece.over is None]
    waiting = [n for n, piece in enumerate(lines.pieces) if piece.over is not None]
    ahead = 2
    lines.y_start(*waiting[:ahead])
    lines.z_steps(ready, 1)
    for copy in loads:
        copy.wait()
    for i in range(CHUNKS):
        r = ch.rows(i)
        ch.arrived(CORE_FAR, i, from_core.at[0, r], near.core)
        from_core[0, r, :] = (own[0, r, :].astype(F32) + from_core[0, r, :].astype(F32)).astype(BF16)
        ch.go(SUM_X, i, from_core.at[0, r], from_x.at[r], near.over_x)
    lines.z_steps(ready, 2)
    gain_sum = jnp.zeros_like(gain)
    for i in range(CHUNKS):
        r = ch.rows(i)
        ch.arrived(CORE_NEAR, i, from_core.at[1, r], near.core)
        ch.arrived(SUM_X, i, from_x.at[r], near.over_x)
        total = own[1, r, :].astype(F32) + from_core[1, r, :].astype(F32) + from_x[r, :].astype(F32)
        value = tok[r, :].astype(F32)
        scale = lax.rsqrt(jnp.mean(value * value, axis=-1, keepdims=True) + EPSILON)
        unit = value * scale
        gain_sum = gain_sum + jnp.sum(total * unit, axis=0, keepdims=True)
        lifted = total * gain[...]
        grad_tok[r, :] = back[r, :] + scale * (
            lifted - unit * jnp.mean(lifted * unit, axis=-1, keepdims=True)
        )

    gain_near[0, :, :] = jnp.concatenate(
        [gain_sum, mid_grad[...], jnp.zeros((TILE - 2, gain.shape[1]), F32)], axis=0
    )
    pairs = [
        remote(gain_near.at[2 * i], gain_near.at[2 * i + 1], (gain_send, gain_recv), i, device)
        for i, device in enumerate((near.core, near.over_x, near.over_y))
    ]
    copies = [
        remote(gain_near.at[6], gain_line.at[i], (gain_send, gain_recv), 3 + i, device) for i, device in enumerate(along)
    ]

    def gain_step(i):
        if 0 < i <= 3:
            pairs[i - 1].wait()
            gain_near[2 * i, :, :] = gain_near[2 * i - 2, :, :] + gain_near[2 * i - 1, :, :]
        for copy in pairs[i : i + 1] if i < 3 else copies if i == 3 else []:
            copy.start()

    gain_step(0)
    for k in range(3, n_q):
        lines.z_steps(ready, k)
    gain_step(1)
    for t in range(len(waiting) + n_q):
        if t < len(waiting):
            lines.pair_up(waiting[t])
            lines.y_start(*waiting[t + ahead : t + ahead + 1])
        for k in range(1, n_q):
            if 0 <= t - (k - 1) < len(waiting):
                lines.z_step(waiting[t - (k - 1)], k)
        if 0 <= t - (n_q - 1) < len(waiting):
            lines.finish(waiting[t - (n_q - 1)])
        if t == 0:
            gain_step(2)
            lines.finish_all(ready)
        if t == 2:
            gain_step(3)
    total = gain_near[6, :, :]
    for i, copy in enumerate(copies):
        copy.wait()
        total = total + gain_line[i, :, :]
    gains[...] = total
    ch.finish()
    lines.close()


def weight_sums(place, part, tok, back, gain, mid_grad, parts, cuts):
    rows, width = tok.shape
    vmem, kept = pl.BlockSpec(memory_space=pltpu.VMEM), pl.BlockSpec(memory_space=pl.ANY)
    outs, scratch = line_scratch(place, parts, cuts)
    n_q = place.n_q
    return pl.pallas_call(
        partial(weight_sums_kernel, cuts),
        in_specs=[kept] + [vmem] * (4 + len(parts)),
        out_specs=[vmem, vmem] + [kept] * len(parts),
        out_shape=[jax.ShapeDtypeStruct((rows, width), F32), jax.ShapeDtypeStruct((TILE, width), F32)] + outs,
        scratch_shapes=[
            pltpu.VMEM((2, rows, width), BF16),
            pltpu.VMEM((2, rows, width), BF16),
            pltpu.VMEM((rows, width), BF16),
            pltpu.VMEM((7, TILE, width), F32),
            pltpu.VMEM((n_q - 1, TILE, width), F32),
            pltpu.SemaphoreType.DMA((3 * CHUNKS,)),
            pltpu.SemaphoreType.DMA((3 * CHUNKS,)),
            pltpu.SemaphoreType.DMA((1,)),
            pltpu.SemaphoreType.DMA((2,)),
            pltpu.SemaphoreType.DMA((2 + n_q,)),
            pltpu.SemaphoreType.DMA((2 + n_q,)),
        ]
        + scratch,
        compiler_params=pltpu.CompilerParams(
            collective_id=3, has_side_effects=True, vmem_limit_bytes=VMEM_BYTES
        ),
        name="weight_sums",
    )(part, tok, back, gain, mid_grad, *parts)


class PlaneSum:
    FAR, TO_X, TO_Y, NEAR = range(4)
    AT = {0: (1, 1), 1: (0, 1), 2: (1, 0), 3: (0, 0)}

    def __init__(self, near, ch, groups, part, local, own, from_core, corner_x, corner_y, got_x, got_y):
        self.near, self.ch, self.part, self.own, self.from_core = near, ch, part, own, from_core
        self.corner_x, self.corner_y, self.got_x, self.got_y = corner_x, corner_y, got_x, got_y
        self.core_group = groups
        self.cx, self.cy, self.gx, self.gy = range(groups + 4, groups + 8)
        half = CHUNKS // 2
        self.half, self.first, self.last = half, range(half), range(half, CHUNKS)
        self.loads = [pltpu.make_async_copy(part.at[i, 0], own.at[i], local.at[i]) for i in range(2)]
        for load in self.loads:
            load.start()

    def to_core(self, group, chunks):
        other_p, other_x = self.AT[group]
        for i in chunks:
            r = self.ch.rows(i)
            self.ch.go(
                self.core_group + group, i, self.part.at[other_p, 1, other_x, r], self.from_core.at[group, r], self.near.core
            )

    def on_chip(self, group, i):
        r = self.ch.rows(i)
        other_p, other_x = self.AT[group]
        self.ch.arrived(self.core_group + group, i, self.from_core.at[group, r], self.near.core)
        return self.own[other_p, other_x, r, :].astype(F32) + self.from_core[group, r, :].astype(F32)

    def start(self):
        for load in self.loads:
            load.wait()
        self.to_core(self.FAR, (0, self.half, 1, self.half + 1))
        self.to_core(self.TO_X, self.first)
        self.to_core(self.TO_Y, self.last)
        self.to_core(self.TO_X, self.last)
        self.to_core(self.TO_Y, self.first)
        self.to_core(self.NEAR, range(CHUNKS))

    def corners(self):
        near, ch = self.near, self.ch
        for i in (0, self.half, 1, self.half + 1):
            r = ch.rows(i)
            self.from_core[self.FAR, r, :] = self.on_chip(self.FAR, i).astype(BF16)
            if i < self.half:
                ch.go(self.cx, i, self.from_core.at[self.FAR, r], self.corner_x.at[r], near.over_x)
            else:
                b = ch.rows(i - self.half)
                ch.go(self.cy, i - self.half, self.from_core.at[self.FAR, r], self.corner_y.at[b], near.over_y)

    def straight(self):
        for i, j in zip(self.first, self.last):
            self.along(self.TO_X, i, self.on_chip(self.TO_X, i))
            self.along(self.TO_Y, j, self.on_chip(self.TO_Y, j))

    def along(self, group, i, total):
        r = self.ch.rows(i)
        self.from_core[group, r, :] = total.astype(BF16)
        if group == self.TO_X:
            self.ch.go(self.gx, i, self.from_core.at[group, r], self.got_x.at[r], self.near.over_x)
        else:
            self.ch.go(self.gy, i, self.from_core.at[group, r], self.got_y.at[r], self.near.over_y)

    def turned(self):
        ch = self.ch
        for i, j in zip(self.first, self.last):
            b = ch.rows(j - self.half)
            ch.arrived(self.cy, j - self.half, self.corner_y.at[b], self.near.over_y)
            self.along(self.TO_X, j, self.on_chip(self.TO_X, j) + self.corner_y[b, :].astype(F32))
            r = ch.rows(i)
            ch.arrived(self.cx, i, self.corner_x.at[r], self.near.over_x)
            self.along(self.TO_Y, i, self.on_chip(self.TO_Y, i) + self.corner_x[r, :].astype(F32))

    def total(self, i):
        r = self.ch.rows(i)
        total = self.on_chip(self.NEAR, i)
        self.ch.arrived(self.gx, i, self.got_x.at[r], self.near.over_x)
        self.ch.arrived(self.gy, i, self.got_y.at[r], self.near.over_y)
        return total + self.got_x[r, :].astype(F32) + self.got_y[r, :].astype(F32)

    @staticmethod
    def scratch(count, width):
        block = pltpu.VMEM((count, width), BF16)
        half = pltpu.VMEM((count // 2, width), BF16)
        return [
            pltpu.VMEM((2, 2, count, width), BF16), pltpu.VMEM((4, count, width), BF16), half, half, block, block
        ]


def back_middle_kernel(cuts, *refs):
    count = len(cuts)
    part, down_part, middle, cot, gain = refs[:5]
    grads = refs[5 : 5 + count]
    back, rows, gain_grad, result = refs[5 + count : 9 + count]
    totals = refs[9 + count : 9 + 2 * count]
    rest = refs[9 + 2 * count :]
    plane_a, plane_b, low = rest[:6], rest[6:12], rest[12]
    send, recv, local, loads_a, loads_b = rest[13:18]
    line_refs = rest[18:]
    near = Near()
    x, c, seq = near.x, near.c, near.seq
    ch = Chunks((send, recv), cot.shape[0])
    seq_x, seq_c = seq + 2 - 4 * x, seq + 1 - 2 * c
    seq_cx = seq_c + 2 - 4 * x
    lines = LineSums(near, line_pieces(cuts, grads, totals, line_refs[:-3]), line_refs[-3:-1], line_refs[-1])
    main = PlaneSum(near, ch, 0, part, loads_a, *plane_a)
    side = PlaneSum(near, ch, 8, down_part, loads_b, *plane_b)
    expected = greet_lines(near, [near.core, near.over_x, near.over_y])
    pl.semaphore_wait(pltpu.get_barrier_semaphore(), expected)
    OWN_X, OWN_C, FWD_C = 16, 17, 18
    half = len(lines.pieces) // 2
    early, late = range(half), range(half, 2 * half)
    steps = range(1, near.n_q)
    schedule = [partial(lines.z_steps, group, k) for k in steps for group in (early, late)]
    schedule += [partial(lines.finish_all, early), partial(lines.finish_all, late)]
    schedule = iter(schedule)

    def along_z():
        work = next(schedule, None)
        if work is not None:
            work()

    main.start()
    along_z()
    along_z()
    main.corners()
    along_z()
    main.straight()
    main.turned()
    side.start()
    along_z()
    gain_sum = jnp.zeros_like(gain)
    kept = []
    for i in range(CHUNKS):
        r = ch.rows(i)
        total = main.total(i)
        value = middle[r, :]
        scale = lax.rsqrt(jnp.mean(value * value, axis=-1, keepdims=True) + EPSILON)
        unit = value * scale
        gain_sum = gain_sum + jnp.sum(total * unit, axis=0, keepdims=True)
        lifted = total * gain[...]
        whole = cot[r, :].astype(F32) + scale * (lifted - unit * jnp.mean(lifted * unit, axis=-1, keepdims=True))
        back[r, :] = whole
        low[r, :] = whole.astype(BF16)
        ch.go(OWN_X, i, low.at[r], rows.at[seq, r], near.over_x)
        ch.go(OWN_C, i, low.at[r], rows.at[seq, r], near.core)
        keep = pltpu.make_async_copy(low.at[r], rows.at[seq, r], local.at[i])
        keep.start()
        kept.append(keep)
    gain_grad[...] = gain_sum
    side.corners()
    along_z()
    side.straight()
    along_z()
    for i in range(CHUNKS):
        here = rows.at[seq_x, ch.rows(i)]
        ch.arrived(OWN_X, i, here, near.over_x)
        ch.go(FWD_C, i, here, here, near.core)
    side.turned()
    along_z()
    for i in range(CHUNKS):
        r = ch.rows(i)
        result[r, :] = (middle[r, :] + side.total(i)).astype(BF16)
    for _ in range(2 * near.n_q):
        along_z()
    for i in range(CHUNKS):
        ch.arrived(OWN_C, i, rows.at[seq_c, ch.rows(i)], near.core)
        ch.arrived(FWD_C, i, rows.at[seq_cx, ch.rows(i)], near.core)
    for keep in kept:
        keep.wait()
    ch.finish()
    lines.close()


def sum_back_middle(place, part, down_part, middle, cot, gain, grads):
    count, width = cot.shape
    cuts = (("columns", 4), ("rows", 4))
    vmem, kept = pl.BlockSpec(memory_space=pltpu.VMEM), pl.BlockSpec(memory_space=pl.ANY)
    outs, scratch = line_scratch(place, grads, cuts)
    return pl.pallas_call(
        partial(back_middle_kernel, cuts),
        in_specs=[kept, kept] + [vmem] * (3 + len(grads)),
        out_specs=[vmem, kept, vmem, vmem] + [kept] * len(grads),
        out_shape=[
            jax.ShapeDtypeStruct((count, width), F32),
            jax.ShapeDtypeStruct((place.n_seq, count, width), BF16),
            jax.ShapeDtypeStruct((1, width), F32),
            jax.ShapeDtypeStruct((count, width), BF16),
        ]
        + outs,
        scratch_shapes=PlaneSum.scratch(count, width)
        + PlaneSum.scratch(count, width)
        + [
            pltpu.VMEM((count, width), BF16),
            pltpu.SemaphoreType.DMA((19 * CHUNKS,)),
            pltpu.SemaphoreType.DMA((19 * CHUNKS,)),
            pltpu.SemaphoreType.DMA((CHUNKS,)),
            pltpu.SemaphoreType.DMA((2,)),
            pltpu.SemaphoreType.DMA((2,)),
        ]
        + scratch,
        compiler_params=pltpu.CompilerParams(
            collective_id=2, has_side_effects=True, vmem_limit_bytes=VMEM_BYTES
        ),
        name="sum_back_middle",
    )(part, down_part, middle, cot, gain, *grads)


def entry_kernel(x_ref, w_ref, normed_ref, branch_ref, inner_ref, gains_ref):
    own = branch_ref.shape[1]

    @pl.when(pl.program_id(0) == 0)
    def _():
        gains_ref[...] = w_ref[:, 2 * own :].astype(F32).T[:TILE, :]

    value = x_ref[...].astype(F32)
    scale = lax.rsqrt(jnp.mean(value * value, axis=-1, keepdims=True) + EPSILON)
    normed = (value * scale * gains_ref[0:1, :]).astype(BF16)
    normed_ref[...] = normed
    inner_ref[...] = dot(normed, w_ref[:, own : 2 * own]).astype(BF16)
    branch_ref[...] = dot(normed, w_ref[:, :own])


def entry_products(x, weights, own, tile):
    rows, width = x.shape
    whole = lambda shape: pl.BlockSpec(shape, lambda i: (0, 0), pipeline_mode=pl.Buffered(1))
    by_tile = lambda cols: pl.BlockSpec((tile, cols), lambda i: (i, 0))
    return pl.pallas_call(
        entry_kernel,
        grid=(rows // tile,),
        in_specs=[by_tile(width), whole(weights.shape)],
        out_specs=[by_tile(width), by_tile(own), by_tile(own), pl.BlockSpec((TILE, width), lambda i: (0, 0))],
        out_shape=[
            jax.ShapeDtypeStruct((rows, width), BF16),
            jax.ShapeDtypeStruct((rows, own), F32),
            jax.ShapeDtypeStruct((rows, own), BF16),
            jax.ShapeDtypeStruct((TILE, width), F32),
        ],
        compiler_params=pltpu.CompilerParams(vmem_limit_bytes=VMEM_BYTES),
        cost_estimate=pl.CostEstimate(
            flops=4 * rows * width * own, bytes_accessed=weights.size * 2 + rows * (width * 4 + own * 6), transcendentals=rows
        ),
        name="entry_products",
    )(x, weights)


def mlp_kernel(p_ref, x_ref, cot_ref, gate_ref, up_ref, down_ref, *result_refs):
    results = mlp_tile(x_ref[...], cot_ref[...], gate_ref[...], up_ref[...], down_ref[...])
    for ref, value in zip(result_refs, results):
        ref[...] = value


def mlp_products(p, x, cot, gate_weight, up_weight, down_weight, tile):
    rows, width = x.shape
    units = gate_weight.shape[1] // 2
    by_tile = lambda cols: pl.BlockSpec((tile, cols), lambda i, p: (i, 0))
    half = lambda shape, at: pl.BlockSpec(shape, at, pipeline_mode=pl.Buffered(1))
    columns = half((width, units), lambda i, p: (0, p[0]))
    return pl.pallas_call(
        mlp_kernel,
        grid_spec=pltpu.PrefetchScalarGridSpec(
            num_scalar_prefetch=1,
            grid=(rows // tile,),
            in_specs=[
                by_tile(width), by_tile(width), columns, columns, half((units, width), lambda i, p: (p[0], 0))
            ],
            out_specs=[by_tile(units)] * 3 + [by_tile(width)] * 2,
        ),
        out_shape=[jax.ShapeDtypeStruct((rows, units), BF16)] * 3 + [jax.ShapeDtypeStruct((rows, width), BF16)] * 2,
        compiler_params=pltpu.CompilerParams(vmem_limit_bytes=VMEM_BYTES),
        cost_estimate=pl.CostEstimate(
            flops=12 * rows * width * units, bytes_accessed=rows * width * 8 + units * width * 6, transcendentals=rows * units
        ),
        name="mlp_products",
    )(p, x, cot, gate_weight, up_weight, down_weight)


def mlp_grads_kernel(x_ref, cot_ref, hidden_ref, back_gate_ref, back_up_ref, down_ref, gate_ref, up_ref):
    x = x_ref[...]
    down_ref[...] = contract_rows(hidden_ref[...], cot_ref[...]).astype(BF16)
    gate_ref[...] = contract_rows(x, back_gate_ref[...]).astype(BF16)
    up_ref[...] = contract_rows(x, back_up_ref[...]).astype(BF16)


def mlp_grads(x, cot, hidden, back_gate, back_up, tile):
    rows, width = x.shape
    units = hidden.shape[1]
    columns = pl.BlockSpec((rows, tile), lambda i: (0, i))
    whole = pl.BlockSpec((rows, units), lambda i: (0, 0), pipeline_mode=pl.Buffered(1))
    by_tile = pl.BlockSpec((tile, units), lambda i: (i, 0))
    return pl.pallas_call(
        mlp_grads_kernel,
        grid=(width // tile,),
        in_specs=[columns, columns, whole, whole, whole],
        out_specs=[pl.BlockSpec((units, tile), lambda i: (0, i)), by_tile, by_tile],
        out_shape=[jax.ShapeDtypeStruct((units, width), BF16)] + [jax.ShapeDtypeStruct((width, units), BF16)] * 2,
        compiler_params=pltpu.CompilerParams(vmem_limit_bytes=VMEM_BYTES),
        cost_estimate=pl.CostEstimate(
            flops=6 * rows * width * units, bytes_accessed=rows * width * 4 + units * (rows + width) * 6, transcendentals=0
        ),
        name="mlp_grads",
    )(x, cot, hidden, back_gate, back_up)


def exit_kernel(
    normed_ref, back_out_ref, w_ref, branch_ref, inner_ref, mixed_ref,
    grad_branch_ref, grad_inner_ref, grad_output_ref, part_ref,
):
    own = branch_ref.shape[1]
    normed = normed_ref[...]
    grad_branch_ref[...] = contract_rows(normed, branch_ref[...]).astype(BF16)
    grad_inner_ref[...] = contract_rows(normed, inner_ref[...]).astype(BF16)
    grad_output_ref[...] = contract_rows(mixed_ref[...], back_out_ref[...]).astype(BF16)
    part_ref[...] = (
        contract_cols(branch_ref[...], w_ref[:, :own]) + contract_cols(inner_ref[...], w_ref[:, own : 2 * own])
    ).astype(BF16)


def exit_products(normed, back_out, weights, back_branch, back_inner, mixed, tile):
    rows, width = normed.shape
    own = mixed.shape[1]
    columns = pl.BlockSpec((rows, tile), lambda i: (0, i))
    whole = pl.BlockSpec((rows, own), lambda i: (0, 0), pipeline_mode=pl.Buffered(1))
    by_tile = lambda cols: pl.BlockSpec((tile, cols), lambda i: (i, 0))
    return pl.pallas_call(
        exit_kernel,
        grid=(width // tile,),
        in_specs=[columns, columns, by_tile(weights.shape[1]), whole, whole, whole],
        out_specs=[by_tile(own), by_tile(own), pl.BlockSpec((own, tile), lambda i: (0, i)), columns],
        out_shape=[
            jax.ShapeDtypeStruct((width, own), BF16),
            jax.ShapeDtypeStruct((width, own), BF16),
            jax.ShapeDtypeStruct((own, width), BF16),
            jax.ShapeDtypeStruct((rows, width), BF16),
        ],
        compiler_params=pltpu.CompilerParams(vmem_limit_bytes=VMEM_BYTES),
        cost_estimate=pl.CostEstimate(
            flops=10 * rows * width * own, bytes_accessed=rows * width * 6 + own * (rows + width) * 10, transcendentals=0
        ),
        name="exit_products",
    )(normed, back_out, weights, back_branch, back_inner, mixed)


def shards(
    tokens, row_lengths, branch_weight, inner_weight, output_weight, rate_weight, entry_weight,
    rate_bias, entry_bias, conv_weight, conv_bias, recur_param, norm_gain, mlp_gain,
    gate_weight, up_weight, down_weight, cotangent,
):
    place = Place()
    n_dp, n_seq = place.n_dp, place.n_seq
    tok, width = tokens.shape
    count = tok * n_seq
    rec = branch_weight.shape[1]
    own = rec // n_seq
    blocks = max(-(-(own * (s + 1)) // BLOCK) - own * s // BLOCK for s in range(n_seq))
    spread = blocks * BLOCK
    d_rows = branch_weight.shape[0]
    r_rows = output_weight.shape[0]

    gains = jnp.stack([norm_gain, mlp_gain], axis=1)
    gains = jnp.pad(gains, ((0, 0), (0, LANES - 2)))
    cut = lambda w: w.reshape(d_rows, n_seq, own).swapaxes(0, 1)
    in_pack = jnp.concatenate(
        [cut(branch_weight), cut(inner_weight), jnp.broadcast_to(gains[None], (n_seq,) + gains.shape)], axis=2
    )
    vectors = jnp.concatenate(
        [conv_weight, jnp.stack([conv_bias, rate_bias, entry_bias, recur_param])], axis=0
    )
    vectors = jnp.pad(vectors.T, ((0, 0), (0, LANES - 2 * WIDTH)))
    out_pack = jnp.concatenate([output_weight, rate_weight, entry_weight, vectors], axis=1)
    fast = place.n_x == 2
    if fast:
        in_all, out_all, group_x, cot_c, cot_o = gather_all(place, in_pack, out_pack, tokens, cotangent)
        in_all = in_all.reshape(n_dp * n_seq * d_rows, -1)
        out_all = out_all.reshape(n_dp * r_rows, -1)
    else:
        in_pack = lax.all_to_all(in_pack, "seq", 0, 0, tiled=True).reshape(n_seq * d_rows, -1)
        out_pack = turned(place, out_pack, False)
        in_all = lax.all_gather(in_pack, "dp", axis=0, tiled=True)
        out_all = lax.all_gather(out_pack, "dp", axis=0, tiled=True)
        group_x = gather_seq(place, tokens)
        group_c = gather_seq(place, cotangent)
    w_out = out_all[:, :width]
    gate_rows = window(place, out_all[:, width : width + 2 * BLOCK], 0, own, spread)
    w_rate, w_entry = gate_rows[:, :BLOCK], gate_rows[:, BLOCK:]
    vec = out_all[:, width + 2 * BLOCK : width + 2 * BLOCK + 2 * WIDTH].astype(F32).T
    taps = jnp.pad(vec[: WIDTH + 1], ((0, 7 - WIDTH), (0, 0)))
    gate_vec = jnp.pad(vec[WIDTH + 1 :], ((0, 9 - 2 * WIDTH + WIDTH), (0, 0)))
    first = own * place.seq - jnp.minimum(own * place.seq // BLOCK * BLOCK, rec - spread)
    owned = lambda a, axis: lax.dynamic_slice_in_dim(a, first, own, axis=axis) if spread != own else a

    group_x = group_x.reshape(count, width)
    away = place.swap_pair(cot_c if fast else group_c)
    offsets = row_offsets(row_lengths[0], jnp.arange(count, dtype=jnp.int32))[:, None]

    normed, branch_pre, inner, gain_rows = entry_products(group_x, in_all, own, ENTRY_TILE)
    gain_in, gain_mid = gain_rows[0:1], gain_rows[1:2]
    heads = partial(jnp.einsum, preferred_element_type=F32)
    if fast:
        gate_first = (own * place.seq % BLOCK // LANES).astype(jnp.int32)[None]
        (conv_wide,) = by_block(
            conv_wide_kernel, gate_first, [("own", inner), ("own", taps), ("one", offsets)],
            [("wide", (count, spread), BF16)], 0, own,
        )
        conv_wide = fill_edge(place, conv_wide, own)
        gate_ins = [("block", conv_wide), ("columns", w_rate), ("columns", w_entry), ("wide", conv_wide)]
        gate_ins += [("own", branch_pre), ("own", gate_vec), ("one", offsets)]
        states, mixed = by_block(
            forward_gates_kernel, gate_first, gate_ins,
            [("own", (count, own), F32), ("own", (count, own), BF16)], 2, own,
        )
    else:
        (conv,) = by_channel(conv_kernel, [inner, taps, offsets], [((count,), BF16)], own)
        conv_wide = window(place, conv, 1, own, spread)
        conv_heads = conv_wide.reshape(count, blocks, BLOCK)
        pre_rate, pre_entry = (
            owned(heads("tbc,bcd->tbd", conv_heads, w.reshape(blocks, BLOCK, BLOCK)).reshape(count, spread), 1)
            for w in (w_rate, w_entry)
        )
        states, mixed = by_channel(
            forward_kernel,
            [pre_rate, pre_entry, conv, branch_pre, gate_vec, offsets],
            [((count,), F32), ((count,), BF16)],
            own,
        )
    mixed, away = lax.optimization_barrier((mixed, away))
    whole_x = tokens.astype(F32)
    if fast:
        middle, rows, pair_cot, hidden, back_gate, back_up, down_part, back_part = sum_middle(
            place, mixed, w_out, tokens, gain_mid, cot_c, cot_o, away, gate_weight, up_weight, down_weight
        )
    else:
        out_part = dot(mixed, w_out).astype(BF16).reshape(n_seq, tok, width)
        middle = whole_x + scatter_seq(place, out_part)
        rows = gather_plane(place, rms_norm(middle, gain_mid).astype(BF16))
        pair_cot = jnp.stack([jnp.where(place.p == 0, group_c, away), jnp.where(place.p == 0, away, group_c)])
        hidden, back_gate, back_up, down_part, back_part = mlp_products(
            place.p.astype(jnp.int32)[None], rows.reshape(2 * count, width), pair_cot.reshape(2 * count, width),
            gate_weight, up_weight, down_weight, MLP_TILE,
        )
    flat = lambda a: a.reshape(2 * count, -1)
    rows, pair_cot, hidden, back_gate, back_up = (flat(a) for a in (rows, pair_cot, hidden, back_gate, back_up))
    units = gate_weight.shape[1] // 2

    n_q = place.n_q
    grad_down_part, grad_gate_part, grad_up_part = mlp_grads(rows, pair_cot, hidden, back_gate, back_up, GRAD_TILE)
    grad_gate_part, grad_up_part = (a.reshape(n_q, -1, units) for a in (grad_gate_part, grad_up_part))
    if fast:
        plane = (2, 2, 2, tok, width)
        back_middle, back_out, grad_mlp_gain, result, down_sum, gate_sum = sum_back_middle(
            place, back_part.reshape(plane), down_part.reshape(plane), middle, cotangent, gain_mid,
            [grad_down_part, grad_gate_part],
        )
        grad_mlp_gain = grad_mlp_gain[0]
    else:
        plane = (2, n_seq, tok, width)
        result = (middle + scatter_plane(place, down_part.reshape(plane))).astype(BF16)
        back_norm, grad_mlp_gain = rms_back(middle, gain_mid, scatter_plane(place, back_part.reshape(plane)))
        back_middle = cotangent.astype(F32) + back_norm
        back_out = gather_seq(place, back_middle.astype(BF16))
        step = q_step(place)
        strip = width // n_q
        down_sum = line_sum(
            lambda i: lax.dynamic_slice_in_dim(grad_down_part, i * strip, strip, 1), n_q, place.q, step
        )
        gate_sum, up_sum = (
            line_sum(partial(lax.dynamic_index_in_dim, a, axis=0, keepdims=False), n_q, place.q, step)
            for a in (grad_gate_part, grad_up_part)
        )
        down_sum, gate_sum, up_sum = (
            split_pair(place, a, axis) for a, axis in ((down_sum, 1), (gate_sum, 0), (up_sum, 0))
        )
    back_out = back_out.reshape(count, width)

    back_mixed = contract_cols(back_out, w_out)
    if fast:
        back_branch, back_gates, direct, gate_sums = by_block(
            backward_gates_kernel, gate_first, gate_ins + [("own", states), ("own", back_mixed)],
            [("own", (count, own), BF16), ("wide2", (2, count, spread), BF16), ("own", (count, own), F32),
             ("own", (TILE, own), F32)], 2, own,
        )
        back_gates = fill_edge(place, back_gates, own)
        back_inner, conv_sums = by_block(
            conv_back_gates_kernel, gate_first,
            [("block2", back_gates), ("rows", w_rate), ("rows", w_entry), ("own", direct), ("own", inner),
             ("own", taps), ("one", offsets)],
            [("own", (count, own), BF16), ("own", (TILE, own), F32)], 1, own,
        )
    else:
        back_branch, back_gates, direct, gate_sums = by_channel(
            backward_kernel,
            [pre_rate, pre_entry, conv, branch_pre, gate_vec, offsets, states, back_mixed],
            [((count,), BF16), ((2, count), BF16), ((count,), F32), ((TILE,), F32)],
            own,
        )
        back_gates = jnp.stack([window(place, a, 1, own, spread) for a in (back_gates[0], back_gates[1])])
        gates_back = sum(
            heads("tbd,bcd->tbc", a.reshape(count, blocks, BLOCK), w.reshape(blocks, BLOCK, BLOCK)).reshape(count, spread)
            for a, w in ((back_gates[0], w_rate), (back_gates[1], w_entry))
        )
        back_inner, conv_sums = by_channel(
            conv_back_kernel,
            [direct, owned(gates_back, 1), inner, taps, offsets],
            [((count,), BF16), ((TILE,), F32)],
            own,
        )
    grad_rate_part, grad_entry_part = (
        owned(
            jnp.concatenate(
                [contract_rows(conv_wide[:, b : b + BLOCK], a[:, b : b + BLOCK]) for b in range(0, spread, BLOCK)], axis=0
            ),
            0,
        )
        for a in (back_gates[0], back_gates[1])
    )
    grad_branch_part, grad_inner_part, grad_output_part, normed_part = exit_products(
        normed, back_out, in_all, back_branch, back_inner, mixed, EXIT_TILE
    )
    normed_part = normed_part.reshape(n_seq, tok, width)

    sums = jnp.concatenate([conv_sums[: WIDTH + 1], gate_sums[:3]], axis=0).T
    sums = jnp.pad(sums, ((0, 0), (0, LANES - 2 * WIDTH))).astype(BF16)
    gate_grads = jnp.concatenate([grad_rate_part.astype(BF16), grad_entry_part.astype(BF16), sums], axis=1)
    parts = [
        a.reshape(n_dp, -1, a.shape[1]) for a in (grad_output_part, grad_branch_part, gate_grads, grad_inner_part)
    ]
    if fast:
        grad_tokens, gains, up_sum, output_sum, branch_sum, gates_sum, inner_sum = weight_sums(
            place, normed_part, tokens, back_middle, gain_in, grad_mlp_gain[None], [grad_up_part] + parts,
            (("rows", 4), ("turn", 1), ("seq", 2), ("turn", 1), ("seq", 2)),
        )
        gains = lax.dynamic_slice_in_dim(gains[:2], (place.dp * n_seq + place.seq) * d_rows, d_rows, axis=1)
    else:
        back_x, grad_norm_gain = rms_back(whole_x, gain_in, scatter_seq(place, normed_part))
        grad_tokens = back_middle + back_x
        gains = lax.psum_scatter(
            jnp.stack([grad_norm_gain, grad_mlp_gain]), BOTH, scatter_dimension=1, tiled=True
        )
        totals = [sum_dp(place, a) for a in parts]
        output_sum, gates_sum = (turned(place, totals[i], True) for i in (0, 2))
        branch_sum, inner_sum = (
            jnp.swapaxes(
                lax.all_to_all(totals[i].reshape(n_seq, d_rows, -1), "seq", 0, 0, tiled=True), 0, 1
            ).reshape(d_rows, rec)
            for i in (1, 3)
        )
    down_sum = down_sum.reshape(-1, width // n_dp)
    grad_output, grad_branch, gates_sum, grad_inner, grad_down, grad_gate, grad_up = (
        a.astype(F32) for a in (output_sum, branch_sum, gates_sum, inner_sum, down_sum, gate_sum, up_sum)
    )
    grad_rate = gates_sum[:, :BLOCK]
    grad_entry = gates_sum[:, BLOCK : 2 * BLOCK]
    vec_sum = gates_sum[:, 2 * BLOCK :]

    return (
        result,
        grad_tokens,
        grad_branch,
        grad_inner,
        grad_output,
        grad_rate,
        grad_entry,
        vec_sum[:, WIDTH + 1],
        vec_sum[:, WIDTH + 2],
        vec_sum[:, :WIDTH].T,
        vec_sum[:, WIDTH],
        vec_sum[:, WIDTH + 3],
        gains[0],
        gains[1],
        grad_gate,
        grad_up,
        grad_down,
    )


def solution(mesh):
    rows, flat = P(BOTH, None), P(BOTH)
    in_specs = (
        rows, P("dp", None), rows, rows, rows, rows, rows, flat, flat, P(None, BOTH), flat, flat, flat, flat,
        P(None, "seq"), P(None, "seq"), P("seq", None), rows,
    )
    out_specs = (
        rows, rows, rows, rows, rows, rows, rows, flat, flat, P(None, BOTH), flat, flat, flat, flat,
        P("dp", "seq"), P("dp", "seq"), P("seq", "dp"),
    )
    return jax.shard_map(shards, mesh=mesh, in_specs=in_specs, out_specs=out_specs, check_vma=False)
```

```python
from functools import partial

import jax
import jax.numpy as jnp
from jax import lax
from jax.experimental import pallas as pl
from jax.experimental.pallas import tpu as pltpu
from jax.sharding import PartitionSpec as P

BLOCK = 256
WIDTH = 4
EPSILON = 1e-06
LANES = 128
VMEM_BYTES = 60 * 1024 * 1024
MOST_VMEM_BYTES = 63 * 1024 * 1024
ENTRY_TILE = 256
MLP_TILE = 256
GRAD_TILE = 512
EXIT_TILE = 256
BOTH = ("dp", "seq")
F32 = jnp.float32
BF16 = jnp.bfloat16


def dot(left, right):
    return jnp.dot(left, right, preferred_element_type=F32)


def contract_rows(left, right):
    return lax.dot_general(left, right, (((0,), (0,)), ((), ())), preferred_element_type=F32)


def contract_cols(left, right):
    return lax.dot_general(left, right, (((1,), (1,)), ((), ())), preferred_element_type=F32)


class Place:
    def __init__(self):
        self.n_dp = lax.axis_size("dp")
        self.n_seq = lax.axis_size("seq")
        self.n_q = self.n_dp // 2
        self.n_x = self.n_seq // 2
        self.dp = lax.axis_index("dp")
        self.seq = lax.axis_index("seq")
        self.p = self.dp % 2
        self.q = self.dp // 2
        self.c = self.seq % 2
        self.x = self.seq // 2

    def swap_core(self, a):
        return lax.ppermute(a, "seq", [(i, i ^ 1) for i in range(self.n_seq)])

    def swap_pair(self, a):
        return lax.ppermute(a, "dp", [(i, i ^ 1) for i in range(self.n_dp)])

    def step_x(self, a, places, way):
        return lax.ppermute(
            a, "seq", [(2 * i + c, 2 * (i + way) + c) for i in places for c in range(2)]
        )

    def step_q(self, a, places, way):
        return lax.ppermute(
            a, "dp", [(2 * i + p, 2 * (i + way) + p) for i in places for p in range(2)]
        )


def add_low(*terms):
    total = terms[0].astype(F32)
    for term in terms[1:]:
        total = total + term.astype(F32)
    return total


def line_sum(block_of, count, here, step):
    if count == 1:
        return block_of(here).astype(F32)
    if count == 2:
        got = step(block_of(1 - here), [0, 1], None)
        return add_low(block_of(here), got)
    up = down = None
    for k in range(1, count):
        send_up = block_of(jnp.minimum(count - k + here, count - 1))
        if up is not None:
            send_up = add_low(send_up, up).astype(BF16)
        up = step(send_up, range(0, min(k, count - 1)), 1)
        send_down = block_of(jnp.maximum(k + here - count, 0))
        if down is not None:
            send_down = add_low(send_down, down).astype(BF16)
        down = step(send_down, range(max(count - k, 1), count), -1)
    return add_low(block_of(here), up, down)


def line_gather(block, count, here, step):
    if count == 1:
        return block[None]
    if count == 2:
        got = step(block, [0, 1], None)
        return jnp.where(here == 0, jnp.stack([block, got]), jnp.stack([got, block]))
    rows = jnp.zeros((count,) + block.shape, block.dtype)
    rows = lax.dynamic_update_index_in_dim(rows, block, here, 0)
    up = down = block
    for k in range(1, count):
        up = step(up, range(k - 1, count - 1), 1)
        down = step(down, range(1, count - k + 1), -1)
        from_up = lax.dynamic_update_index_in_dim(rows, up, jnp.maximum(here - k, 0), 0)
        rows = jnp.where(here - k >= 0, from_up, rows)
        from_down = lax.dynamic_update_index_in_dim(rows, down, jnp.minimum(here + k, count - 1), 0)
        rows = jnp.where(here + k < count, from_down, rows)
    return rows


def x_step(place):
    def step(a, places, way):
        if way is None:
            return lax.ppermute(a, "seq", [(i, i ^ 2) for i in range(place.n_seq)])
        return place.step_x(a, places, way)

    return step


def q_step(place):
    def step(a, places, way):
        if way is None:
            return lax.ppermute(a, "dp", [(i, i ^ 2) for i in range(place.n_dp)])
        return place.step_q(a, places, way)

    return step


def gather_seq(place, block):
    rows = line_gather(block, place.n_x, place.x, x_step(place))
    other = place.swap_core(rows)
    first = jnp.where(place.c == 0, rows, other)
    second = jnp.where(place.c == 0, other, rows)
    return jnp.stack([first, second], axis=1).reshape((place.n_seq,) + block.shape)


def scatter_seq(place, whole):
    view = whole.reshape((place.n_x, 2) + whole.shape[1:])
    mine = lax.dynamic_index_in_dim(view, place.c, 1, False)
    theirs = lax.dynamic_index_in_dim(view, 1 - place.c, 1, False)
    chip = add_low(mine, place.swap_core(theirs)).astype(BF16)
    return line_sum(
        lambda i: lax.dynamic_index_in_dim(chip, i, 0, False), place.n_x, place.x, x_step(place)
    )


def gather_plane(place, block):
    if place.n_x != 2:
        both = jnp.where(
            place.p == 0,
            jnp.stack([block, place.swap_pair(block)]),
            jnp.stack([place.swap_pair(block), block]),
        )
        rows = gather_seq(place, both)
        return jnp.swapaxes(rows, 0, 1)
    half = block.shape[0] // 2
    step = x_step(place)
    by_x = step(block, [0, 1], None)
    by_y = place.swap_pair(block)
    corner_low = step(by_y[:half], [0, 1], None)
    corner_high = place.swap_pair(by_x[half:])
    corner = jnp.concatenate([corner_low, corner_high], axis=0)
    mine = jnp.where(place.x == 0, jnp.stack([block, by_x]), jnp.stack([by_x, block]))
    away = jnp.where(place.x == 0, jnp.stack([by_y, corner]), jnp.stack([corner, by_y]))
    rows = jnp.where(place.p == 0, jnp.stack([mine, away]), jnp.stack([away, mine]))
    other = place.swap_core(rows)
    first = jnp.where(place.c == 0, rows, other)
    second = jnp.where(place.c == 0, other, rows)
    return jnp.stack([first, second], axis=2).reshape((2, place.n_seq) + block.shape)


def scatter_plane(place, whole):
    view = whole.reshape((2, place.n_x, 2) + whole.shape[2:])
    mine = lax.dynamic_index_in_dim(view, place.c, 2, False)
    theirs = lax.dynamic_index_in_dim(view, 1 - place.c, 2, False)
    chip = add_low(mine, place.swap_core(theirs)).astype(BF16)
    if place.n_x != 2:
        near = lax.dynamic_index_in_dim(chip, place.p, 0, False)
        far = lax.dynamic_index_in_dim(chip, 1 - place.p, 0, False)
        pair = add_low(near, place.swap_pair(far)).astype(BF16)
        return line_sum(
            lambda i: lax.dynamic_index_in_dim(pair, i, 0, False), place.n_x, place.x, x_step(place)
        )
    half = whole.shape[2] // 2
    step = x_step(place)

    def part(p, x):
        return lax.dynamic_index_in_dim(lax.dynamic_index_in_dim(chip, p, 0, False), x, 0, False)

    corner = part(1 - place.p, 1 - place.x)
    low = step(corner[:half], [0, 1], None)
    high = place.swap_pair(corner[half:])
    to_y = part(1 - place.p, place.x)
    to_x = part(place.p, 1 - place.x)
    to_y = jnp.concatenate([add_low(to_y[:half], low).astype(BF16), to_y[half:]], axis=0)
    to_x = jnp.concatenate([to_x[:half], add_low(to_x[half:], high).astype(BF16)], axis=0)
    got_y = place.swap_pair(to_y)
    got_x = step(to_x, [0, 1], None)
    return add_low(part(place.p, place.x), got_x, got_y)


def sum_dp(place, whole):
    view = whole.reshape((place.n_q, 2) + whole.shape[1:])
    mine = lax.dynamic_index_in_dim(view, place.p, 1, False)
    theirs = lax.dynamic_index_in_dim(view, 1 - place.p, 1, False)
    pair = add_low(mine, place.swap_pair(theirs)).astype(BF16)
    return line_sum(
        lambda i: lax.dynamic_index_in_dim(pair, i, 0, False), place.n_q, place.q, q_step(place)
    )


def split_pair(place, total, axis):
    half = total.shape[axis] // 2
    mine = lax.dynamic_slice_in_dim(total, place.p * half, half, axis)
    theirs = lax.dynamic_slice_in_dim(total, (1 - place.p) * half, half, axis).astype(BF16)
    got = place.swap_pair(theirs).astype(F32)
    pair = [jnp.concatenate(two, axis=1 - axis) for two in ([mine, got], [got, mine])]
    return jnp.where(place.p == 0, *pair)


def turned(place, a, back):
    route = [(s * place.n_dp + j, j * place.n_seq + s) for s in range(place.n_seq) for j in range(place.n_dp)]
    if back:
        route = [(there, here) for here, there in route]
    return lax.ppermute(a, BOTH, route)


def window(place, a, axis, own, spread):
    start = own * place.seq % BLOCK
    if own % BLOCK == 0:
        return a
    if 2 * own % BLOCK == 0 and spread == own + BLOCK // 2:
        edge = BLOCK // 2
        last = lax.slice_in_dim(a, own - edge, own, axis=axis)
        first = lax.slice_in_dim(a, 0, edge, axis=axis)
        got = place.swap_core(jnp.where(place.c == 0, last, first))
        return jnp.where(
            place.c == 0,
            jnp.concatenate([a, got], axis=axis),
            jnp.concatenate([got, a], axis=axis),
        )
    whole = lax.all_gather(a, "seq", axis=axis, tiled=True)
    begin = jnp.minimum(own * place.seq - start, whole.shape[axis] - spread)
    return lax.dynamic_slice_in_dim(whole, begin, spread, axis=axis)


def row_offsets(lengths, places):
    row_ends = jnp.cumsum(lengths)
    starts = row_ends - lengths
    row_begin = jnp.max(jnp.where(starts[None, :] <= places[:, None], starts[None, :], 0), axis=1)
    return places - row_begin


def shift_rows(a, distance, fill):
    count = a.shape[0]
    if distance > 0:
        return jnp.concatenate([jnp.full((distance, a.shape[1]), fill, a.dtype), a[: count - distance]], 0)
    return jnp.concatenate([a[-distance:], jnp.full((-distance, a.shape[1]), fill, a.dtype)], 0)


def scan_rows(decay, source, way):
    distance = 1
    while distance < decay.shape[0]:
        source = source + decay * shift_rows(source, way * distance, 0.0)
        decay = decay * shift_rows(decay, way * distance, 1.0)
        distance *= 2
    return decay, source


def gelu_parts(v):
    root = 0.7978845608028654
    cubic = 0.044715
    inner = root * (v + cubic * v * v * v)
    tanh = jnp.tanh(inner)
    value = 0.5 * v * (1.0 + tanh)
    slope = 0.5 * (1.0 + tanh) + 0.5 * v * (1.0 - tanh * tanh) * root * (1.0 + 3.0 * cubic * v * v)
    return value, slope


def softplus_row(recur):
    return jnp.maximum(-recur, 0.0) + jnp.log1p(jnp.exp(-jnp.abs(recur)))


def lru_parts(pre_rate, pre_entry, soft):
    rate = jax.nn.sigmoid(pre_rate)
    entry = jax.nn.sigmoid(pre_entry)
    power = 8.0 * soft * rate
    decay = jnp.exp(-power)
    twice = 2.0 * power
    series = twice * (
        1.0 - twice * (0.5 - twice * (1.0 / 6.0 - twice * (1.0 / 24.0 - twice * (1.0 / 120.0))))
    )
    square = jnp.where(twice < 0.25, series, 1.0 - decay * decay)
    return rate, entry, decay, square


STEP_ROWS = 64
TILE = 8


def row_steps(count):
    return count // STEP_ROWS


def step_rows(i):
    return pl.ds(pl.multiple_of(i * STEP_ROWS, STEP_ROWS), STEP_ROWS)


def tile_before(i):
    return pl.ds(pl.multiple_of(jnp.maximum(i * STEP_ROWS - TILE, 0), TILE), TILE)


def tile_after(i, count):
    return pl.ds(pl.multiple_of(jnp.minimum((i + 1) * STEP_ROWS, count - TILE), TILE), TILE)


def tile_sum(a):
    return jnp.sum(a.reshape(-1, TILE, a.shape[1]), axis=0)


def mlp_tile(x, cot, gate_weight, up_weight, down_weight):
    gate_pre = dot(x, gate_weight)
    up_pre = dot(x, up_weight)
    back_hidden = contract_cols(cot, down_weight)
    value, slope = gelu_parts(gate_pre)
    hidden = (value * up_pre).astype(BF16)
    back_gate = (back_hidden * up_pre * slope).astype(BF16)
    back_up = (back_hidden * value).astype(BF16)
    down = dot(hidden, down_weight).astype(BF16)
    back = (contract_cols(back_gate, gate_weight) + contract_cols(back_up, up_weight)).astype(BF16)
    return hidden, back_gate, back_up, down, back


def conv_kernel(inner_ref, taps_ref, offset_ref, conv_ref):
    taps = taps_ref[...]

    def step(i, carry):
        r = step_rows(i)
        near = jnp.concatenate([inner_ref[tile_before(i), :], inner_ref[r, :]], axis=0).astype(F32)
        offset = offset_ref[r, :]
        total = taps[WIDTH : WIDTH + 1, :] + taps[0:1, :] * near[TILE:]
        for k in range(1, WIDTH):
            total = total + taps[k : k + 1, :] * jnp.where(offset >= k, near[TILE - k : TILE - k + STEP_ROWS], 0.0)
        conv_ref[r, :] = total.astype(BF16)
        return carry

    lax.fori_loop(0, row_steps(inner_ref.shape[0]), step, 0, unroll=4)


def forward_kernel(rate_ref, entry_ref, conv_ref, branch_ref, vec_ref, offset_ref, states_ref, mixed_ref):
    vec = vec_ref[...]
    soft = softplus_row(vec[2:3, :])

    def step(i, carry):
        r = step_rows(i)
        _, entry, decay, square = lru_parts(rate_ref[r, :] + vec[0:1, :], entry_ref[r, :] + vec[1:2, :], soft)
        source = jnp.sqrt(square) * entry * conv_ref[r, :].astype(F32)
        decay = jnp.where(offset_ref[r, :] > 0, decay, 0.0)
        product, local = scan_rows(decay, source, 1)
        states = local + product * carry
        states_ref[r, :] = states
        mixed_ref[r, :] = (gelu_parts(branch_ref[r, :])[0] * states).astype(BF16)
        return states[STEP_ROWS - 1 :, :]

    lax.fori_loop(0, row_steps(states_ref.shape[0]), step, jnp.zeros_like(soft), unroll=4)


def backward_kernel(
    rate_ref, entry_ref, conv_ref, branch_ref, vec_ref, offset_ref, states_ref, back_ref,
    back_branch_ref, back_gates_ref, direct_ref, sums_ref,
):
    vec = vec_ref[...]
    recur = vec[2:3, :]
    soft = softplus_row(recur)
    steps = row_steps(states_ref.shape[0])

    def step(n, carry):
        later, later_decay, rate_sum, entry_sum, recur_sum = carry
        i = steps - 1 - n
        r = step_rows(i)
        rate, entry, decay, square = lru_parts(rate_ref[r, :] + vec[0:1, :], entry_ref[r, :] + vec[1:2, :], soft)
        conv = conv_ref[r, :].astype(F32)
        states = states_ref[r, :]
        back_mixed = back_ref[r, :]
        value, slope = gelu_parts(branch_ref[r, :])
        back_branch_ref[r, :] = (back_mixed * states * slope).astype(BF16)
        keep = offset_ref[r, :] > 0
        kept_decay = jnp.where(keep, decay, 0.0)
        following = jnp.concatenate([kept_decay[1:], later_decay], axis=0)
        product, local = scan_rows(following, back_mixed * value, -1)
        adjoint = local + product * later
        inverse = lax.rsqrt(square)
        root = square * inverse
        pulled = adjoint * entry * conv
        previous = jnp.concatenate([states_ref[tile_before(i), :][TILE - 1 :], states[: STEP_ROWS - 1]], axis=0)
        back_decay = adjoint * jnp.where(keep, previous, 0.0) - pulled * decay * inverse
        back_power = back_decay * decay * rate
        back_rate = back_power * (-8.0 * soft) * (1.0 - rate)
        back_entry = pulled * root * (1.0 - entry)
        back_gates_ref[0, r, :] = back_rate.astype(BF16)
        back_gates_ref[1, r, :] = back_entry.astype(BF16)
        direct_ref[r, :] = adjoint * root * entry
        return (
            adjoint[:1], kept_decay[:1], rate_sum + tile_sum(back_rate), entry_sum + tile_sum(back_entry),
            recur_sum + tile_sum(back_power),
        )

    row, tile = jnp.zeros_like(recur), jnp.zeros((TILE, recur.shape[1]), F32)
    _, _, rate_sum, entry_sum, recur_sum = lax.fori_loop(0, steps, step, (row, row, tile, tile, tile), unroll=4)
    total = lambda a: jnp.sum(a, axis=0, keepdims=True)
    sums_ref[...] = jnp.concatenate(
        [
            total(rate_sum),
            total(entry_sum),
            total(recur_sum) * (8.0 * jax.nn.sigmoid(-recur)),
            jnp.zeros((TILE - 3,) + recur.shape[1:], F32),
        ],
        axis=0,
    )


def conv_back_kernel(direct_ref, gates_ref, inner_ref, taps_ref, offset_ref, back_ref, sums_ref):
    count = direct_ref.shape[0]
    taps = taps_ref[...]
    steps = row_steps(count)

    def step(i, sums):
        r, before, after = step_rows(i), tile_before(i), tile_after(i, count)
        last = jnp.where(i + 1 < steps, 1.0, 0.0)
        here = direct_ref[r, :] + gates_ref[r, :]
        wide = jnp.concatenate([here, (direct_ref[after, :] + gates_ref[after, :]) * last], axis=0)
        offset = jnp.concatenate([offset_ref[r, :], offset_ref[after, :]], axis=0)
        inner = jnp.concatenate([inner_ref[before, :], inner_ref[r, :]], axis=0).astype(F32)
        total = taps[0:1, :] * here
        new = [sums[0] + tile_sum(here * inner[TILE:])]
        for k in range(1, WIDTH):
            masked = jnp.where(offset >= k, wide, 0.0)
            total = total + taps[k : k + 1, :] * masked[k : k + STEP_ROWS]
            new.append(sums[k] + tile_sum(masked[:STEP_ROWS] * inner[TILE - k : TILE - k + STEP_ROWS]))
        new.append(sums[WIDTH] + tile_sum(here))
        back_ref[r, :] = total.astype(BF16)
        return tuple(new)

    tile = jnp.zeros((TILE, taps.shape[1]), F32)
    sums = lax.fori_loop(0, steps, step, (tile,) * (WIDTH + 1), unroll=4)
    rows = [jnp.sum(a, axis=0, keepdims=True) for a in sums]
    sums_ref[...] = jnp.concatenate(rows + [jnp.zeros((TILE - len(rows), taps.shape[1]), F32)], axis=0)


def forward_gates_kernel(
    first_ref, block_ref, w_rate_ref, w_entry_ref, conv_ref, branch_ref, vec_ref, offset_ref, states_ref, mixed_ref,
    rate_ref, entry_ref,
):
    rate_ref[...] = dot(block_ref[...], w_rate_ref[...])
    entry_ref[...] = dot(block_ref[...], w_entry_ref[...])
    forward_kernel(rate_ref, entry_ref, conv_ref, branch_ref, vec_ref, offset_ref, states_ref, mixed_ref)


def backward_gates_kernel(
    first_ref, block_ref, w_rate_ref, w_entry_ref, conv_ref, branch_ref, vec_ref, offset_ref, states_ref, back_ref,
    back_branch_ref, back_gates_ref, direct_ref, sums_ref, rate_ref, entry_ref,
):
    rate_ref[...] = dot(block_ref[...], w_rate_ref[...])
    entry_ref[...] = dot(block_ref[...], w_entry_ref[...])
    backward_kernel(
        rate_ref, entry_ref, conv_ref, branch_ref, vec_ref, offset_ref, states_ref, back_ref,
        back_branch_ref, back_gates_ref, direct_ref, sums_ref,
    )


def conv_wide_kernel(first_ref, inner_ref, taps_ref, offset_ref, conv_ref):
    conv_kernel(inner_ref, taps_ref, offset_ref, conv_ref)


def conv_back_gates_kernel(
    first_ref, gates_ref, w_rate_ref, w_entry_ref, direct_ref, inner_ref, taps_ref, offset_ref, back_ref, sums_ref,
    total_ref,
):
    total_ref[...] = contract_cols(gates_ref[0], w_rate_ref[...]) + contract_cols(gates_ref[1], w_entry_ref[...])
    conv_back_kernel(direct_ref, total_ref, inner_ref, taps_ref, offset_ref, back_ref, sums_ref)


def by_block(kernel, first, ins, outs, scratch, own):
    def spec(how, shape):
        rows = shape[-2]
        half = BLOCK // LANES
        return {
            "own": pl.BlockSpec((rows, LANES), lambda j, f: (0, j)),
            "wide": pl.BlockSpec((rows, LANES), lambda j, f: (0, f[0] + j)),
            "block": pl.BlockSpec((rows, BLOCK), lambda j, f: (0, (f[0] + j) // half)),
            "wide2": pl.BlockSpec((2, rows, LANES), lambda j, f: (0, 0, f[0] + j)),
            "block2": pl.BlockSpec((2, rows, BLOCK), lambda j, f: (0, 0, (f[0] + j) // half)),
            "columns": pl.BlockSpec((BLOCK, LANES), lambda j, f: ((f[0] + j) // half, (f[0] + j) % half)),
            "rows": pl.BlockSpec((LANES, BLOCK), lambda j, f: (f[0] + j, 0)),
            "one": pl.BlockSpec((rows, 1), lambda j, f: (0, 0)),
        }[how]

    count = ins[0][1].shape[-2]
    return pl.pallas_call(
        kernel,
        grid_spec=pltpu.PrefetchScalarGridSpec(
            num_scalar_prefetch=1,
            grid=(own // LANES,),
            in_specs=[spec(how, a.shape) for how, a in ins],
            out_specs=[spec(how, shape) for how, shape, _ in outs],
            scratch_shapes=[pltpu.VMEM((count, LANES), F32)] * scratch,
        ),
        out_shape=[jax.ShapeDtypeStruct(shape, kind) for _, shape, kind in outs],
        compiler_params=pltpu.CompilerParams(vmem_limit_bytes=VMEM_BYTES),
        cost_estimate=pl.CostEstimate(
            flops=60 * count * own,
            bytes_accessed=sum(a.size * a.dtype.itemsize for _, a in ins) * 2,
            transcendentals=4 * count * own,
        ),
    )(first, *(a for _, a in ins))


def fill_edge(place, wide, own):
    edge = wide.shape[-1] - own
    from_lane = jnp.where(place.c == 0, own - edge, edge)
    to_lane = jnp.where(place.c == 0, own, 0)
    got = place.swap_core(lax.dynamic_slice_in_dim(wide, from_lane, edge, axis=wide.ndim - 1))
    return lax.dynamic_update_slice_in_dim(wide, got, to_lane, axis=wide.ndim - 1)


def by_channel(kernel, ins, outs, width, cost=40):
    padded = -(-width // LANES) * LANES

    def widened(a):
        return a if a.shape[1] in (1, padded) else jnp.pad(a, ((0, 0), (0, padded - width)))

    ins = [widened(a) for a in ins]
    specs = [
        pl.BlockSpec((a.shape[0], 1), lambda i: (0, 0))
        if a.shape[1] == 1
        else pl.BlockSpec((a.shape[0], LANES), lambda i: (0, i))
        for a in ins
    ]
    results = pl.pallas_call(
        kernel,
        grid=(padded // LANES,),
        in_specs=specs,
        out_specs=[
            pl.BlockSpec(rows + (LANES,), lambda i, rows=rows: (0,) * len(rows) + (i,)) for rows, _ in outs
        ],
        out_shape=[jax.ShapeDtypeStruct(rows + (padded,), kind) for rows, kind in outs],
        compiler_params=pltpu.CompilerParams(vmem_limit_bytes=VMEM_BYTES),
        cost_estimate=pl.CostEstimate(
            flops=cost * outs[0][0][0] * padded,
            bytes_accessed=sum(a.size * a.dtype.itemsize for a in ins) * 2,
            transcendentals=4 * outs[0][0][0] * padded,
        ),
    )(*ins)
    return [a[..., :width] for a in results]


def rms_norm(values, gain):
    return values * lax.rsqrt(jnp.mean(values * values, axis=-1, keepdims=True) + EPSILON) * gain


def rms_back(values, gain, back):
    scale = lax.rsqrt(jnp.mean(values * values, axis=-1, keepdims=True) + EPSILON)
    unit = values * scale
    grad_gain = jnp.sum(back * unit, axis=0)
    lifted = back * gain
    return scale * (lifted - unit * jnp.mean(lifted * unit, axis=-1, keepdims=True)), grad_gain


class Near:
    def __init__(self):
        self.n_dp, self.n_seq = lax.axis_size("dp"), lax.axis_size("seq")
        self.n_q = self.n_dp // 2
        self.dp, self.seq = lax.axis_index("dp"), lax.axis_index("seq")
        self.p, self.q = self.dp % 2, self.dp // 2
        self.c, self.x = self.seq % 2, self.seq // 2
        self.core = {"dp": self.dp, "seq": self.seq + 1 - 2 * self.c}
        self.over_x = {"dp": self.dp, "seq": self.seq + 2 - 4 * self.x}
        self.over_y = {"dp": self.dp + 1 - 2 * self.p, "seq": self.seq}

    def z(self, way):
        return {"dp": self.dp + 2 * way, "seq": self.seq}


def signal(device):
    pl.semaphore_signal(
        pltpu.get_barrier_semaphore(), inc=1, device_id=device, device_id_type=pl.DeviceIdType.MESH
    )


def remote(source, target, sems, index, device):
    return pltpu.make_async_remote_copy(
        src_ref=source,
        dst_ref=target,
        send_sem=sems[0].at[index],
        recv_sem=sems[1].at[index],
        device_id=device,
        device_id_type=pl.DeviceIdType.MESH,
    )


def gather_kernel(in_pack, out_pack, tok, cot, in_all, out_all, group_x, cot_c, cot_o, send, recv, local):
    near = Near()
    n_q, n_seq, n_dp = near.n_q, near.n_seq, near.n_dp
    dp, seq, p, q = near.dp, near.seq, near.p, near.q
    sems = (send, recv)
    place = dp * n_seq + seq
    to_dp, to_seq = place % n_dp, place // n_dp
    origin = seq * n_dp + dp
    turned_to = {"dp": to_dp, "seq": to_seq}
    turned_from = {"dp": origin // n_seq, "seq": origin % n_seq}
    moves = jnp.logical_or(to_dp != dp, to_seq != seq)
    above, below = q + 1 < n_q, q >= 1

    A2A, TURN, TOK, COT, TOKC, COTC, YB, YIN = 0, 3, 4, 5, 6, 8, 10, 11
    YOUT = YIN + n_q
    ZIN, ZOUT, ZB = YOUT + n_q, YOUT + n_q + n_q, YOUT + 3 * n_q
    SEND_DOWN = ZB + 2 * n_q

    for d in range(1, n_seq):
        signal({"dp": dp, "seq": (seq + d) % n_seq})
    signal(near.over_y)
    pl.when(above)(lambda: signal(near.z(1)))
    pl.when(below)(lambda: signal(near.z(-1)))
    pl.when(moves)(lambda: signal(turned_from))
    pl.semaphore_wait(
        pltpu.get_barrier_semaphore(),
        n_seq + above.astype(jnp.int32) + below.astype(jnp.int32) + moves.astype(jnp.int32),
    )

    sent = []

    def go(copy):
        copy.start()
        sent.append(copy)
        return copy

    for d in range(1, n_seq):
        peer = (seq + d) % n_seq
        go(remote(in_pack.at[peer], in_all.at[dp, seq], sems, A2A + d - 1, {"dp": dp, "seq": peer}))
    turn = remote(out_pack, out_all.at[to_dp], sems, TURN, turned_to)
    keep = [
        pltpu.make_async_copy(in_pack.at[seq], in_all.at[dp, seq], local.at[0]),
        pltpu.make_async_copy(tok, group_x.at[seq], local.at[1]),
        pltpu.make_async_copy(cot, cot_c.at[0], local.at[2]),
    ]
    stay = pltpu.make_async_copy(out_pack, out_all.at[dp], local.at[3])
    pl.when(moves)(turn.start)
    pl.when(jnp.logical_not(moves))(stay.start)
    for copy in keep:
        copy.start()
    go(remote(tok, group_x.at[seq], sems, TOK, near.over_x))
    go(remote(cot, cot_c.at[1], sems, COT, near.over_x))
    go(remote(tok, group_x.at[seq], sems, TOKC, near.core))
    go(remote(cot, cot_o.at[0], sems, COTC, near.core))

    def lines(block):
        d = 2 * block + p
        return [(ZIN + block, in_all.at[d, pl.ds(0, n_seq - 1)]), (ZOUT + block, out_all.at[d])]

    def corners(block):
        return [(ZB + 2 * block + i, in_all.at[2 * block + i, n_seq - 1]) for i in range(2)]

    def z_copy(number, ref, way):
        index = number if way > 0 else number + (SEND_DOWN - ZIN)
        return pltpu.make_async_remote_copy(
            src_ref=ref, dst_ref=ref, send_sem=send.at[index], recv_sem=recv.at[number],
            device_id=near.z(way), device_id_type=pl.DeviceIdType.MESH,
        )

    def y_copies(block):
        d = 2 * block + p
        return [
            remote(in_all.at[d, pl.ds(0, n_seq - 1)], in_all.at[d, pl.ds(0, n_seq - 1)], sems, YIN + block, near.over_y),
            remote(out_all.at[d], out_all.at[d], sems, YOUT + block, near.over_y),
        ]

    def y_arrivals(block):
        d = 2 * block + 1 - p
        return [
            remote(in_all.at[d, pl.ds(0, n_seq - 1)], in_all.at[d, pl.ds(0, n_seq - 1)], sems, YIN + block, near.over_y),
            remote(out_all.at[d], out_all.at[d], sems, YOUT + block, near.over_y),
        ]

    for d in range(1, n_seq):
        source = (seq + n_seq - d) % n_seq
        remote(in_pack.at[0], in_all.at[dp, source], sems, A2A + d - 1, {"dp": dp, "seq": source}).wait_recv()
    keep[0].wait()
    y_first = remote(in_all.at[dp, n_seq - 1], in_all.at[dp, n_seq - 1], sems, YB, near.over_y)
    go(y_first)

    def both_ways(pairs):
        for number, ref in pairs:
            pl.when(above)(lambda number=number, ref=ref: z_copy(number, ref, 1).start())
            pl.when(below)(lambda number=number, ref=ref: z_copy(number, ref, -1).start())

    own, own_y = lines(q), y_copies(q)
    both_ways(own[:1])
    go(own_y[0])
    pl.when(moves)(lambda: remote(out_pack, out_all.at[dp], sems, TURN, turned_to).wait_recv())
    pl.when(jnp.logical_not(moves))(stay.wait)
    both_ways(own[1:])
    go(own_y[1])
    other = 2 * q + 1 - p
    remote(in_all.at[other, n_seq - 1], in_all.at[other, n_seq - 1], sems, YB, near.over_y).wait_recv()
    both_ways(corners(q))

    for k in range(1, n_q):
        for way in (1, -1):
            block = q - way * k
            there = block >= 0 if way > 0 else block < n_q
            on = above if way > 0 else below

            def arrived(block=block, way=way, on=on):
                for (number, ref), y_copy in zip(lines(block), y_copies(block)):
                    z_copy(number, ref, way).wait_recv()
                    pl.when(on)(lambda number=number, ref=ref: z_copy(number, ref, way).start())
                    y_copy.start()
                for number, ref in corners(block):
                    z_copy(number, ref, way).wait_recv()
                    pl.when(on)(lambda number=number, ref=ref: z_copy(number, ref, way).start())

            pl.when(there)(arrived)
        if k == 1:
            other_x = seq + 2 - 4 * near.x
            remote(tok, group_x.at[other_x], sems, TOK, near.over_x).wait_recv()
            go(remote(group_x.at[other_x], group_x.at[other_x], sems, TOKC + 1, near.core))
            remote(cot, cot_c.at[1], sems, COT, near.over_x).wait_recv()
            go(remote(cot_c.at[1], cot_o.at[1], sems, COTC + 1, near.core))

    for block in range(n_q):
        for copy in y_arrivals(block):
            copy.wait_recv()
    for number, place_at in ((0, seq + 1 - 2 * near.c), (1, seq + 1 - 2 * near.c + 2 - 4 * near.x)):
        remote(tok, group_x.at[place_at], sems, TOKC + number, near.core).wait_recv()
        remote(cot, cot_o.at[number], sems, COTC + number, near.core).wait_recv()

    for copy in sent:
        copy.wait_send()
    pl.when(moves)(turn.wait_send)
    keep[1].wait()
    keep[2].wait()
    for k in range(n_q):
        for way in (1, -1):
            block = q - way * k
            there = block >= 0 if way > 0 else block < n_q
            on = above if way > 0 else below

            def gone(block=block, way=way, on=on, k=k):
                for number, ref in lines(block) + corners(block):
                    pl.when(on)(lambda number=number, ref=ref: z_copy(number, ref, way).wait_send())
                if k > 0:
                    for copy in y_copies(block):
                        copy.wait_send()

            pl.when(there)(gone)


def gather_all(place, in_pack, out_pack, tok, cot):
    n_dp, n_seq, n_q = place.n_dp, place.n_seq, place.n_q
    kept = [pl.BlockSpec(memory_space=pl.ANY)] * 5
    total = 11 + 6 * n_q + 4 * n_q
    return pl.pallas_call(
        gather_kernel,
        in_specs=[pl.BlockSpec(memory_space=pltpu.VMEM)] * 4,
        out_specs=kept,
        out_shape=[
            jax.ShapeDtypeStruct((n_dp,) + in_pack.shape, BF16),
            jax.ShapeDtypeStruct((n_dp,) + out_pack.shape, BF16),
            jax.ShapeDtypeStruct((n_seq,) + tok.shape, BF16),
            jax.ShapeDtypeStruct((2,) + cot.shape, BF16),
            jax.ShapeDtypeStruct((2,) + cot.shape, BF16),
        ],
        scratch_shapes=[
            pltpu.SemaphoreType.DMA((total,)),
            pltpu.SemaphoreType.DMA((total,)),
            pltpu.SemaphoreType.DMA((4,)),
        ],
        compiler_params=pltpu.CompilerParams(
            collective_id=0, has_side_effects=True, vmem_limit_bytes=VMEM_BYTES
        ),
        name="gather_all",
    )(in_pack, out_pack, tok, cot)


CHUNKS = 4


class Chunks:
    def __init__(self, sems, rows):
        self.sems, self.size, self.sent = sems, rows // CHUNKS, []

    def rows(self, i):
        return pl.ds(i * self.size, self.size)

    def copy(self, group, i, source, target, device):
        return remote(source, target, self.sems, CHUNKS * group + i, device)

    def go(self, group, i, source, target, device):
        copy = self.copy(group, i, source, target, device)
        copy.start()
        self.sent.append(copy)

    def arrived(self, group, i, target, device):
        self.copy(group, i, target, target, device).wait_recv()

    def finish(self):
        for copy in self.sent:
            copy.wait_send()


def greet(devices):
    for device in devices:
        signal(device)
    pl.semaphore_wait(pltpu.get_barrier_semaphore(), len(devices))


def middle_kernel(
    mixed, w_out, tok, gain, cot_c, cot_o, away, gate_weight, up_weight, down_weight,
    middle, rows, pair_cot, hidden, back_gate, back_up, down_part, back_part,
    part, from_core, to_x, from_x, rows_here, cots_here, w_gate, w_up, w_down, units, wides,
    send, recv, cot_send, cot_recv, load_sem, keep_sem, out_sem,
):
    near = Near()
    p, x, c, seq = near.p, near.x, near.c, near.seq
    ch = Chunks((send, recv), tok.shape[0])
    all_chunks = range(CHUNKS)
    seq_x, seq_c = seq + 2 - 4 * x, seq + 1 - 2 * c
    seq_cx = seq_c + 2 - 4 * x
    count = units.shape[-1]
    half = pl.ds(pl.multiple_of(p * count, count), count)
    loads = [
        pltpu.make_async_copy(source, target, load_sem.at[n])
        for n, (source, target) in enumerate(
            (
                (cot_c, cots_here.at[pl.ds(0, 2)]),
                (cot_o, cots_here.at[pl.ds(2, 2)]),
                (away, cots_here.at[pl.ds(4, 2)]),
                (gate_weight.at[:, half], w_gate),
                (up_weight.at[:, half], w_up),
                (down_weight.at[half], w_down),
            )
        )
    ]
    for load in loads:
        load.start()
    greet([near.core, near.over_x, near.over_y])
    CORE_FAR, CORE_NEAR, SUM_X, OWN_X, OWN_Y, OWN_C, FWD_X, FWD_Y, FWD_C = 0, 1, 2, 3, 4, 5, 6, 7, 8
    FWD_C2, FWD_C3 = 9, 10
    OWN, X, C, CX, Y, XY, CY, CXY = range(8)

    for group, slot, at in ((CORE_FAR, 0, seq_cx), (CORE_NEAR, 1, seq_c)):
        part[at, :, :] = dot(mixed[at], w_out[...]).astype(BF16)
        for i in all_chunks:
            r = ch.rows(i)
            ch.go(group, i, part.at[at, r], from_core.at[slot, r], near.core)
        own = seq_x if slot == 0 else seq
        part[own, :, :] = dot(mixed[own], w_out[...]).astype(BF16)
    for i in all_chunks:
        r = ch.rows(i)
        ch.arrived(CORE_FAR, i, from_core.at[0, r], near.core)
        to_x[r, :] = (part[seq_x, r, :].astype(F32) + from_core[0, r, :].astype(F32)).astype(BF16)
        ch.go(SUM_X, i, to_x.at[r], from_x.at[r], near.over_x)
    for load in loads:
        load.wait()
    far_cot = remote(cots_here.at[pl.ds(Y, 2)], cots_here.at[pl.ds(CY, 2)], (cot_send, cot_recv), 0, near.core)
    far_cot.start()
    for i in all_chunks:
        r = ch.rows(i)
        ch.arrived(CORE_NEAR, i, from_core.at[1, r], near.core)
        ch.arrived(SUM_X, i, from_x.at[r], near.over_x)
        total = tok[r, :].astype(F32) + (
            part[seq, r, :].astype(F32) + from_core[1, r, :].astype(F32) + from_x[r, :].astype(F32)
        )
        middle[r, :] = total
        scale = lax.rsqrt(jnp.mean(total * total, axis=-1, keepdims=True) + EPSILON)
        rows_here[OWN, r, :] = (total * scale * gain[...]).astype(BF16)
        own = rows_here.at[OWN, r]
        ch.go(OWN_X, i, own, rows_here.at[X, r], near.over_x)
        ch.go(OWN_Y, i, own, rows_here.at[Y, r], near.over_y)
        ch.go(OWN_C, i, own, rows_here.at[C, r], near.core)
    keeps = []

    def keep(*slots):
        for slot in slots:
            copy = pltpu.make_async_copy(rows_here.at[slot], rows.at[slot], keep_sem.at[slot])
            copy.start()
            keeps.append(copy)

    def stored(n, slot):
        whole = [(units.at[n, i], ref.at[slot]) for i, ref in enumerate((hidden, back_gate, back_up))]
        whole += [(wides.at[n, i], ref.at[slot]) for i, ref in enumerate((down_part, back_part))]
        return [pltpu.make_async_copy(here, there, out_sem.at[n, i]) for i, (here, there) in enumerate(whole)]

    def products(first, second, before):
        def one(n, carry):
            slot = first + (second - first) * n
            if before is not None:
                for copy in stored(n, before[0] + (before[1] - before[0]) * n):
                    copy.wait()
            results = mlp_tile(rows_here[slot], cots_here[slot], w_gate[...], w_up[...], w_down[...])
            for i in range(3):
                units[n, i, :, :] = results[i]
            for i in range(2):
                wides[n, i, :, :] = results[3 + i]
            for copy in stored(n, slot):
                copy.start()
            return carry

        lax.fori_loop(0, 2, one, 0)

    def core_arrived(group, slot):
        for i in all_chunks:
            ch.arrived(group, i, rows_here.at[slot, ch.rows(i)], near.core)

    core_arrived(OWN_C, C)
    keep(OWN, C)
    products(OWN, C, None)
    for i in all_chunks:
        r = ch.rows(i)
        here = rows_here.at[X, r]
        ch.arrived(OWN_X, i, here, near.over_x)
        if i >= CHUNKS // 2:
            ch.go(FWD_Y, i, here, rows_here.at[XY, r], near.over_y)
        ch.go(FWD_C, i, here, rows_here.at[CX, r], near.core)
        here = rows_here.at[Y, r]
        ch.arrived(OWN_Y, i, here, near.over_y)
        if i < CHUNKS // 2:
            ch.go(FWD_X, i, here, rows_here.at[XY, r], near.over_x)
        ch.go(FWD_C2, i, here, rows_here.at[CY, r], near.core)
    keep(X, Y)
    products(X, Y, (OWN, C))
    for i in all_chunks:
        r = ch.rows(i)
        here = rows_here.at[XY, r]
        if i < CHUNKS // 2:
            ch.arrived(FWD_X, i, here, near.over_x)
        else:
            ch.arrived(FWD_Y, i, here, near.over_y)
        ch.go(FWD_C3, i, here, rows_here.at[CXY, r], near.core)
    core_arrived(FWD_C, CX)
    core_arrived(FWD_C2, CY)
    far_cot.wait()
    cots = pltpu.make_async_copy(cots_here, pair_cot, load_sem.at[0])
    cots.start()
    keep(CX, CY, XY)
    products(CX, CY, (X, Y))
    core_arrived(FWD_C3, CXY)
    keep(CXY)
    products(XY, CXY, (CX, CY))
    for n, slot in enumerate((XY, CXY)):
        for copy in stored(n, slot):
            copy.wait()
    for copy in keeps + [cots]:
        copy.wait()
    ch.finish()


def sum_middle(place, mixed, w_out, tok, gain, cot_c, cot_o, away, gate_weight, up_weight, down_weight):
    count, width = tok.shape
    units = gate_weight.shape[1] // 2
    vmem, kept = pl.BlockSpec(memory_space=pltpu.VMEM), pl.BlockSpec(memory_space=pl.ANY)
    wide, narrow = (jax.ShapeDtypeStruct((8, count, cols), BF16) for cols in (width, units))
    return pl.pallas_call(
        middle_kernel,
        in_specs=[vmem] * 4 + [kept] * 6,
        out_specs=[vmem] + [kept] * 7,
        out_shape=[jax.ShapeDtypeStruct((count, width), F32), wide, wide, narrow, narrow, narrow, wide, wide],
        scratch_shapes=[
            pltpu.VMEM((place.n_seq, count, width), BF16),
            pltpu.VMEM((2, count, width), BF16),
            pltpu.VMEM((count, width), BF16),
            pltpu.VMEM((count, width), BF16),
            pltpu.VMEM((8, count, width), BF16),
            pltpu.VMEM((8, count, width), BF16),
            pltpu.VMEM((width, units), BF16),
            pltpu.VMEM((width, units), BF16),
            pltpu.VMEM((units, width), BF16),
            pltpu.VMEM((2, 3, count, units), BF16),
            pltpu.VMEM((2, 2, count, width), BF16),
            pltpu.SemaphoreType.DMA((11 * CHUNKS,)),
            pltpu.SemaphoreType.DMA((11 * CHUNKS,)),
            pltpu.SemaphoreType.DMA((1,)),
            pltpu.SemaphoreType.DMA((1,)),
            pltpu.SemaphoreType.DMA((6,)),
            pltpu.SemaphoreType.DMA((8,)),
            pltpu.SemaphoreType.DMA((2, 5)),
        ],
        compiler_params=pltpu.CompilerParams(
            collective_id=1, has_side_effects=True, vmem_limit_bytes=VMEM_BYTES
        ),
        name="sum_middle",
    )(mixed.reshape(place.n_seq, count, -1), w_out, tok, gain, cot_c, cot_o, away, gate_weight, up_weight, down_weight)


class Piece:
    def __init__(self, kind, refs, start, rows):
        self.kind = kind
        self.part, self.total, self.up, self.down, self.low = refs[:5]
        self.over = refs[5] if len(refs) > 5 else None
        self.pair = self.part if self.over is None else self.over
        self.start, self.count = start, rows
        self.rows = pl.ds(start, rows)
        self.width = self.low.shape[1]

    def at(self, ref, block):
        return ref.at[block, self.rows]

    def read(self, ref, block):
        return ref[block, self.rows, :]

    def columns(self, block, width):
        return pl.ds(block * width if isinstance(block, int) else pl.multiple_of(block * width, width), width)

    def pair_at(self, block):
        if self.kind == "columns":
            return self.pair.at[self.rows, self.columns(block, self.width)]
        return self.pair.at[block, self.rows]

    def pair_value(self, block):
        if self.kind == "columns":
            return self.pair[self.rows, self.columns(block, self.width)]
        return self.pair[block, self.rows, :]

    def side(self, way):
        return self.up if way > 0 else self.down


class LineSums:
    def __init__(self, near, pieces, sems, local):
        self.near, self.pieces, self.sems, self.local = near, pieces, sems, local
        n_q, n_seq, n_dp = near.n_q, near.n_seq, near.n_dp
        self.ends = n_q + 2 * (n_q - 1)
        self.per = self.ends + n_seq
        owner = near.seq * n_dp + near.dp
        self.to_dp, self.to_seq = owner // n_seq, owner % n_seq
        self.moves = jnp.logical_or(self.to_dp != near.dp, self.to_seq != near.seq)
        self.above, self.below = near.q + 1 < n_q, near.q >= 1

    def y_copy(self, n, block):
        piece, near = self.pieces[n], self.near
        source = piece.at(piece.part, 2 * block + 1 - near.p)
        return remote(source, piece.at(piece.over, block), self.sems, n * self.per + block, near.over_y)

    def z_copy(self, n, k, way, arrival=False):
        piece, n_q = self.pieces[n], self.near.n_q
        side = piece.side(way)
        target = piece.at(side, k - 1)
        if arrival:
            source = target
        elif k == 1:
            source = piece.pair_at(n_q - 1 if way > 0 else 0)
        else:
            source = piece.at(side, k - 2)
        number = n * self.per + n_q + (k - 1) * 2 + (way < 0)
        return remote(source, target, self.sems, number, self.near.z(way))

    def sends(self, k, way):
        q, n_q = self.near.q, self.near.n_q
        if way > 0:
            return jnp.logical_and(q <= k - 1, self.above)
        return jnp.logical_and(q >= n_q - k, self.below)

    def gets(self, k, way):
        q, n_q = self.near.q, self.near.n_q
        if way > 0:
            return jnp.logical_and(q <= k, self.below)
        return jnp.logical_and(q + 1 >= n_q - k, self.above)

    def y_start(self, *numbers):
        for n in numbers:
            for block in range(self.near.n_q):
                self.y_copy(n, block).start()

    def pair_up(self, n):
        piece = self.pieces[n]
        for block in range(self.near.n_q):
            self.y_copy(n, block).wait_recv()
            total = piece.read(piece.part, 2 * block + self.near.p) + piece.read(piece.over, block)
            piece.pair[block, piece.rows, :] = total

    def z_step(self, n, k):
        piece, q, n_q = self.pieces[n], self.near.q, self.near.n_q
        for way in (1, -1):

            def stage(way=way):
                side = piece.side(way)
                if k > 1:
                    block = n_q - k + q if way > 0 else k + q - n_q
                    came = self.gets(k - 1, way)

                    def add():
                        self.z_copy(n, k - 1, way, True).wait_recv()
                        total = piece.read(side, k - 2) + piece.pair_value(block)
                        side[k - 2, piece.rows, :] = total

                    def begin():
                        side[k - 2, piece.rows, :] = piece.pair_value(block)

                    pl.when(came)(add)
                    pl.when(jnp.logical_not(came))(begin)
                self.z_copy(n, k, way).start()

            pl.when(self.sends(k, way))(stage)

    def owners(self, n):
        piece, near = self.pieces[n], self.near
        if piece.kind == "turn":
            return [(None, self.moves)]
        if piece.kind == "rows":
            other = piece.start // (piece.low.shape[0] // 2)
            return [(other, near.p != other)]
        if piece.kind == "columns":
            return [(near.p, None), (1 - near.p, True)]
        each = piece.low.shape[0] // near.n_seq
        first = piece.start // each
        return [(j, near.seq != j) for j in range(first, first + piece.count // each)]

    def end_refs(self, n, j, source=None):
        piece, near = self.pieces[n], self.near
        if piece.kind == "turn":
            return piece.low.at[piece.rows], piece.total.at[piece.rows]
        if piece.kind == "rows":
            to = pl.ds(piece.start % (piece.low.shape[0] // 2), piece.count)
            p = near.p if source is None else source
            return piece.low.at[piece.rows], piece.total.at[to, piece.columns(p, piece.width)]
        if piece.kind == "columns":
            p = near.p if source is None else source
            return piece.low.at[piece.rows, piece.columns(j, piece.width // 2)], piece.total.at[p, piece.rows]
        each = piece.low.shape[0] // near.n_seq
        seq = near.seq if source is None else source
        return piece.low.at[pl.ds(j * each, each)], piece.total.at[:, piece.columns(seq, piece.width)]

    def end_copy(self, n, j, source=None):
        piece, near = self.pieces[n], self.near
        here, target = self.end_refs(n, j, source)
        first = n * self.per + self.ends
        if piece.kind == "turn":
            return remote(here, target, self.sems, first, {"dp": self.to_dp, "seq": self.to_seq})
        if piece.kind in ("rows", "columns"):
            return remote(target if source is not None else here, target, self.sems, first, near.over_y)
        if source is not None:
            return remote(target, target, self.sems, first + source, {"dp": near.dp, "seq": j})
        return pltpu.make_async_remote_copy(
            src_ref=here, dst_ref=target, send_sem=self.sems[0].at[first + j],
            recv_sem=self.sems[1].at[first + near.seq],
            device_id={"dp": near.dp, "seq": j}, device_id_type=pl.DeviceIdType.MESH,
        )

    def stay_copy(self, n, j):
        here, target = self.end_refs(n, j)
        return pltpu.make_async_copy(here, target, self.local.at[n])

    def finish(self, n):
        piece, k = self.pieces[n], self.near.n_q - 1
        piece.low[piece.rows, :] = piece.pair_value(self.near.q)

        def add(way):
            self.z_copy(n, k, way, True).wait_recv()
            piece.low[piece.rows, :] = piece.low[piece.rows, :] + piece.read(piece.side(way), k - 1)

        pl.when(self.below)(lambda: add(1))
        pl.when(self.above)(lambda: add(-1))
        for j, away in self.owners(n):
            if piece.kind == "columns":
                (self.end_copy if away else self.stay_copy)(n, j).start()
                continue
            pl.when(away)(lambda j=j: self.end_copy(n, j).start())
            pl.when(jnp.logical_not(away))(lambda j=j: self.stay_copy(n, j).start())

    def z_steps(self, numbers, k):
        for n in numbers:
            self.z_step(n, k)

    def finish_all(self, numbers):
        for n in numbers:
            self.finish(n)

    def arrive(self, n, j):
        piece, near = self.pieces[n], self.near
        self.stay_copy(n, j).wait()
        if piece.kind in ("rows", "columns"):
            self.end_copy(n, j, 1 - near.p).wait_recv()
            return
        for source in range(near.n_seq):
            if source != j:
                self.end_copy(n, j, source).wait_recv()

    def close(self):
        for n, piece in enumerate(self.pieces):
            for j, away in self.owners(n):
                if piece.kind == "turn":
                    pl.when(away)(lambda n=n, j=j: self.end_copy(n, j).wait())
                    pl.when(jnp.logical_not(away))(lambda n=n, j=j: self.stay_copy(n, j).wait())
                elif piece.kind == "columns":
                    self.end_copy(n, j).wait_send() if away else self.arrive(n, j)
                else:
                    pl.when(away)(lambda n=n, j=j: self.end_copy(n, j).wait_send())
                    pl.when(jnp.logical_not(away))(lambda n=n, j=j: self.arrive(n, j))
            if piece.over is not None:
                for block in range(self.near.n_q):
                    self.y_copy(n, block).wait_send()
            for k in range(1, self.near.n_q):
                for way in (1, -1):
                    pl.when(self.sends(k, way))(lambda n=n, k=k, way=way: self.z_copy(n, k, way).wait_send())


def line_scratch(place, parts, cuts):
    n_q, n_seq = place.n_q, place.n_seq
    outs, scratch, pieces = [], [], 0
    for part, (kind, cut) in zip(parts, cuts):
        rows, cols = part.shape[-2:]
        if kind == "columns":
            cols = cols // n_q
        shape = {
            "seq": (rows // n_seq, n_seq * cols),
            "turn": (rows, cols),
            "rows": (rows // 2, 2 * cols),
            "columns": (2, rows, cols // 2),
        }[kind]
        outs.append(jax.ShapeDtypeStruct(shape, BF16))
        sizes = [(n_q - 1, rows, cols)] * 2 + [(rows, cols)]
        if kind in ("seq", "turn"):
            sizes += [(n_q, rows, cols)]
        scratch += [pltpu.VMEM(size, BF16) for size in sizes]
        pieces += cut
    total = pieces * (n_q + 2 * (n_q - 1) + n_seq)
    sems = [
        pltpu.SemaphoreType.DMA((total,)),
        pltpu.SemaphoreType.DMA((total,)),
        pltpu.SemaphoreType.DMA((pieces,)),
    ]
    return outs, scratch + sems


def line_pieces(cuts, parts, totals, scratch):
    pieces, scratch = [], list(scratch)
    for (kind, cut), part, total in zip(cuts, parts, totals):
        take = 4 if kind in ("seq", "turn") else 3
        refs = [part, total] + scratch[:take]
        scratch = scratch[take:]
        rows = part.shape[-2] // cut
        pieces += [Piece(kind, refs, i * rows, rows) for i in range(cut)]
    return pieces


def greet_lines(near, others=()):
    above, below = near.q + 1 < near.n_q, near.q >= 1
    for device in others:
        signal(device)
    pl.when(above)(lambda: signal(near.z(1)))
    pl.when(below)(lambda: signal(near.z(-1)))
    return len(others) + above.astype(jnp.int32) + below.astype(jnp.int32)


def weight_sums_kernel(cuts, *refs):
    near = Near()
    x, c, seq, p, q, n_q = near.x, near.c, near.seq, near.p, near.q, near.n_q
    normed, weights, branch, inner, tok, back, gain, mid_grad, up_part, out_part, gate_part = refs[:11]
    grad_tok, gains = refs[11:13]
    totals = refs[13:18]
    branch_part, inner_part, part, from_core, from_x, gain_near, gain_line = refs[18:25]
    send, recv, gain_send, gain_recv = refs[25:29]
    line_refs = refs[29:]
    own = branch.shape[-1]
    parts = [up_part, out_part, branch_part, gate_part, inner_part]
    lines = LineSums(near, line_pieces(cuts, parts, totals, line_refs[:-3]), line_refs[-3:-1], line_refs[-1])
    ch = Chunks((send, recv), tok.shape[0])
    seq_x, seq_c = seq + 2 - 4 * x, seq + 1 - 2 * c
    seq_cx = seq_c + 2 - 4 * x
    origin = near.dp * near.n_seq + seq
    others = [{"dp": near.dp, "seq": (seq + d) % near.n_seq} for d in range(1, near.n_seq)]
    others += [near.over_y]
    along = [{"dp": 2 * ((q + d) % n_q) + p, "seq": seq} for d in range(1, n_q)]
    for device in others + along:
        signal(device)
    pl.when(lines.moves)(lambda: signal({"dp": origin % near.n_dp, "seq": origin // near.n_dp}))
    pl.semaphore_wait(
        pltpu.get_barrier_semaphore(), len(others + along) + lines.moves.astype(jnp.int32)
    )

    def enter_norm(at):
        rows = branch[at], inner[at]
        part[at, :, :] = (
            contract_cols(rows[0], weights[:, :own]) + contract_cols(rows[1], weights[:, own : 2 * own])
        ).astype(BF16)

    def weight_blocks(target, grads, places):
        height = target.shape[1]

        def one(block, carry):
            at = 2 * block + places
            columns = normed[:, pl.ds(pl.multiple_of(at * height, height), height)]
            target[at, :, :] = contract_rows(columns, grads[...].reshape(-1, own)).astype(BF16)
            return carry

        lax.fori_loop(0, n_q, one, 0)

    numbers = [[n for n, piece in enumerate(lines.pieces) if piece.part is ref] for ref in parts]
    ready, out_n, branch_n, gate_n, inner_n = numbers
    waiting = out_n + branch_n + gate_n + inner_n
    CORE_FAR, CORE_NEAR, SUM_X = range(3)
    lines.z_steps(ready, 1)
    lines.y_start(*out_n)
    for group, slot, at, mine in ((CORE_FAR, 0, seq_cx, seq_x), (CORE_NEAR, 1, seq_c, seq)):
        enter_norm(at)
        for i in range(CHUNKS):
            r = ch.rows(i)
            ch.go(group, i, part.at[at, r], from_core.at[slot, r], near.core)
        enter_norm(mine)
    weight_blocks(branch_part, branch, 1 - p)
    lines.y_start(*branch_n)
    for i in range(CHUNKS):
        r = ch.rows(i)
        ch.arrived(CORE_FAR, i, from_core.at[0, r], near.core)
        from_core[0, r, :] = from_core[0, r, :] + part[seq_x, r, :]
        ch.go(SUM_X, i, from_core.at[0, r], from_x.at[r], near.over_x)
    lines.z_steps(ready, 2)
    weight_blocks(branch_part, branch, p)
    weight_blocks(inner_part, inner, 1 - p)
    lines.y_start(*gate_n, *inner_n)
    for k in range(3, n_q):
        lines.z_steps(ready, k)
    weight_blocks(inner_part, inner, p)
    gain_sum = jnp.zeros_like(gain)
    for i in range(CHUNKS):
        r = ch.rows(i)
        ch.arrived(CORE_NEAR, i, from_core.at[1, r], near.core)
        ch.arrived(SUM_X, i, from_x.at[r], near.over_x)
        total = part[seq, r, :].astype(F32) + from_core[1, r, :].astype(F32) + from_x[r, :].astype(F32)
        value = tok[r, :].astype(F32)
        scale = lax.rsqrt(jnp.mean(value * value, axis=-1, keepdims=True) + EPSILON)
        unit = value * scale
        gain_sum = gain_sum + jnp.sum(total * unit, axis=0, keepdims=True)
        lifted = total * gain[...]
        grad_tok[r, :] = back[r, :] + scale * (
            lifted - unit * jnp.mean(lifted * unit, axis=-1, keepdims=True)
        )

    gain_near[0, :, :] = jnp.concatenate(
        [gain_sum, mid_grad[...], jnp.zeros((TILE - 2, gain.shape[1]), F32)], axis=0
    )
    pairs = [
        remote(gain_near.at[2 * i], gain_near.at[2 * i + 1], (gain_send, gain_recv), i, device)
        for i, device in enumerate((near.core, near.over_x, near.over_y))
    ]
    copies = [
        remote(gain_near.at[6], gain_line.at[i], (gain_send, gain_recv), 3 + i, device) for i, device in enumerate(along)
    ]

    def gain_step(i):
        if 0 < i <= 3:
            pairs[i - 1].wait()
            gain_near[2 * i, :, :] = gain_near[2 * i - 2, :, :] + gain_near[2 * i - 1, :, :]
        for copy in pairs[i : i + 1] if i < 3 else copies if i == 3 else []:
            copy.start()

    gain_step(0)
    for t in range(len(waiting) + n_q - 1):
        if t < len(waiting):
            lines.pair_up(waiting[t])
        for k in range(1, n_q):
            if 0 <= t - (k - 1) < len(waiting):
                lines.z_step(waiting[t - (k - 1)], k)
        if 0 <= t - (n_q - 1) < len(waiting):
            lines.finish(waiting[t - (n_q - 1)])
        if t == 0:
            gain_step(1)
            lines.finish_all(ready)
        if t == 1:
            gain_step(2)
        if t == len(waiting) - 1:
            gain_step(3)
    total = gain_near[6, :, :]
    for i, copy in enumerate(copies):
        copy.wait()
        total = total + gain_line[i, :, :]
    gains[...] = total
    ch.finish()
    lines.close()


def weight_sums(place, normed, weights, back_branch, back_inner, tok, back, gain, mid_grad, up_part, out_part, gate_part):
    rows, width = tok.shape
    n_q, n_seq, n_dp = place.n_q, place.n_seq, place.n_dp
    own = back_branch.shape[1]
    vmem, kept = pl.BlockSpec(memory_space=pltpu.VMEM), pl.BlockSpec(memory_space=pl.ANY)
    made = jax.ShapeDtypeStruct((n_dp, width // n_dp, own), BF16)
    cuts = (("rows", 4), ("turn", 1), ("seq", 2), ("turn", 1), ("seq", 2))
    outs, scratch = line_scratch(place, [up_part, out_part, made, gate_part, made], cuts)
    by_seq = lambda a: a.reshape(n_seq, rows, own)
    return pl.pallas_call(
        partial(weight_sums_kernel, cuts),
        in_specs=[vmem] * 11,
        out_specs=[vmem, vmem] + [kept] * len(cuts),
        out_shape=[jax.ShapeDtypeStruct((rows, width), F32), jax.ShapeDtypeStruct((TILE, width), F32)] + outs,
        scratch_shapes=[
            pltpu.VMEM(made.shape, BF16),
            pltpu.VMEM(made.shape, BF16),
            pltpu.VMEM((n_seq, rows, width), BF16),
            pltpu.VMEM((2, rows, width), BF16),
            pltpu.VMEM((rows, width), BF16),
            pltpu.VMEM((7, TILE, width), F32),
            pltpu.VMEM((n_q - 1, TILE, width), F32),
            pltpu.SemaphoreType.DMA((3 * CHUNKS,)),
            pltpu.SemaphoreType.DMA((3 * CHUNKS,)),
            pltpu.SemaphoreType.DMA((2 + n_q,)),
            pltpu.SemaphoreType.DMA((2 + n_q,)),
        ]
        + scratch,
        compiler_params=pltpu.CompilerParams(
            collective_id=3, has_side_effects=True, vmem_limit_bytes=VMEM_BYTES
        ),
        name="weight_sums",
    )(normed, weights, by_seq(back_branch), by_seq(back_inner), tok, back, gain, mid_grad, up_part, out_part, gate_part)


class PlaneSum:
    FAR, TO_X, TO_Y, NEAR = range(4)
    AT = {0: (1, 1), 1: (0, 1), 2: (1, 0), 3: (0, 0)}

    def __init__(self, near, ch, groups, part, local, own, from_core, corner_x, corner_y, got_x, got_y):
        self.near, self.ch, self.part, self.own, self.from_core = near, ch, part, own, from_core
        self.corner_x, self.corner_y, self.got_x, self.got_y = corner_x, corner_y, got_x, got_y
        self.core_group = groups
        self.cx, self.cy, self.gx, self.gy = range(groups + 4, groups + 8)
        half = CHUNKS // 2
        self.half, self.first, self.last = half, range(half), range(half, CHUNKS)
        self.loads = [pltpu.make_async_copy(part.at[i, 0], own.at[i], local.at[i]) for i in range(2)]

    def load(self):
        for load in self.loads:
            load.start()

    def to_core(self, group, chunks):
        other_p, other_x = self.AT[group]
        for i in chunks:
            r = self.ch.rows(i)
            self.ch.go(
                self.core_group + group, i, self.part.at[other_p, 1, other_x, r], self.from_core.at[group, r], self.near.core
            )

    def on_chip(self, group, i):
        r = self.ch.rows(i)
        other_p, other_x = self.AT[group]
        self.ch.arrived(self.core_group + group, i, self.from_core.at[group, r], self.near.core)
        return self.own[other_p, other_x, r, :].astype(F32) + self.from_core[group, r, :].astype(F32)

    def start(self):
        self.to_core(self.FAR, (0, self.half, 1, self.half + 1))
        self.to_core(self.TO_X, self.first)
        self.to_core(self.TO_Y, self.last)
        self.to_core(self.TO_X, self.last)
        self.to_core(self.TO_Y, self.first)
        self.to_core(self.NEAR, range(CHUNKS))

    def corners(self):
        near, ch = self.near, self.ch
        for load in self.loads:
            load.wait()
        for i in (0, self.half, 1, self.half + 1):
            r = ch.rows(i)
            self.from_core[self.FAR, r, :] = self.on_chip(self.FAR, i).astype(BF16)
            if i < self.half:
                ch.go(self.cx, i, self.from_core.at[self.FAR, r], self.corner_x.at[r], near.over_x)
            else:
                b = ch.rows(i - self.half)
                ch.go(self.cy, i - self.half, self.from_core.at[self.FAR, r], self.corner_y.at[b], near.over_y)

    def straight(self):
        for i, j in zip(self.first, self.last):
            self.along(self.TO_X, i, self.on_chip(self.TO_X, i))
            self.along(self.TO_Y, j, self.on_chip(self.TO_Y, j))

    def along(self, group, i, total):
        r = self.ch.rows(i)
        self.from_core[group, r, :] = total.astype(BF16)
        if group == self.TO_X:
            self.ch.go(self.gx, i, self.from_core.at[group, r], self.got_x.at[r], self.near.over_x)
        else:
            self.ch.go(self.gy, i, self.from_core.at[group, r], self.got_y.at[r], self.near.over_y)

    def turned(self):
        ch = self.ch
        for i, j in zip(self.first, self.last):
            b = ch.rows(j - self.half)
            ch.arrived(self.cy, j - self.half, self.corner_y.at[b], self.near.over_y)
            self.along(self.TO_X, j, self.on_chip(self.TO_X, j) + self.corner_y[b, :].astype(F32))
            r = ch.rows(i)
            ch.arrived(self.cx, i, self.corner_x.at[r], self.near.over_x)
            self.along(self.TO_Y, i, self.on_chip(self.TO_Y, i) + self.corner_x[r, :].astype(F32))

    def total(self, i):
        r = self.ch.rows(i)
        total = self.on_chip(self.NEAR, i)
        self.ch.arrived(self.gx, i, self.got_x.at[r], self.near.over_x)
        self.ch.arrived(self.gy, i, self.got_y.at[r], self.near.over_y)
        return total + self.got_x[r, :].astype(F32) + self.got_y[r, :].astype(F32)

    @staticmethod
    def scratch(count, width):
        block = pltpu.VMEM((count, width), BF16)
        half = pltpu.VMEM((count // 2, width), BF16)
        return [pltpu.VMEM((4, count, width), BF16), half, half, block, block]


def back_middle_kernel(cuts, *refs):
    part, down_part, rows_in, cots_in, middle, cot, gain, hidden, back_gate, back_up = refs[:10]
    back, rows, gain_grad, result, up_out = refs[10:15]
    totals = refs[15:17]
    own, plane_a, plane_b, low = refs[17], refs[18:23], refs[23:28], refs[28]
    grad_down, grad_gate, grad_up, tiles = refs[29:33]
    send, recv, local, loads_a, loads_b, tile_sem, up_sem = refs[33:40]
    line_refs = refs[40:]
    near = Near()
    x, c, seq = near.x, near.c, near.seq
    ch = Chunks((send, recv), cot.shape[0])
    seq_x, seq_c = seq + 2 - 4 * x, seq + 1 - 2 * c
    seq_cx = seq_c + 2 - 4 * x
    lines = LineSums(
        near, line_pieces(cuts, (grad_down, grad_gate), totals, line_refs[:-3]), line_refs[-3:-1], line_refs[-1]
    )
    main = PlaneSum(near, ch, 0, part, loads_a, own, *plane_a)
    side = PlaneSum(near, ch, 8, down_part, loads_b, own, *plane_b)
    main.load()

    cols = tiles.shape[2]
    order = [(source, t) for group in ((3, 0), (2, 1)) for source in (cots_in, rows_in) for t in group]
    fetches = [
        pltpu.make_async_copy(source.at[:, pl.ds(t * cols, cols)], tiles.at[n % 2], tile_sem.at[n % 2])
        for n, (source, t) in enumerate(order)
    ]
    tile_number = iter(range(len(order)))
    for fetch in fetches[:2]:
        fetch.start()
    ups = []

    def gradients(times):
        for _ in range(times):
            n = next(tile_number)
            source, t = order[n]
            fetches[n].wait()
            if source is cots_in:
                grad_down[:, t * cols : (t + 1) * cols] = contract_rows(hidden[...], tiles[n % 2]).astype(BF16)
            else:
                grad_gate[t, :, :] = contract_rows(tiles[n % 2], back_gate[...]).astype(BF16)
                if ups:
                    ups[-1].wait()
                grad_up[...] = contract_rows(tiles[n % 2], back_up[...]).astype(BF16)
                ups.append(pltpu.make_async_copy(grad_up, up_out.at[t], up_sem.at[0]))
                ups[-1].start()
            if n + 2 < len(order):
                fetches[n + 2].start()

    expected = greet_lines(near, [near.core, near.over_x, near.over_y])
    pl.semaphore_wait(pltpu.get_barrier_semaphore(), expected)
    OWN_X, OWN_C, FWD_C = 16, 17, 18
    half = len(lines.pieces) // 2
    early, late = range(half), range(half, 2 * half)
    main.start()
    gradients(2)
    lines.z_steps(early, 1)
    main.corners()
    gradients(1)
    main.straight()
    gradients(1)
    lines.z_steps(late, 1)
    gradients(2)
    main.turned()
    side.start()
    lines.z_steps(early, 2)
    gradients(2)
    lines.z_steps(late, 2)
    gain_sum = jnp.zeros_like(gain)
    kept = []
    for i in range(CHUNKS):
        r = ch.rows(i)
        total = main.total(i)
        value = middle[r, :]
        scale = lax.rsqrt(jnp.mean(value * value, axis=-1, keepdims=True) + EPSILON)
        unit = value * scale
        gain_sum = gain_sum + jnp.sum(total * unit, axis=0, keepdims=True)
        lifted = total * gain[...]
        whole = cot[r, :].astype(F32) + scale * (lifted - unit * jnp.mean(lifted * unit, axis=-1, keepdims=True))
        back[r, :] = whole
        low[r, :] = whole.astype(BF16)
        ch.go(OWN_X, i, low.at[r], rows.at[seq, r], near.over_x)
        ch.go(OWN_C, i, low.at[r], rows.at[seq, r], near.core)
        keep = pltpu.make_async_copy(low.at[r], rows.at[seq, r], local.at[i])
        keep.start()
        kept.append(keep)
    gain_grad[...] = gain_sum
    side.load()
    lines.z_steps(early, 3)
    side.corners()
    side.straight()
    lines.z_steps(late, 3)
    for i in range(CHUNKS):
        here = rows.at[seq_x, ch.rows(i)]
        ch.arrived(OWN_X, i, here, near.over_x)
        ch.go(FWD_C, i, here, here, near.core)
    side.turned()
    lines.finish_all(early)
    for i in range(CHUNKS):
        r = ch.rows(i)
        result[r, :] = (middle[r, :] + side.total(i)).astype(BF16)
    lines.finish_all(late)
    ups[-1].wait()
    for i in range(CHUNKS):
        ch.arrived(OWN_C, i, rows.at[seq_c, ch.rows(i)], near.core)
        ch.arrived(FWD_C, i, rows.at[seq_cx, ch.rows(i)], near.core)
    for keep in kept:
        keep.wait()
    ch.finish()
    lines.close()


def sum_back_middle(place, part, down_part, rows, cots, middle, cot, gain, hidden, back_gate, back_up):
    count, width = cot.shape
    tokens, units = hidden.shape
    n_q = place.n_q
    cuts = (("columns", 4), ("rows", 4))
    vmem, kept = pl.BlockSpec(memory_space=pltpu.VMEM), pl.BlockSpec(memory_space=pl.ANY)
    made = jax.ShapeDtypeStruct((units, width), BF16), jax.ShapeDtypeStruct((n_q, width // n_q, units), BF16)
    outs, scratch = line_scratch(place, made, cuts)
    return pl.pallas_call(
        partial(back_middle_kernel, cuts),
        in_specs=[kept] * 4 + [vmem] * 6,
        out_specs=[vmem, kept, vmem, vmem, kept, kept, kept],
        out_shape=[
            jax.ShapeDtypeStruct((count, width), F32),
            jax.ShapeDtypeStruct((place.n_seq, count, width), BF16),
            jax.ShapeDtypeStruct((1, width), F32),
            jax.ShapeDtypeStruct((count, width), BF16),
            made[1],
        ]
        + outs,
        scratch_shapes=[pltpu.VMEM((2, 2, count, width), BF16)]
        + PlaneSum.scratch(count, width)
        + PlaneSum.scratch(count, width)
        + [
            pltpu.VMEM((count, width), BF16),
            pltpu.VMEM(made[0].shape, BF16),
            pltpu.VMEM(made[1].shape, BF16),
            pltpu.VMEM(made[1].shape[1:], BF16),
            pltpu.VMEM((2, tokens, width // n_q), BF16),
            pltpu.SemaphoreType.DMA((19 * CHUNKS,)),
            pltpu.SemaphoreType.DMA((19 * CHUNKS,)),
            pltpu.SemaphoreType.DMA((CHUNKS,)),
            pltpu.SemaphoreType.DMA((2,)),
            pltpu.SemaphoreType.DMA((2,)),
            pltpu.SemaphoreType.DMA((2,)),
            pltpu.SemaphoreType.DMA((1,)),
        ]
        + scratch,
        compiler_params=pltpu.CompilerParams(
            collective_id=2, has_side_effects=True, vmem_limit_bytes=MOST_VMEM_BYTES
        ),
        name="sum_back_middle",
    )(part, down_part, rows, cots, middle, cot, gain, hidden, back_gate, back_up)


def entry_kernel(x_ref, w_ref, normed_ref, branch_ref, inner_ref, gains_ref):
    own = branch_ref.shape[1]

    @pl.when(pl.program_id(0) == 0)
    def _():
        gains_ref[...] = w_ref[:, 2 * own :].astype(F32).T[:TILE, :]

    value = x_ref[...].astype(F32)
    scale = lax.rsqrt(jnp.mean(value * value, axis=-1, keepdims=True) + EPSILON)
    normed = (value * scale * gains_ref[0:1, :]).astype(BF16)
    normed_ref[...] = normed
    inner_ref[...] = dot(normed, w_ref[:, own : 2 * own]).astype(BF16)
    branch_ref[...] = dot(normed, w_ref[:, :own])


def entry_products(x, weights, own, tile):
    rows, width = x.shape
    whole = lambda shape: pl.BlockSpec(shape, lambda i: (0, 0), pipeline_mode=pl.Buffered(1))
    by_tile = lambda cols: pl.BlockSpec((tile, cols), lambda i: (i, 0))
    return pl.pallas_call(
        entry_kernel,
        grid=(rows // tile,),
        in_specs=[by_tile(width), whole(weights.shape)],
        out_specs=[by_tile(width), by_tile(own), by_tile(own), pl.BlockSpec((TILE, width), lambda i: (0, 0))],
        out_shape=[
            jax.ShapeDtypeStruct((rows, width), BF16),
            jax.ShapeDtypeStruct((rows, own), F32),
            jax.ShapeDtypeStruct((rows, own), BF16),
            jax.ShapeDtypeStruct((TILE, width), F32),
        ],
        compiler_params=pltpu.CompilerParams(vmem_limit_bytes=VMEM_BYTES),
        cost_estimate=pl.CostEstimate(
            flops=4 * rows * width * own, bytes_accessed=weights.size * 2 + rows * (width * 4 + own * 6), transcendentals=rows
        ),
        name="entry_products",
    )(x, weights)


def mlp_kernel(p_ref, x_ref, cot_ref, gate_ref, up_ref, down_ref, *result_refs):
    results = mlp_tile(x_ref[...], cot_ref[...], gate_ref[...], up_ref[...], down_ref[...])
    for ref, value in zip(result_refs, results):
        ref[...] = value


def mlp_products(p, x, cot, gate_weight, up_weight, down_weight, tile):
    rows, width = x.shape
    units = gate_weight.shape[1] // 2
    by_tile = lambda cols: pl.BlockSpec((tile, cols), lambda i, p: (i, 0))
    half = lambda shape, at: pl.BlockSpec(shape, at, pipeline_mode=pl.Buffered(1))
    columns = half((width, units), lambda i, p: (0, p[0]))
    return pl.pallas_call(
        mlp_kernel,
        grid_spec=pltpu.PrefetchScalarGridSpec(
            num_scalar_prefetch=1,
            grid=(rows // tile,),
            in_specs=[
                by_tile(width), by_tile(width), columns, columns, half((units, width), lambda i, p: (p[0], 0))
            ],
            out_specs=[by_tile(units)] * 3 + [by_tile(width)] * 2,
        ),
        out_shape=[jax.ShapeDtypeStruct((rows, units), BF16)] * 3 + [jax.ShapeDtypeStruct((rows, width), BF16)] * 2,
        compiler_params=pltpu.CompilerParams(vmem_limit_bytes=VMEM_BYTES),
        cost_estimate=pl.CostEstimate(
            flops=12 * rows * width * units, bytes_accessed=rows * width * 8 + units * width * 6, transcendentals=rows * units
        ),
        name="mlp_products",
    )(p, x, cot, gate_weight, up_weight, down_weight)


def mlp_grads_kernel(x_ref, cot_ref, hidden_ref, back_gate_ref, back_up_ref, down_ref, gate_ref, up_ref):
    x = x_ref[...]
    down_ref[...] = contract_rows(hidden_ref[...], cot_ref[...]).astype(BF16)
    gate_ref[...] = contract_rows(x, back_gate_ref[...]).astype(BF16)
    up_ref[...] = contract_rows(x, back_up_ref[...]).astype(BF16)


def mlp_grads(x, cot, hidden, back_gate, back_up, tile):
    rows, width = x.shape
    units = hidden.shape[1]
    columns = pl.BlockSpec((rows, tile), lambda i: (0, i))
    whole = pl.BlockSpec((rows, units), lambda i: (0, 0), pipeline_mode=pl.Buffered(1))
    by_tile = pl.BlockSpec((tile, units), lambda i: (i, 0))
    return pl.pallas_call(
        mlp_grads_kernel,
        grid=(width // tile,),
        in_specs=[columns, columns, whole, whole, whole],
        out_specs=[pl.BlockSpec((units, tile), lambda i: (0, i)), by_tile, by_tile],
        out_shape=[jax.ShapeDtypeStruct((units, width), BF16)] + [jax.ShapeDtypeStruct((width, units), BF16)] * 2,
        compiler_params=pltpu.CompilerParams(vmem_limit_bytes=VMEM_BYTES),
        cost_estimate=pl.CostEstimate(
            flops=6 * rows * width * units, bytes_accessed=rows * width * 4 + units * (rows + width) * 6, transcendentals=0
        ),
        name="mlp_grads",
    )(x, cot, hidden, back_gate, back_up)


def exit_kernel(
    normed_ref, w_ref, branch_ref, inner_ref, grad_branch_ref, grad_inner_ref, part_ref
):
    own = branch_ref.shape[1]
    normed = normed_ref[...]
    grad_branch_ref[...] = contract_rows(normed, branch_ref[...]).astype(BF16)
    grad_inner_ref[...] = contract_rows(normed, inner_ref[...]).astype(BF16)
    part_ref[...] = (
        contract_cols(branch_ref[...], w_ref[:, :own]) + contract_cols(inner_ref[...], w_ref[:, own : 2 * own])
    ).astype(BF16)


def exit_products(normed, weights, back_branch, back_inner, tile):
    rows, width = normed.shape
    own = back_inner.shape[1]
    columns = pl.BlockSpec((rows, tile), lambda i: (0, i))
    whole = pl.BlockSpec((rows, own), lambda i: (0, 0), pipeline_mode=pl.Buffered(1))
    by_tile = lambda cols: pl.BlockSpec((tile, cols), lambda i: (i, 0))
    return pl.pallas_call(
        exit_kernel,
        grid=(width // tile,),
        in_specs=[columns, by_tile(weights.shape[1]), whole, whole],
        out_specs=[by_tile(own), by_tile(own), columns],
        out_shape=[
            jax.ShapeDtypeStruct((width, own), BF16),
            jax.ShapeDtypeStruct((width, own), BF16),
            jax.ShapeDtypeStruct((rows, width), BF16),
        ],
        compiler_params=pltpu.CompilerParams(vmem_limit_bytes=VMEM_BYTES),
        cost_estimate=pl.CostEstimate(
            flops=8 * rows * width * own, bytes_accessed=rows * width * 6 + own * (rows + width) * 10, transcendentals=0
        ),
        name="exit_products",
    )(normed, weights, back_branch, back_inner)


def shards(
    tokens, row_lengths, branch_weight, inner_weight, output_weight, rate_weight, entry_weight,
    rate_bias, entry_bias, conv_weight, conv_bias, recur_param, norm_gain, mlp_gain,
    gate_weight, up_weight, down_weight, cotangent,
):
    place = Place()
    n_dp, n_seq = place.n_dp, place.n_seq
    tok, width = tokens.shape
    count = tok * n_seq
    rec = branch_weight.shape[1]
    own = rec // n_seq
    blocks = max(-(-(own * (s + 1)) // BLOCK) - own * s // BLOCK for s in range(n_seq))
    spread = blocks * BLOCK
    d_rows = branch_weight.shape[0]
    r_rows = output_weight.shape[0]

    gains = jnp.stack([norm_gain, mlp_gain], axis=1)
    gains = jnp.pad(gains, ((0, 0), (0, LANES - 2)))
    cut = lambda w: w.reshape(d_rows, n_seq, own).swapaxes(0, 1)
    in_pack = jnp.concatenate(
        [cut(branch_weight), cut(inner_weight), jnp.broadcast_to(gains[None], (n_seq,) + gains.shape)], axis=2
    )
    vectors = jnp.concatenate(
        [conv_weight, jnp.stack([conv_bias, rate_bias, entry_bias, recur_param])], axis=0
    )
    vectors = jnp.pad(vectors.T, ((0, 0), (0, LANES - 2 * WIDTH)))
    out_pack = jnp.concatenate([output_weight, rate_weight, entry_weight, vectors], axis=1)
    fast = place.n_x == 2 and place.n_q == 4
    if fast:
        in_all, out_all, group_x, cot_c, cot_o = gather_all(place, in_pack, out_pack, tokens, cotangent)
        in_all = in_all.reshape(n_dp * n_seq * d_rows, -1)
        out_all = out_all.reshape(n_dp * r_rows, -1)
    else:
        in_pack = lax.all_to_all(in_pack, "seq", 0, 0, tiled=True).reshape(n_seq * d_rows, -1)
        out_pack = turned(place, out_pack, False)
        in_all = lax.all_gather(in_pack, "dp", axis=0, tiled=True)
        out_all = lax.all_gather(out_pack, "dp", axis=0, tiled=True)
        group_x = gather_seq(place, tokens)
        group_c = gather_seq(place, cotangent)
    w_out = out_all[:, :width]
    gate_rows = window(place, out_all[:, width : width + 2 * BLOCK], 0, own, spread)
    w_rate, w_entry = gate_rows[:, :BLOCK], gate_rows[:, BLOCK:]
    vec = out_all[:, width + 2 * BLOCK : width + 2 * BLOCK + 2 * WIDTH].astype(F32).T
    taps = jnp.pad(vec[: WIDTH + 1], ((0, 7 - WIDTH), (0, 0)))
    gate_vec = jnp.pad(vec[WIDTH + 1 :], ((0, 9 - 2 * WIDTH + WIDTH), (0, 0)))
    first = own * place.seq - jnp.minimum(own * place.seq // BLOCK * BLOCK, rec - spread)
    owned = lambda a, axis: lax.dynamic_slice_in_dim(a, first, own, axis=axis) if spread != own else a

    group_x = group_x.reshape(count, width)
    away = place.swap_pair(cot_c if fast else group_c)
    offsets = row_offsets(row_lengths[0], jnp.arange(count, dtype=jnp.int32))[:, None]

    normed, branch_pre, inner, gain_rows = entry_products(group_x, in_all, own, ENTRY_TILE)
    gain_in, gain_mid = gain_rows[0:1], gain_rows[1:2]
    heads = partial(jnp.einsum, preferred_element_type=F32)
    if fast:
        gate_first = (own * place.seq % BLOCK // LANES).astype(jnp.int32)[None]
        (conv_wide,) = by_block(
            conv_wide_kernel, gate_first, [("own", inner), ("own", taps), ("one", offsets)],
            [("wide", (count, spread), BF16)], 0, own,
        )
        conv_wide = fill_edge(place, conv_wide, own)
        gate_ins = [("block", conv_wide), ("columns", w_rate), ("columns", w_entry), ("wide", conv_wide)]
        gate_ins += [("own", branch_pre), ("own", gate_vec), ("one", offsets)]
        states, mixed = by_block(
            forward_gates_kernel, gate_first, gate_ins,
            [("own", (count, own), F32), ("own", (count, own), BF16)], 2, own,
        )
    else:
        (conv,) = by_channel(conv_kernel, [inner, taps, offsets], [((count,), BF16)], own)
        conv_wide = window(place, conv, 1, own, spread)
        conv_heads = conv_wide.reshape(count, blocks, BLOCK)
        pre_rate, pre_entry = (
            owned(heads("tbc,bcd->tbd", conv_heads, w.reshape(blocks, BLOCK, BLOCK)).reshape(count, spread), 1)
            for w in (w_rate, w_entry)
        )
        states, mixed = by_channel(
            forward_kernel,
            [pre_rate, pre_entry, conv, branch_pre, gate_vec, offsets],
            [((count,), F32), ((count,), BF16)],
            own,
        )
    mixed, away = lax.optimization_barrier((mixed, away))
    whole_x = tokens.astype(F32)
    if fast:
        middle, rows, pair_cot, hidden, back_gate, back_up, down_part, back_part = sum_middle(
            place, mixed, w_out, tokens, gain_mid, cot_c, cot_o, away, gate_weight, up_weight, down_weight
        )
    else:
        out_part = dot(mixed, w_out).astype(BF16).reshape(n_seq, tok, width)
        middle = whole_x + scatter_seq(place, out_part)
        rows = gather_plane(place, rms_norm(middle, gain_mid).astype(BF16))
        pair_cot = jnp.stack([jnp.where(place.p == 0, group_c, away), jnp.where(place.p == 0, away, group_c)])
        hidden, back_gate, back_up, down_part, back_part = mlp_products(
            place.p.astype(jnp.int32)[None], rows.reshape(2 * count, width), pair_cot.reshape(2 * count, width),
            gate_weight, up_weight, down_weight, MLP_TILE,
        )
    flat = lambda a: a.reshape(2 * count, -1)
    rows, pair_cot, hidden, back_gate, back_up = (flat(a) for a in (rows, pair_cot, hidden, back_gate, back_up))
    units = gate_weight.shape[1] // 2

    n_q = place.n_q
    if fast:
        plane = (2, 2, 2, tok, width)
        back_middle, back_out, grad_mlp_gain, result, grad_up_part, down_sum, gate_sum = sum_back_middle(
            place, back_part.reshape(plane), down_part.reshape(plane), rows, pair_cot, middle, cotangent, gain_mid,
            hidden, back_gate, back_up,
        )
        grad_mlp_gain = grad_mlp_gain[0]
    else:
        grad_down_part, grad_gate_part, grad_up_part = mlp_grads(rows, pair_cot, hidden, back_gate, back_up, GRAD_TILE)
        grad_gate_part, grad_up_part = (a.reshape(n_q, -1, units) for a in (grad_gate_part, grad_up_part))
        plane = (2, n_seq, tok, width)
        result = (middle + scatter_plane(place, down_part.reshape(plane))).astype(BF16)
        back_norm, grad_mlp_gain = rms_back(middle, gain_mid, scatter_plane(place, back_part.reshape(plane)))
        back_middle = cotangent.astype(F32) + back_norm
        back_out = gather_seq(place, back_middle.astype(BF16))
        step = q_step(place)
        strip = width // n_q
        down_sum = line_sum(
            lambda i: lax.dynamic_slice_in_dim(grad_down_part, i * strip, strip, 1), n_q, place.q, step
        )
        gate_sum, up_sum = (
            line_sum(partial(lax.dynamic_index_in_dim, a, axis=0, keepdims=False), n_q, place.q, step)
            for a in (grad_gate_part, grad_up_part)
        )
        down_sum, gate_sum, up_sum = (
            split_pair(place, a, axis) for a, axis in ((down_sum, 1), (gate_sum, 0), (up_sum, 0))
        )
    back_out = back_out.reshape(count, width)

    back_mixed = contract_cols(back_out, w_out)
    grad_output_part = contract_rows(mixed, back_out).astype(BF16)
    if fast:
        back_branch, back_gates, direct, gate_sums = by_block(
            backward_gates_kernel, gate_first, gate_ins + [("own", states), ("own", back_mixed)],
            [("own", (count, own), BF16), ("wide2", (2, count, spread), BF16), ("own", (count, own), F32),
             ("own", (TILE, own), F32)], 2, own,
        )
        back_gates = fill_edge(place, back_gates, own)
        back_inner, conv_sums = by_block(
            conv_back_gates_kernel, gate_first,
            [("block2", back_gates), ("rows", w_rate), ("rows", w_entry), ("own", direct), ("own", inner),
             ("own", taps), ("one", offsets)],
            [("own", (count, own), BF16), ("own", (TILE, own), F32)], 1, own,
        )
    else:
        back_branch, back_gates, direct, gate_sums = by_channel(
            backward_kernel,
            [pre_rate, pre_entry, conv, branch_pre, gate_vec, offsets, states, back_mixed],
            [((count,), BF16), ((2, count), BF16), ((count,), F32), ((TILE,), F32)],
            own,
        )
        back_gates = jnp.stack([window(place, a, 1, own, spread) for a in (back_gates[0], back_gates[1])])
        gates_back = sum(
            heads("tbd,bcd->tbc", a.reshape(count, blocks, BLOCK), w.reshape(blocks, BLOCK, BLOCK)).reshape(count, spread)
            for a, w in ((back_gates[0], w_rate), (back_gates[1], w_entry))
        )
        back_inner, conv_sums = by_channel(
            conv_back_kernel,
            [direct, owned(gates_back, 1), inner, taps, offsets],
            [((count,), BF16), ((TILE,), F32)],
            own,
        )
    grad_rate_part, grad_entry_part = (
        owned(
            jnp.concatenate(
                [contract_rows(conv_wide[:, b : b + BLOCK], a[:, b : b + BLOCK]) for b in range(0, spread, BLOCK)], axis=0
            ),
            0,
        )
        for a in (back_gates[0], back_gates[1])
    )

    sums = jnp.concatenate([conv_sums[: WIDTH + 1], gate_sums[:3]], axis=0).T
    sums = jnp.pad(sums, ((0, 0), (0, LANES - 2 * WIDTH))).astype(BF16)
    gate_grads = jnp.concatenate([grad_rate_part.astype(BF16), grad_entry_part.astype(BF16), sums], axis=1)
    by_dp = lambda a: a.reshape(n_dp, -1, a.shape[1])
    if fast:
        grad_tokens, gains, up_sum, output_sum, branch_sum, gates_sum, inner_sum = weight_sums(
            place, normed, in_all, back_branch, back_inner, tokens, back_middle, gain_in, grad_mlp_gain[None],
            grad_up_part, by_dp(grad_output_part), by_dp(gate_grads),
        )
        gains = lax.dynamic_slice_in_dim(gains[:2], (place.dp * n_seq + place.seq) * d_rows, d_rows, axis=1)
    else:
        grad_branch_part, grad_inner_part, normed_part = exit_products(normed, in_all, back_branch, back_inner, EXIT_TILE)
        back_x, grad_norm_gain = rms_back(
            whole_x, gain_in, scatter_seq(place, normed_part.reshape(n_seq, tok, width))
        )
        grad_tokens = back_middle + back_x
        gains = lax.psum_scatter(
            jnp.stack([grad_norm_gain, grad_mlp_gain]), BOTH, scatter_dimension=1, tiled=True
        )
        parts = [by_dp(a) for a in (grad_output_part, grad_branch_part, gate_grads, grad_inner_part)]
        totals = [sum_dp(place, a) for a in parts]
        output_sum, gates_sum = (turned(place, totals[i], True) for i in (0, 2))
        branch_sum, inner_sum = (
            jnp.swapaxes(
                lax.all_to_all(totals[i].reshape(n_seq, d_rows, -1), "seq", 0, 0, tiled=True), 0, 1
            ).reshape(d_rows, rec)
            for i in (1, 3)
        )
    down_sum = down_sum.reshape(-1, width // n_dp)
    grad_output, grad_branch, gates_sum, grad_inner, grad_down, grad_gate, grad_up = (
        a.astype(F32) for a in (output_sum, branch_sum, gates_sum, inner_sum, down_sum, gate_sum, up_sum)
    )
    grad_rate = gates_sum[:, :BLOCK]
    grad_entry = gates_sum[:, BLOCK : 2 * BLOCK]
    vec_sum = gates_sum[:, 2 * BLOCK :]

    return (
        result,
        grad_tokens,
        grad_branch,
        grad_inner,
        grad_output,
        grad_rate,
        grad_entry,
        vec_sum[:, WIDTH + 1],
        vec_sum[:, WIDTH + 2],
        vec_sum[:, :WIDTH].T,
        vec_sum[:, WIDTH],
        vec_sum[:, WIDTH + 3],
        gains[0],
        gains[1],
        grad_gate,
        grad_up,
        grad_down,
    )


def solution(mesh):
    rows, flat = P(BOTH, None), P(BOTH)
    in_specs = (
        rows, P("dp", None), rows, rows, rows, rows, rows, flat, flat, P(None, BOTH), flat, flat, flat, flat,
        P(None, "seq"), P(None, "seq"), P("seq", None), rows,
    )
    out_specs = (
        rows, rows, rows, rows, rows, rows, rows, flat, flat, P(None, BOTH), flat, flat, flat, flat,
        P("dp", "seq"), P("dp", "seq"), P("seq", "dp"),
    )
    return jax.shard_map(shards, mesh=mesh, in_specs=in_specs, out_specs=out_specs, check_vma=False)
```
